256 devices in a mesh: grp: 8 (over x, core), dev: 32 (over y, z).
Axes of the slice: x: 4, y: 4, z: 8, core: 2. Of those that a mesh axis runs over, the one named last changes fastest.
Arguments:
- features: bfloat16 [512, 128, 512], P(('grp', 'dev')), may hold values from -6 to 6
- grad_out: bfloat16 [512, 128, 512], P(('grp', 'dev')), may hold values from -6 to 6
- conv_weight: bfloat16 [27, 128, 128], replicated, may hold values from -0.109375 to 0.109375
- coarse_up: bfloat16 [128, 256], replicated, may hold values from -0.5 to 0.5
- coarse_down: bfloat16 [256, 128], replicated, may hold values from -0.375 to 0.375
- counts: int32 [256], P(('grp', 'dev')), may hold values from 1 to 2, as said below
- neighbour_owner: int32 [512, 26], P(('grp', 'dev')), may hold values from -1 to 31, as said below
- neighbour_slot: int32 [512, 26], P(('grp', 'dev')), may hold values from -1 to 1, as said below
- parent: int32 [512], P(('grp', 'dev')), may hold values from -1 to 3, as said below
- child_slot: int32 [512], P(('grp', 'dev')), may hold values from -1 to 63, as said below
Outputs:
- output: bfloat16 [512, 128, 512], P(('grp', 'dev'))
- grad_features: bfloat16 [512, 128, 512], P(('grp', 'dev'))
- grad_conv: float32 [27, 128, 128], replicated
- grad_up: float32 [128, 256], replicated
- grad_down: float32 [256, 128], replicated
The draws below stay inside these ranges and needn't reach their ends.
Inputs may be any that keep to these rules, and one draw needn't show every extreme that they name: counts: each region has a device with exactly 2 live bricks. neighbour_owner: -1 for no neighbour and on every slot that is not live; otherwise a device of the same region. The bricks of one device name at most one distinct brick of any other device, and some device names one. neighbour_slot: -1 exactly where neighbour_owner is -1; otherwise a live slot of that owner. parent: -1 on slots that are not live; live slots of one region have distinct (parent, child_slot) pairs. child_slot: -1 on slots that are not live.
All inputs are finite; a program needn't handle non-finite values.
Results may differ from the reference program's by a relative error of at most 0.0067.
Values may be sent and summed in bfloat16 or wider, within the bound.
No kernel may reach another device: no remote copies, remote signals or barrier semaphores. Data moves between devices by JAX's collectives and lax.ppermute only.
A program may use at most 192 MiB of HBM per device.

```python
import jax
import jax.numpy as jnp
from jax import lax

C = 128
C2 = 256
B_DEV = 2
TOTAL = 512
N_GRP = 8
N_DEV = 32


def brick_tables(key):
    keys = jax.random.split(key, 8)
    groups, owners, per = (N_GRP, N_DEV, B_DEV)
    counts = jax.random.randint(keys[0], (groups, owners), 1, per + 1)
    fullest = jax.random.randint(keys[1], (groups, 1), 0, owners)
    counts = jnp.where(jnp.arange(owners)[None, :] == fullest, per, counts)
    shape = (groups, owners, per, 26)
    local_dev = jnp.arange(owners)[None, :, None, None]
    slot_ids = jnp.arange(per)[None, None, :, None]
    mine = counts[:, :, None, None]
    living = slot_ids < mine
    exists = jax.random.randint(keys[2], shape, 0, 8) < 5
    remote = jax.random.randint(keys[3], shape, 0, 2) == 1
    remote = remote | (mine == 1)
    forced = (slot_ids == 0) & (jnp.arange(26)[None, None, None, :] == 0)
    exists = exists | forced
    remote = remote | forced
    shifted = jax.random.randint(keys[4], shape, 1, owners)
    far_owner = (local_dev + shifted) % owners
    stepped = jax.random.randint(keys[5], shape, 0, 1 << 20) % jnp.maximum(mine - 1, 1)
    near_slot = (slot_ids + 1 + stepped) % mine
    chosen = jax.random.randint(keys[6], (groups, owners, owners), 0, 1 << 20) % counts[:, None, :]
    far_slot = jnp.take_along_axis(chosen, far_owner.reshape(groups, owners, per * 26), axis=2).reshape(shape)
    present = exists & living
    owner_table = jnp.where(present, jnp.where(remote, far_owner, local_dev), -1)
    slot_table = jnp.where(present, jnp.where(remote, far_slot, near_slot), -1)
    kc_count = owners * per // 16
    group_keys = jax.random.split(keys[7], groups)
    places = jax.vmap(lambda k: jax.random.permutation(k, kc_count * 64)[:owners * per])(group_keys)
    places = places.reshape(groups, owners, per)
    alive = jnp.arange(per)[None, None, :] < counts[:, :, None]
    parent_table = jnp.where(alive, places // 64, -1)
    child_table = jnp.where(alive, places % 64, -1)
    total = groups * owners * per
    return (counts.reshape(-1).astype(jnp.int32), owner_table.reshape(total, 26).astype(jnp.int32), slot_table.reshape(total, 26).astype(jnp.int32), parent_table.reshape(total).astype(jnp.int32), child_table.reshape(total).astype(jnp.int32))


def draw_counts(key, part):
    return brick_tables(key)[0]


def draw_neighbour_owner(key, part):
    return brick_tables(key)[1]


def draw_neighbour_slot(key, part):
    return brick_tables(key)[2]


def draw_parent(key, part):
    return brick_tables(key)[3]


def draw_child_slot(key, part):
    return brick_tables(key)[4]


def shard_levels(rng, extent, shards, low, largest):
    gain, own = 1.0, jax.random.fold_in(rng, 6)
    for dim, parts in shards:
        steps = jnp.exp(jax.random.uniform(jax.random.fold_in(own, dim), (parts,), jnp.float32, low / len(shards), largest / len(shards)))
        gain = gain * jnp.repeat(steps, extent[dim] // parts).reshape([-1 if axis == dim else 1 for axis in range(len(extent))])
    return gain


def scatter_about(key, extent, scale, reach, cuts=(), held_as=jnp.bfloat16):
    entries = scale * jax.random.normal(key, extent, jnp.float32)
    if cuts:
        entries = entries * shard_levels(key, extent, cuts, -0.22, 0.18)
    return jnp.clip(entries, -reach, reach).astype(held_as)


def setup_inputs(seed: int = 0) -> dict:
    seeds = jax.random.split(jax.random.key(seed), 11)
    return {
        "features": scatter_about(seeds[0], (TOTAL, C, 512), 1.0, 6.0, ((0, 256),)),
        "grad_out": scatter_about(seeds[1], (TOTAL, C, 512), 1.0, 6.0, ((0, 256),)),
        "conv_weight": scatter_about(seeds[2], (27, C, C), (27 * C) ** -0.5, 0.109375),
        "coarse_up": scatter_about(seeds[3], (C, C2), C ** -0.5, 0.5),
        "coarse_down": scatter_about(seeds[4], (C2, C), C2 ** -0.5, 0.375),
        "counts": draw_counts(jax.random.fold_in(seeds[10], 71), 0),
        "neighbour_owner": draw_neighbour_owner(jax.random.fold_in(seeds[10], 71), 0),
        "neighbour_slot": draw_neighbour_slot(jax.random.fold_in(seeds[10], 71), 0),
        "parent": draw_parent(jax.random.fold_in(seeds[10], 71), 0),
        "child_slot": draw_child_slot(jax.random.fold_in(seeds[10], 71), 0),
    }


OFFSETS = [(a, b, c) for a in (-1, 0, 1) for b in (-1, 0, 1) for c in (-1, 0, 1) if (a, b, c) != (0, 0, 0)]


def source_cut(step):
    if step < 0:
        return slice(7, 8)
    if step == 0:
        return slice(0, 8)
    return slice(0, 1)


def padded_span(step):
    if step < 0:
        return slice(0, 1)
    if step == 0:
        return slice(1, 9)
    return slice(9, 10)


def assemble(center, source, lookup):
    rows = source.shape[0]
    pieces = {(0, 0, 0): center}
    for n, (a, b, c) in enumerate(OFFSETS):
        faces = source[:, :, source_cut(a), source_cut(b), source_cut(c)]
        wanted = lookup[:, n]
        taken = jnp.take(faces, jnp.clip(wanted, 0, rows - 1), axis=0)
        pieces[(a, b, c)] = jnp.where((wanted >= 0)[:, None, None, None, None], taken, jnp.zeros_like(taken))
    planes = []
    for a in (-1, 0, 1):
        lines = [jnp.concatenate([pieces[(a, b, c)] for c in (-1, 0, 1)], axis=4) for b in (-1, 0, 1)]
        planes.append(jnp.concatenate(lines, axis=3))
    return jnp.concatenate(planes, axis=2)


def columns(padded):
    rows, width = padded.shape[0], padded.shape[1]
    return jnp.stack([padded[:, :, a:a + 8, b:b + 8, c:c + 8].reshape(rows, width, 512)
                      for a in range(3) for b in range(3) for c in range(3)], axis=1)


def spread(grad_cols):
    rows, width = grad_cols.shape[0], grad_cols.shape[2]
    total = jnp.zeros((rows, width, 10, 10, 10), jnp.float32)
    k = 0
    for a in range(3):
        for b in range(3):
            for c in range(3):
                block = grad_cols[:, k].reshape(rows, width, 8, 8, 8)
                total = total + jnp.pad(block, ((0, 0), (0, 0), (a, 2 - a), (b, 2 - b), (c, 2 - c)))
                k += 1
    return total


def scatter_pieces(total, grad_pad, lookup):
    rows = total.shape[0]
    for n, (a, b, c) in enumerate(OFFSETS):
        target = jnp.where(lookup[:, n] >= 0, lookup[:, n], rows)
        total = total.at[target, :, source_cut(a), source_cut(b), source_cut(c)].add(
            grad_pad[:, :, padded_span(a), padded_span(b), padded_span(c)], mode="drop")
    return total


def pool_blocks(values):
    rows, width = values.shape[0], values.shape[1]
    return values.reshape(rows, width, 2, 4, 2, 4, 2, 4).sum(axis=(3, 5, 7)).reshape(rows, width, 8)


def expand(values):
    rows, width = values.shape[0], values.shape[1]
    shaped = values.reshape(rows, width, 2, 1, 2, 1, 2, 1)
    return jnp.broadcast_to(shaped, (rows, width, 2, 4, 2, 4, 2, 4)).reshape(rows, width, 512)


def silu_slope(value):
    gate = jax.nn.sigmoid(value)
    return gate * (1.0 + value * (1.0 - gate))


def reference(features, grad_out, conv_weight, coarse_up, coarse_down, counts, neighbour_owner, neighbour_slot, parent, child_slot):
    total_rows, width = features.shape[0], features.shape[1]
    slot_ids = jnp.arange(total_rows, dtype=jnp.int32)
    device = slot_ids // B_DEV
    live_rows = (slot_ids % B_DEV) < counts[device]
    live_in = jnp.where(live_rows[:, None, None], features, jnp.zeros_like(features))
    live_grad = jnp.where(live_rows[:, None, None], grad_out.astype(jnp.float32), jnp.float32(0.0))
    group_base = (device // N_DEV) * N_DEV
    lookup = jnp.where(neighbour_owner >= 0, (group_base[:, None] + neighbour_owner) * B_DEV + neighbour_slot, -1).astype(jnp.int32)
    bricks = live_in.reshape(total_rows, width, 8, 8, 8)
    padded = assemble(bricks, bricks, lookup)
    weight32 = conv_weight.astype(jnp.float32)
    blocked = padded.reshape(-1, B_DEV, width, 10, 10, 10)

    def conv_block(block):
        return jnp.einsum('mkiv,kio->mov', columns(block).astype(jnp.float32), weight32)

    pre_conv = lax.map(conv_block, blocked).reshape(total_rows, width, 512)
    active = jax.nn.silu(pre_conv)
    pooled = (pool_blocks(active) / 64.0).astype(jnp.bfloat16)
    regions = N_GRP
    members = N_DEV * B_DEV
    kc_count = members // 16
    position = jnp.where(live_rows & (parent >= 0), parent * 64 + child_slot, -1)
    onehot = (position.reshape(regions, members)[:, :, None] == jnp.arange(kc_count * 64)[None, None, :]).astype(jnp.float32)
    onehot = onehot.reshape(regions, members, kc_count, 64)
    coarse_in = jnp.einsum('gbkq,gbcs->gkcqs', onehot, pooled.astype(jnp.float32).reshape(regions, members, width, 8))
    coarse_in = coarse_in.reshape(regions, kc_count, width, 512).astype(jnp.bfloat16)
    coarse_pre = jnp.einsum('gkcv,ce->gkev', coarse_in.astype(jnp.float32), coarse_up.astype(jnp.float32))
    coarse_mid = jax.nn.silu(coarse_pre).astype(jnp.bfloat16)
    coarse_out = jnp.einsum('gkev,ec->gkcv', coarse_mid.astype(jnp.float32), coarse_down.astype(jnp.float32)).astype(jnp.bfloat16)
    lifted = jnp.einsum('gbkq,gkcqs->gbcs', onehot, coarse_out.astype(jnp.float32).reshape(regions, kc_count, width, 64, 8))
    lifted = expand(lifted.reshape(total_rows, width, 8))
    output = (live_in.astype(jnp.float32) + active + lifted).astype(jnp.bfloat16)

    grad_pool = pool_blocks(live_grad).astype(jnp.bfloat16)
    grad_coarse = jnp.einsum('gbkq,gbcs->gkcqs', onehot, grad_pool.astype(jnp.float32).reshape(regions, members, width, 8))
    grad_coarse = grad_coarse.reshape(regions, kc_count, width, 512).astype(jnp.bfloat16)
    grad_mid = jnp.einsum('gkcv,ec->gkev', grad_coarse.astype(jnp.float32), coarse_down.astype(jnp.float32))
    grad_pre = (grad_mid * silu_slope(coarse_pre)).astype(jnp.bfloat16)
    grad_down = jnp.einsum('gkev,gkcv->ec', coarse_mid.astype(jnp.float32), grad_coarse.astype(jnp.float32))
    grad_up = jnp.einsum('gkcv,gkev->ce', coarse_in.astype(jnp.float32), grad_pre.astype(jnp.float32))
    grad_cin = jnp.einsum('gkev,ce->gkcv', grad_pre.astype(jnp.float32), coarse_up.astype(jnp.float32)).astype(jnp.bfloat16)
    grad_back = jnp.einsum('gbkq,gkcqs->gbcs', onehot, grad_cin.astype(jnp.float32).reshape(regions, kc_count, width, 64, 8))
    grad_back = expand(grad_back.reshape(total_rows, width, 8)) / 64.0
    grad_conv_in = ((live_grad + grad_back) * silu_slope(pre_conv)).astype(jnp.bfloat16)

    def back_block(pair):
        block, grad_block = pair
        grad32 = grad_block.astype(jnp.float32)
        grad_cols = jnp.einsum('mov,kio->mkiv', grad32, weight32)
        weight_part = jnp.einsum('mkiv,mov->kio', columns(block).astype(jnp.float32), grad32)
        return spread(grad_cols), weight_part

    grad_pad, weight_parts = lax.map(back_block, (blocked, grad_conv_in.reshape(-1, B_DEV, width, 512)))
    grad_pad = grad_pad.reshape(total_rows, width, 10, 10, 10)
    grad_conv = jnp.sum(weight_parts, axis=0)
    grad_total = live_grad.reshape(total_rows, width, 8, 8, 8) + grad_pad[:, :, 1:9, 1:9, 1:9]
    grad_total = scatter_pieces(grad_total, grad_pad, lookup)
    grad_features = grad_total.reshape(total_rows, width, 512).astype(jnp.bfloat16)
    return output, grad_features, grad_conv, grad_up, grad_down
```

```python
import jax
import jax.numpy as jnp
import numpy as np
from jax import lax
from jax.experimental import pallas as pl
from jax.experimental.pallas import tpu as pltpu
from jax.sharding import PartitionSpec as P

BF = jnp.bfloat16
F32 = jnp.float32

OFFSETS = [
    (a, b, c) for a in (-1, 0, 1) for b in (-1, 0, 1) for c in (-1, 0, 1) if (a, b, c) != (0, 0, 0)
]
FACES = [d for d in OFFSETS if sum(map(abs, d)) == 1]
EDGES = [d for d in OFFSETS if sum(map(abs, d)) == 2]
CORNERS = [d for d in OFFSETS if sum(map(abs, d)) == 3]
PIECE = {d: 64 * n for n, d in enumerate(FACES)}
PIECE.update({d: 384 + 8 * n for n, d in enumerate(EDGES)})
PIECE.update({d: 480 + n for n, d in enumerate(CORNERS)})


def piece_row(i, q):
    if q < 12:
        face = q // 2
        return 64 * face + 2 * i + q % 2, OFFSETS.index(FACES[face])
    if q < 15:
        flat = 32 * (q - 12) + i
        return 384 + flat, OFFSETS.index(EDGES[flat // 8])
    return 480 + i // 4, OFFSETS.index(CORNERS[i // 4])


def cut(step):
    return [7] if step < 0 else ([0] if step > 0 else list(range(8)))


def tables():
    voxel = np.full(512, -1)
    for (a, b, c), base in PIECE.items():
        cells = [x * 64 + y * 8 + z for x in cut(a) for y in cut(b) for z in cut(c)]
        voxel[base : base + len(cells)] = cells
    take = np.zeros((512, 512), np.float32)
    pack = np.zeros((512, 512), np.float32)
    unpack = np.zeros((512, 512), np.float32)
    give = np.zeros((512, 512), np.float32)
    ask = np.zeros((512, 128), np.float32)
    for i in range(32):
        for q in range(16):
            row, direction = piece_row(i, q)
            at = 16 * i + q
            take[at, voxel[row]] = 1
            pack[at, row] = 1
            ask[at, direction] = 1
            if q < 15 or i % 4 == 0:
                unpack[row, at] = 1
                give[voxel[row], at] = 1
    pool = np.zeros((16, 512), np.float32)
    for v in range(512):
        a, b, c = v // 64, v // 8 % 8, v % 8
        pool[(a // 4) * 4 + (b // 4) * 2 + c // 4, v] = 1
    return take, pack, unpack, give, ask, pool


TAKE, PACK, UNPACK, GIVE, ASK, POOL = tables()


def nn(x, y):
    return lax.dot_general(x, y, (((1,), (0,)), ((), ())), preferred_element_type=F32)


def nt(x, y):
    return lax.dot_general(x, y, (((1,), (1,)), ((), ())), preferred_element_type=F32)


def identity():
    rows = lax.broadcasted_iota(jnp.int32, (128, 128), 0)
    lanes = lax.broadcasted_iota(jnp.int32, (128, 128), 1)
    return (rows == lanes).astype(F32).astype(BF)


def ask_kernel(counts, feat, bricks, take, ask, msg):
    rows = nt(ask[...], bricks[...]).astype(BF)
    msg[:, 32:48, :] = rows.reshape(32, 16, 128)
    for s in range(2):
        live = (counts[0] > s).astype(F32)
        held = nt(take[...], feat[s]) * live
        msg[:, 16 * s : 16 * s + 16, :] = held.astype(BF).reshape(32, 16, 128)


def route_kernel(got, out):
    lanes = lax.broadcasted_iota(jnp.int32, (128, 1024), 1)
    part = lax.broadcasted_iota(jnp.int32, (128, 1), 0) & 15
    data = got[:, 0:32, :].reshape(1024, 128)
    for s in range(2):

        def step(n, _):
            rows = pl.multiple_of(n * 8, 8)
            table = got[pl.ds(rows, 8), 32:48, :].reshape(128, 128).astype(F32)
            target = table[:, s : s + 1].astype(jnp.int32) * 16 + part
            hot = (lanes == target).astype(F32).astype(BF)
            picked = nn(hot, data).astype(BF)
            out[pl.ds(rows, 8), 16 * s : 16 * s + 16, :] = picked.reshape(8, 16, 128)
            return 0

        lax.fori_loop(0, 4, step, 0)


def forward_kernel(
    counts, parent, child, core, feat, got, gout, weight, up, down, unpack, pool,
    out, grad, wsum,
    pc, s0, s1, s2, cols, grad_t, up_acc, down_acc,
):
    eye = identity()

    def brick(s, _):
        live = (counts[0] > s).astype(F32)
        place = parent[s] * 64 + child[s]
        held = (counts[0] > s) & (parent[s] >= 0) & (place >= 0)
        valid = held.astype(F32)
        live_in = feat[s].astype(F32) * live
        mine = live_in.T
        rows = got[:, pl.ds(pl.multiple_of(s * 16, 16), 16), :].reshape(512, 128)
        pc[...] = nn(unpack[...], rows)
        for a in range(8):
            s1[pl.ds(8 + ((a + 1) * 10 + 1) * 8, 64), :] = mine[a * 64 : a * 64 + 64]
            for d, b in (((0, -1, 0), 0), ((0, 1, 0), 9)):
                s1[pl.ds(8 + ((a + 1) * 10 + b) * 8, 8), :] = pc[pl.ds(PIECE[d] + 8 * a, 8), :]
        for a, x in ((-1, 0), (1, 9)):
            s1[pl.ds(8 + (x * 10 + 1) * 8, 64), :] = pc[pl.ds(PIECE[a, 0, 0], 64), :]
            for b, y in ((-1, 0), (1, 9)):
                s1[pl.ds(8 + (x * 10 + y) * 8, 8), :] = pc[pl.ds(PIECE[a, b, 0], 8), :]
        s0[...] = s1[pl.ds(7, 800), :]
        s2[...] = s1[pl.ds(9, 800), :]
        for c, ref, lane in ((-1, s0, 0), (1, s2, 7)):
            for a in range(8):
                ref[pl.ds(((a + 1) * 10 + 1) * 8 + lane, 8, stride=8), :] = pc[
                    pl.ds(PIECE[0, 0, c] + 8 * a, 8), :
                ]
            for a, x in ((-1, 0), (1, 9)):
                ref[pl.ds((x * 10 + 1) * 8 + lane, 8, stride=8), :] = pc[
                    pl.ds(PIECE[a, 0, c], 8), :
                ]
                ref[pl.ds((10 + x) * 8 + lane, 8, stride=80), :] = pc[pl.ds(PIECE[0, a, c], 8), :]
                for b, y in ((-1, 0), (1, 9)):
                    ref[pl.ds((x * 10 + y) * 8 + lane, 1), :] = pc[pl.ds(PIECE[a, b, c], 1), :]

        def plane(a, _):
            for b in range(3):
                for c, ref in enumerate((s0, s1, s2)):
                    start = pl.multiple_of((a * 10 + b) * 8 + (8 if c == 1 else 0), 8)
                    cols[s, pl.ds(pl.multiple_of(a * 64, 64), 64), pl.ds((3 * b + c) * 128, 128)] = ref[
                        pl.ds(start, 64), :
                    ].astype(BF)
            return 0

        lax.fori_loop(0, 10, plane, 0)
        pre = nn(cols[s, 0:512, :], weight[0])
        pre = pre + nn(cols[s, 64:576, :], weight[1])
        pre = pre + nn(cols[s, 128:640, :], weight[2])
        pre = pre.T
        gate = 1.0 / (1.0 + jnp.exp(-pre))
        active = pre * gate
        slope = gate * (1.0 + pre * (1.0 - gate))
        grad_in = gout[s].astype(F32) * live
        high = active.astype(BF)
        low = (active - high.astype(F32)).astype(BF)
        pooled = (nt(pool[...], high) + nt(pool[...], low)) * (1.0 / 64.0)
        coarse_in = (pooled * valid).astype(BF)
        coarse_pre = nn(coarse_in, up[...])
        coarse_gate = 1.0 / (1.0 + jnp.exp(-coarse_pre))
        coarse_mid = (coarse_pre * coarse_gate).astype(BF)
        coarse_out = nn(coarse_mid, down[...]).astype(BF)
        grad_coarse = (nt(pool[...], grad_in.astype(BF)) * valid).astype(BF)
        grad_mid = nt(grad_coarse, down[...])
        grad_pre = (
            grad_mid * (coarse_gate * (1.0 + coarse_pre * (1.0 - coarse_gate)))
        ).astype(BF)
        grad_cin = nt(grad_pre, up[...]).astype(BF)
        lifted = nn(nt(eye, coarse_out).astype(BF), pool[...])
        out[s] = (live_in + active + lifted).astype(BF)
        back = nn(nt(eye, grad_cin).astype(BF), pool[...])
        grad_pre_conv = (grad_in + back * (1.0 / 64.0)) * slope
        grad_t[s] = grad_pre_conv.astype(BF)
        grad[s] = grad_pre_conv.T.astype(BF)
        up_acc[s] = nn(nt(eye, coarse_in).astype(BF), grad_pre)
        for h in range(2):
            down_acc[s, h * 128 : h * 128 + 128, :] = nn(
                nt(eye, coarse_mid[:, h * 128 : h * 128 + 128]).astype(BF), grad_coarse
            )
        return 0

    lax.fori_loop(0, 2, brick, 0)
    mine = core[0]

    def put(block, value):
        half, at = divmod(block, 16)
        wsum[half ^ mine, pl.ds(at * 128, 128), :] = value.astype(BF)

    for a in range(3):
        total = nn(grad_t[0], cols[0, a * 64 : a * 64 + 512, :])
        total = total + nn(grad_t[1], cols[1, a * 64 : a * 64 + 512, :])
        total = total.astype(BF)
        for n in range(9):
            put(9 * a + n, nt(eye, total[:, n * 128 : n * 128 + 128]))
    up_all = up_acc[0] + up_acc[1]
    down_all = down_acc[0] + down_acc[1]
    for h in range(2):
        put(27 + h, up_all[:, h * 128 : h * 128 + 128])
        put(29 + h, down_all[h * 128 : h * 128 + 128, :])
    put(31, jnp.zeros((128, 128), F32))


def backward_kernel(grad, weight, pack, own, msg, planes, acc, pc):
    planes[0:128, :] = jnp.zeros((128, 128), BF)
    planes[640:768, :] = jnp.zeros((128, 128), BF)
    pc[488:512, :] = jnp.zeros((24, 128), F32)
    low = (lax.broadcasted_iota(jnp.int32, (64, 1), 0) & 7) != 0
    high = (lax.broadcasted_iota(jnp.int32, (64, 1), 0) & 7) != 7

    def brick(s, _):
        planes[128:640, :] = grad[s]
        acc[...] = jnp.zeros_like(acc)

        def tap(n, _):
            c = lax.rem(n, 3)
            b = lax.div(n, 3)
            part = nt(planes[128:768, :], weight[n])
            part = part + nt(planes[64:704, :], weight[n + 9])
            part = part + nt(planes[0:640, :], weight[n + 18])
            for a in range(10):
                at = pl.ds(pl.multiple_of(8 + (a * 10 + b) * 8, 8), 64)
                acc[c, at, :] = acc[c, at, :] + part[a * 64 : a * 64 + 64]
            return 0

        lax.fori_loop(0, 9, tap, 0)

        def middle(row, size):
            at = 8 + row
            total = acc[1, pl.ds(at, size), :]
            total = total + jnp.where(high[:size], acc[0, pl.ds(at + 1, size), :], 0.0)
            return total + jnp.where(low[:size], acc[2, pl.ds(at - 1, size), :], 0.0)

        for a in range(8):
            own[s, pl.ds(a * 64, 64), :] = middle(((a + 1) * 10 + 1) * 8, 64)
            for d, b in (((0, -1, 0), 0), ((0, 1, 0), 9)):
                pc[pl.ds(PIECE[d] + 8 * a, 8), :] = middle(((a + 1) * 10 + b) * 8, 8)
        for a, x in ((-1, 0), (1, 9)):
            pc[pl.ds(PIECE[a, 0, 0], 64), :] = middle((x * 10 + 1) * 8, 64)
            for b, y in ((-1, 0), (1, 9)):
                pc[pl.ds(PIECE[a, b, 0], 8), :] = middle((x * 10 + y) * 8, 8)
        for c, ref, lane in ((-1, acc.at[0], 8), (1, acc.at[2], 15)):
            for a in range(8):
                pc[pl.ds(PIECE[0, 0, c] + 8 * a, 8), :] = ref[
                    pl.ds(((a + 1) * 10 + 1) * 8 + lane, 8, stride=8), :
                ]
            for a, x in ((-1, 0), (1, 9)):
                pc[pl.ds(PIECE[a, 0, c], 8), :] = ref[
                    pl.ds((x * 10 + 1) * 8 + lane, 8, stride=8), :
                ]
                pc[pl.ds(PIECE[0, a, c], 8), :] = ref[pl.ds((10 + x) * 8 + lane, 8, stride=80), :]
                for b, y in ((-1, 0), (1, 9)):
                    pc[pl.ds(PIECE[a, b, c], 1), :] = ref[pl.ds((x * 10 + y) * 8 + lane, 1), :]
        sent = nn(pack[...], pc[...].astype(BF)).astype(BF)
        msg[:, pl.ds(pl.multiple_of(s * 16, 16), 16), :] = sent.reshape(32, 16, 128)
        return 0

    lax.fori_loop(0, 2, brick, 0)


def merge_kernel(got, table, out):
    part = lax.broadcasted_iota(jnp.int32, (1, 1024), 1) & 15
    target = table[0:1, :].astype(jnp.int32) * 16 + part
    rows = lax.broadcasted_iota(jnp.int32, (128, 1024), 0)
    data = got[:, 0:32, :].reshape(1024, 128)
    share = jnp.sum(got[:, 32:48, :].astype(F32), axis=0).astype(BF)

    def step(n, _):
        hot = (rows + n * 128 == target).astype(F32).astype(BF)
        total = nn(hot, data).astype(BF).reshape(4, 32, 128)
        at = pl.ds(pl.multiple_of(n * 4, 4), 4)
        out[at, 0:32, :] = total
        out[at, 32:48, :] = jnp.broadcast_to(share[None], (4, 16, 128))
        return 0

    lax.fori_loop(0, 8, step, 0)


def finish_kernel(counts, got, own, gout, give, out):
    for s in range(2):
        live = (counts[0] > s).astype(F32)
        rows = got[:, 16 * s : 16 * s + 16, :].reshape(512, 128)
        total = own[s] + nn(give[...], rows)
        out[s] = (total.T + gout[s].astype(F32) * live).astype(BF)


VM = pl.BlockSpec(memory_space=pltpu.VMEM)
SM = pl.BlockSpec(memory_space=pltpu.SMEM)


def call(kernel, shapes, scalars, arrays, scratch=(), flops=1e6, name=None):
    moved = sum(x.size * x.dtype.itemsize for x in arrays)
    moved += sum(int(np.prod(s.shape)) * s.dtype.itemsize for s in shapes)
    outs = pl.pallas_call(
        kernel,
        out_shape=shapes,
        in_specs=[SM] * len(scalars) + [VM] * len(arrays),
        out_specs=[VM] * len(shapes),
        scratch_shapes=list(scratch),
        compiler_params=pltpu.CompilerParams(vmem_limit_bytes=40 * 2**20),
        cost_estimate=pl.CostEstimate(
            flops=int(flops), bytes_accessed=int(moved), transcendentals=0
        ),
        name=name,
    )(*scalars, *arrays)
    return outs


def shape(dims, dtype):
    return jax.ShapeDtypeStruct(dims, dtype)


def on_device(
    features,
    grad_out,
    conv_weight,
    coarse_up,
    coarse_down,
    counts,
    neighbour_owner,
    neighbour_slot,
    parent,
    child_slot,
):
    grp = lax.axis_index("grp").astype(jnp.int32)
    core = lax.rem(grp, 2)
    line = lax.div(grp, 2)
    bricks = jnp.where(neighbour_owner >= 0, neighbour_owner * 2 + neighbour_slot, -1)
    bricks = jnp.pad(bricks.astype(BF), ((0, 126), (0, 102)))
    (msg,) = call(
        ask_kernel,
        [shape((32, 48, 128), BF)],
        [counts],
        [features, bricks, jnp.asarray(TAKE, BF), jnp.asarray(ASK, BF)],
        flops=2e8,
        name="ask",
    )
    first = lax.all_to_all(msg, "dev", split_axis=0, concat_axis=0, tiled=True)
    (answer,) = call(route_kernel, [shape((32, 32, 128), BF)], [], [first], flops=3e8, name="route")
    halo = lax.all_to_all(answer, "dev", split_axis=0, concat_axis=0, tiled=True)
    table = first[:, 32:48, 0:2].transpose(0, 2, 1).reshape(1, 1024).astype(F32)
    table = jnp.broadcast_to(table, (8, 1024))
    output, grad_pre, wsum = call(
        forward_kernel,
        [shape((2, 128, 512), BF), shape((2, 512, 128), BF), shape((2, 2048, 128), BF)],
        [counts, parent, child_slot, core.reshape(1)],
        [
            features,
            halo,
            grad_out,
            conv_weight.reshape(3, 1152, 128),
            coarse_up,
            coarse_down,
            jnp.asarray(UNPACK, BF),
            jnp.asarray(POOL, BF),
        ],
        [
            pltpu.VMEM((512, 128), F32),
            pltpu.VMEM((800, 128), F32),
            pltpu.VMEM((816, 128), F32),
            pltpu.VMEM((800, 128), F32),
            pltpu.VMEM((2, 640, 1152), BF),
            pltpu.VMEM((2, 128, 512), BF),
            pltpu.VMEM((2, 128, 256), F32),
            pltpu.VMEM((2, 256, 128), F32),
        ],
        flops=2e9,
        name="forward",
    )
    other = lax.ppermute(wsum[1], "grp", [(i, i ^ 1) for i in range(8)])
    pair = (wsum[0].astype(F32) + other.astype(F32)).reshape(4, 512, 128)
    chunk = lax.dynamic_index_in_dim(pair, line, 0, keepdims=False)
    pair = pair.astype(BF)
    for step in (1, 2, 3):
        away = lax.dynamic_index_in_dim(pair, lax.rem(line + step, 4), 0, keepdims=False)
        away = lax.ppermute(away, "grp", [(i, (i + 2 * step) % 8) for i in range(8)])
        chunk = chunk + away.astype(F32)
    own, terms = call(
        backward_kernel,
        [shape((2, 512, 128), F32), shape((32, 32, 128), BF)],
        [],
        [grad_pre, conv_weight, jnp.asarray(PACK, BF)],
        [
            pltpu.VMEM((768, 128), BF),
            pltpu.VMEM((3, 816, 128), F32),
            pltpu.VMEM((512, 128), F32),
        ],
        flops=4e9,
        name="backward",
    )
    terms = jnp.concatenate([terms, chunk.astype(BF).reshape(32, 16, 128)], axis=1)
    terms = lax.all_to_all(terms, "dev", split_axis=0, concat_axis=0, tiled=True)
    (sums,) = call(
        merge_kernel, [shape((32, 48, 128), BF)], [], [terms, table], flops=3e8, name="merge"
    )
    back = lax.all_to_all(sums, "dev", split_axis=0, concat_axis=0, tiled=True)
    chunk = back[:, 32:48, :].reshape(512, 128)
    parts = [chunk]
    for step in (1, 2, 3):
        parts.append(lax.ppermute(chunk, "grp", [(i, (i - 2 * step) % 8) for i in range(8)]))
    (grad_features,) = call(
        finish_kernel,
        [shape((2, 128, 512), BF)],
        [counts],
        [back, own, grad_out, jnp.asarray(GIVE, BF)],
        flops=3e8,
        name="finish",
    )
    half = jnp.stack(parts)
    half = jnp.take(half, lax.rem(jnp.arange(4) - line + 4, 4), axis=0).reshape(2048, 128)
    other = lax.ppermute(half, "grp", [(i, i ^ 1) for i in range(8)])
    first_half = jnp.where(core == 0, half, other)
    second_half = jnp.where(core == 0, other, half)
    weights = jnp.concatenate([first_half, second_half]).astype(F32).reshape(32, 128, 128)
    grad_conv = weights[:27]
    grad_up = jnp.concatenate([weights[27], weights[28]], axis=1)
    grad_down = jnp.concatenate([weights[29], weights[30]], axis=0)
    return (output, grad_features, grad_conv, grad_up, grad_down)


def solution(mesh):
    return jax.shard_map(
        on_device,
        mesh=mesh,
        in_specs=(
            P(("grp", "dev"), None, None),
            P(("grp", "dev"), None, None),
            P(),
            P(),
            P(),
            P(("grp", "dev")),
            P(("grp", "dev"), None),
            P(("grp", "dev"), None),
            P(("grp", "dev")),
            P(("grp", "dev")),
        ),
        out_specs=(P(("grp", "dev"), None, None), P(("grp", "dev"), None, None), P(), P(), P()),
        check_vma=False,
    )
```

```python
import functools

import jax
import jax.numpy as jnp
import numpy as np
from jax import lax
from jax.experimental import pallas as pl
from jax.experimental.pallas import tpu as pltpu
from jax.sharding import PartitionSpec as P

BF = jnp.bfloat16
F32 = jnp.float32

OFFSETS = [
    (a, b, c) for a in (-1, 0, 1) for b in (-1, 0, 1) for c in (-1, 0, 1) if (a, b, c) != (0, 0, 0)
]
FACES = [d for d in OFFSETS if sum(map(abs, d)) == 1]
EDGES = [d for d in OFFSETS if sum(map(abs, d)) == 2]
CORNERS = [d for d in OFFSETS if sum(map(abs, d)) == 3]
PIECE = {d: 64 * n for n, d in enumerate(FACES)}
PIECE.update({d: 384 + 8 * n for n, d in enumerate(EDGES)})
PIECE.update({d: 480 + n for n, d in enumerate(CORNERS)})


def piece_row(i, q):
    if q < 12:
        face = q // 2
        return 64 * face + 2 * i + q % 2, OFFSETS.index(FACES[face])
    if q < 15:
        flat = 32 * (q - 12) + i
        return 384 + flat, OFFSETS.index(EDGES[flat // 8])
    return 480 + i // 4, OFFSETS.index(CORNERS[i // 4])


def cut(step):
    return [7] if step < 0 else ([0] if step > 0 else list(range(8)))


def tables():
    voxel = np.full(512, -1)
    for (a, b, c), base in PIECE.items():
        cells = [x * 64 + y * 8 + z for x in cut(a) for y in cut(b) for z in cut(c)]
        voxel[base : base + len(cells)] = cells
    take = np.zeros((512, 512), np.float32)
    pack = np.zeros((512, 512), np.float32)
    unpack = np.zeros((512, 512), np.float32)
    give = np.zeros((512, 512), np.float32)
    ask = np.zeros((512, 128), np.float32)
    for i in range(32):
        for q in range(16):
            row, direction = piece_row(i, q)
            at = 16 * i + q
            take[at, voxel[row]] = 1
            pack[at, row] = 1
            ask[at, direction] = 1
            if q < 15 or i % 4 == 0:
                unpack[row, at] = 1
                give[voxel[row], at] = 1
    pool = np.zeros((2, 16, 512), np.float32)
    for v in range(512):
        a, b, c = v // 64, v // 8 % 8, v % 8
        at = (a // 4) * 4 + (b // 4) * 2 + c // 4
        pool[0, at, v] = pool[1, 8 + at, v] = 1
    return take, pack, unpack, give, ask, pool


TAKE, PACK, UNPACK, GIVE, ASK, POOL = tables()


def nn(x, y):
    return lax.dot_general(x, y, (((1,), (0,)), ((), ())), preferred_element_type=F32)


def nt(x, y):
    return lax.dot_general(x, y, (((1,), (1,)), ((), ())), preferred_element_type=F32)


def identity():
    rows = lax.broadcasted_iota(jnp.int32, (128, 128), 0)
    lanes = lax.broadcasted_iota(jnp.int32, (128, 128), 1)
    return (rows == lanes).astype(F32).astype(BF)


def ask_kernel(
    counts, feat, owner, slot, take, ask, msg, feat_v, owner_v, slot_v, take_v, ask_v, bricks, sems
):
    pairs = ((owner, owner_v), (slot, slot_v), (ask, ask_v), (feat, feat_v), (take, take_v))
    copies = [
        pltpu.make_async_copy(src, dst, sems.at[n]) for n, (src, dst) in enumerate(pairs)
    ]
    for copy in copies:
        copy.start()
    bricks[...] = jnp.zeros((128, 128), F32)
    copies[0].wait()
    copies[1].wait()
    named = jnp.where(owner_v[...] >= 0, owner_v[...] * 2 + slot_v[...], -1)
    bricks[0:2, 0:26] = named.astype(F32)
    copies[2].wait()
    rows = nt(ask_v[...], bricks[...].astype(BF)).astype(BF)
    msg[:, 32:48, :] = rows.reshape(32, 16, 128)
    copies[3].wait()
    copies[4].wait()
    for s in range(2):
        live = (counts[0] > s).astype(F32)
        held = nt(take_v[...], feat_v[s]) * live
        msg[:, 16 * s : 16 * s + 16, :] = held.astype(BF).reshape(32, 16, 128)


def same_part():
    rows = lax.broadcasted_iota(jnp.int32, (16, 128), 0)
    lanes = lax.broadcasted_iota(jnp.int32, (16, 128), 1) & 15
    return (rows == lanes).astype(F32).astype(BF)


def route_kernel(got, out, hot):
    same = jnp.broadcast_to(same_part()[None], (32, 16, 128))
    zero = jnp.zeros((32, 16, 128), BF)
    lanes = lax.broadcasted_iota(jnp.int32, (128, 128), 0)
    brick = lax.broadcasted_iota(jnp.int32, (16, 128), 1) >> 4
    table = got[:, 32:48, :].reshape(512, 128)
    data = got[:, 0:32, :].reshape(1024, 128)
    for s in range(2):
        spread = (lanes == s).astype(F32).astype(BF)
        asked = nn(table, spread).astype(BF).reshape(32, 16, 128)
        for n in range(8):
            here = (brick + 8 * n).astype(F32).astype(BF)
            hot[:, n * 128 : n * 128 + 128] = jnp.where(asked == here[None], same, zero).reshape(
                512, 128
            )
        picked = nn(hot[...], data).astype(BF)
        out[:, 16 * s : 16 * s + 16, :] = picked.reshape(32, 16, 128)


def prepare_kernel(counts, feat, gout, down, pool, mine, grad_coarse, grad_mid):
    pooled = jnp.zeros((16, 128), F32)
    for s in range(2):
        live = (counts[0] > s).astype(F32)
        mine[s] = (feat[s].astype(F32) * live).T
        pooled = pooled + nt(pool[s], gout[s]) * live
    grad_coarse[...] = pooled.astype(BF)
    grad_mid[...] = nt(grad_coarse[...], down[...])


def forward_kernel(
    counts, parent, child, core, feat, mine, grad_coarse, grad_mid, got, gout, weight, up, down,
    unpack, pool,
    out, grad, wsum,
    pc, s0, s1, s2, cols, grad_t, acts, slopes, pooled,
):
    eye = identity()
    pooled[...] = jnp.zeros((16, 128), F32)

    def brick(s, _):
        rows = got[:, pl.ds(pl.multiple_of(s * 16, 16), 16), :].reshape(512, 128)
        pc[...] = nn(unpack[...], rows)
        for a in range(8):
            s1[pl.ds(8 + ((a + 1) * 10 + 1) * 8, 64), :] = mine[s, a * 64 : a * 64 + 64, :]
            for d, b in (((0, -1, 0), 0), ((0, 1, 0), 9)):
                s1[pl.ds(8 + ((a + 1) * 10 + b) * 8, 8), :] = pc[pl.ds(PIECE[d] + 8 * a, 8), :]
        for a, x in ((-1, 0), (1, 9)):
            s1[pl.ds(8 + (x * 10 + 1) * 8, 64), :] = pc[pl.ds(PIECE[a, 0, 0], 64), :]
            for b, y in ((-1, 0), (1, 9)):
                s1[pl.ds(8 + (x * 10 + y) * 8, 8), :] = pc[pl.ds(PIECE[a, b, 0], 8), :]
        s0[...] = s1[pl.ds(7, 800), :]
        s2[...] = s1[pl.ds(9, 800), :]
        for c, ref, lane in ((-1, s0, 0), (1, s2, 7)):
            for a in range(8):
                ref[pl.ds(((a + 1) * 10 + 1) * 8 + lane, 8, stride=8), :] = pc[
                    pl.ds(PIECE[0, 0, c] + 8 * a, 8), :
                ]
            for a, x in ((-1, 0), (1, 9)):
                ref[pl.ds((x * 10 + 1) * 8 + lane, 8, stride=8), :] = pc[
                    pl.ds(PIECE[a, 0, c], 8), :
                ]
                ref[pl.ds((10 + x) * 8 + lane, 8, stride=80), :] = pc[pl.ds(PIECE[0, a, c], 8), :]
                for b, y in ((-1, 0), (1, 9)):
                    ref[pl.ds((x * 10 + y) * 8 + lane, 1), :] = pc[pl.ds(PIECE[a, b, c], 1), :]

        def plane(a, _):
            for b in range(3):
                for c, ref in enumerate((s0, s1, s2)):
                    start = pl.multiple_of((a * 10 + b) * 8 + (8 if c == 1 else 0), 8)
                    cols[s, pl.ds(pl.multiple_of(a * 64, 64), 64), pl.ds((3 * b + c) * 128, 128)] = ref[
                        pl.ds(start, 64), :
                    ].astype(BF)
            return 0

        lax.fori_loop(0, 10, plane, 0)
        pre = nn(cols[s, 0:512, :], weight[0])
        pre = pre + nn(cols[s, 64:576, :], weight[1])
        pre = pre + nn(cols[s, 128:640, :], weight[2])
        pre = pre.T
        gate = 1.0 / (1.0 + jnp.exp(-pre))
        active = pre * gate
        acts[s] = active
        slopes[s] = gate * (1.0 + pre * (1.0 - gate))
        high = active.astype(BF)
        low = (active - high.astype(F32)).astype(BF)
        pooled[...] += nt(pool[s], high) + nt(pool[s], low)
        return 0

    lax.fori_loop(0, 2, brick, 0)
    second = lax.broadcasted_iota(jnp.int32, (16, 1), 0) >= 8
    valid = [
        (
            (counts[0] > s) & (parent[s] >= 0) & (parent[s] * 64 + child[s] >= 0)
        ).astype(F32)
        for s in range(2)
    ]
    valid = jnp.where(second, valid[1], valid[0])
    coarse_in = (pooled[...] * (1.0 / 64.0) * valid).astype(BF)
    grad_out = (grad_coarse[...].astype(F32) * valid).astype(BF)
    coarse_pre = nn(coarse_in, up[...])
    gate = 1.0 / (1.0 + jnp.exp(-coarse_pre))
    coarse_mid = (coarse_pre * gate).astype(BF)
    grad_pre = grad_mid[...] * valid * (gate * (1.0 + coarse_pre * (1.0 - gate)))
    grad_pre = grad_pre.astype(BF)
    coarse_out = nn(coarse_mid, down[...]).astype(BF)
    grad_cin = nt(grad_pre, up[...]).astype(BF)
    lift = nt(eye, coarse_out).astype(BF)
    back = nt(eye, grad_cin).astype(BF)

    def blend(s, _):
        live = (counts[0] > s).astype(F32)
        out[s] = (feat[s].astype(F32) * live + acts[s] + nn(lift, pool[s])).astype(BF)
        grad_in = gout[s].astype(F32) * live + nn(back, pool[s]) * (1.0 / 64.0)
        grad_pre_conv = grad_in * slopes[s]
        grad_t[s] = grad_pre_conv.astype(BF)
        grad[s] = grad_pre_conv.T.astype(BF)
        return 0

    lax.fori_loop(0, 2, blend, 0)
    mine_core = core[0]

    def put(block, value):
        half, at = divmod(block, 16)
        wsum[half ^ mine_core, pl.ds(at * 128, 128), :] = value.astype(BF)

    grad_up = nn(nt(eye, coarse_in).astype(BF), grad_pre)
    for h in range(2):
        put(27 + h, grad_up[:, h * 128 : h * 128 + 128])
        middle = nt(eye, coarse_mid[:, h * 128 : h * 128 + 128]).astype(BF)
        put(29 + h, nn(middle, grad_out))
    put(31, jnp.zeros((128, 128), F32))
    for a in range(3):
        total = nn(grad_t[0], cols[0, a * 64 : a * 64 + 512, :])
        total = total + nn(grad_t[1], cols[1, a * 64 : a * 64 + 512, :])
        total = total.astype(BF)
        for n in range(9):
            put(9 * a + n, nt(eye, total[:, n * 128 : n * 128 + 128]))


def pair_kernel(line, wsum, other, own, one, two, three):
    for step, ref in enumerate((own, one, two, three)):
        at = pl.ds(pl.multiple_of(((line[0] + step) & 3) * 512, 512), 512)
        ref[...] = (wsum[0, at, :].astype(F32) + other[at, :].astype(F32)).astype(ref.dtype)


def backward_kernel(s, grad, weight, pack, own, msg, planes, acc, pc):
    planes[0:128, :] = jnp.zeros((128, 128), BF)
    planes[640:768, :] = jnp.zeros((128, 128), BF)
    planes[128:640, :] = grad[s]
    pc[488:512, :] = jnp.zeros((24, 128), F32)
    acc[...] = jnp.zeros_like(acc)
    low = (lax.broadcasted_iota(jnp.int32, (64, 1), 0) & 7) != 0
    high = (lax.broadcasted_iota(jnp.int32, (64, 1), 0) & 7) != 7

    def tap(n, _):
        c = lax.rem(n, 3)
        b = lax.div(n, 3)
        part = nt(planes[128:768, :], weight[n])
        part = part + nt(planes[64:704, :], weight[n + 9])
        part = part + nt(planes[0:640, :], weight[n + 18])
        for a in range(10):
            at = pl.ds(pl.multiple_of(8 + (a * 10 + b) * 8, 8), 64)
            acc[c, at, :] = acc[c, at, :] + part[a * 64 : a * 64 + 64]
        return 0

    lax.fori_loop(0, 9, tap, 0)

    def middle(row, size):
        at = 8 + row
        total = acc[1, pl.ds(at, size), :]
        total = total + jnp.where(high[:size], acc[0, pl.ds(at + 1, size), :], 0.0)
        return total + jnp.where(low[:size], acc[2, pl.ds(at - 1, size), :], 0.0)

    for a in range(8):
        own[pl.ds(a * 64, 64), :] = middle(((a + 1) * 10 + 1) * 8, 64)
        for d, b in (((0, -1, 0), 0), ((0, 1, 0), 9)):
            pc[pl.ds(PIECE[d] + 8 * a, 8), :] = middle(((a + 1) * 10 + b) * 8, 8)
    for a, x in ((-1, 0), (1, 9)):
        pc[pl.ds(PIECE[a, 0, 0], 64), :] = middle((x * 10 + 1) * 8, 64)
        for b, y in ((-1, 0), (1, 9)):
            pc[pl.ds(PIECE[a, b, 0], 8), :] = middle((x * 10 + y) * 8, 8)
    for c, ref, lane in ((-1, acc.at[0], 8), (1, acc.at[2], 15)):
        for a in range(8):
            pc[pl.ds(PIECE[0, 0, c] + 8 * a, 8), :] = ref[
                pl.ds(((a + 1) * 10 + 1) * 8 + lane, 8, stride=8), :
            ]
        for a, x in ((-1, 0), (1, 9)):
            pc[pl.ds(PIECE[a, 0, c], 8), :] = ref[pl.ds((x * 10 + 1) * 8 + lane, 8, stride=8), :]
            pc[pl.ds(PIECE[0, a, c], 8), :] = ref[pl.ds((10 + x) * 8 + lane, 8, stride=80), :]
            for b, y in ((-1, 0), (1, 9)):
                pc[pl.ds(PIECE[a, b, c], 1), :] = ref[pl.ds((x * 10 + y) * 8 + lane, 1), :]
    msg[...] = nn(pack[...], pc[...].astype(BF)).astype(BF).reshape(32, 16, 128)


def join_kernel(zero, one, own, away1, away2, away3, msg):
    msg[:, 0:16, :] = zero[...]
    msg[:, 16:32, :] = one[...]
    total = own[...] + away1[...].astype(F32) + away2[...].astype(F32) + away3[...].astype(F32)
    msg[:, 32:48, :] = total.astype(BF).reshape(32, 16, 128)


def merge_kernel(got, table, out, hot):
    same = same_part()
    zero = jnp.zeros((16, 128), BF)
    share = jnp.sum(got[:, 32:48, :].astype(F32), axis=0).astype(BF)
    out[:, 32:48, :] = jnp.broadcast_to(share[None], (32, 16, 128))
    for n in range(8):
        asked = table[:, n * 128 : n * 128 + 128]
        for brick in range(64):
            hot[brick * 16 : brick * 16 + 16, n * 128 : n * 128 + 128] = jnp.where(
                asked == jnp.full((16, 128), brick, BF), same, zero
            )
    total = nn(hot[...], got[:, 0:32, :].reshape(1024, 128))
    out[:, 0:32, :] = total.astype(BF).reshape(32, 32, 128)


def finish_kernel(counts, got, own0, own1, gout, give, out):
    for s, own in enumerate((own0, own1)):
        live = (counts[0] > s).astype(F32)
        rows = got[:, 16 * s : 16 * s + 16, :].reshape(512, 128)
        total = own[...] + nn(give[...], rows)
        out[s] = (total.T + gout[s].astype(F32) * live).astype(BF)


def assemble_kernel(core, line, *refs):
    parts, (conv, up, down) = refs[:8], refs[8:]
    for n, part in enumerate(parts):
        half = core[0] ^ (n // 4)
        first = half * 16 + ((line[0] + n % 4) & 3) * 4

        def block(at):
            return part[at * 128 : at * 128 + 128, :].astype(F32)

        @pl.when(first < 24)
        def _():
            for at in range(4):
                conv[first + at] = block(at)

        @pl.when(first == 24)
        def _():
            for at in range(3):
                conv[24 + at] = block(at)
            up[:, 0:128] = block(3)

        @pl.when(first == 28)
        def _():
            up[:, 128:256] = block(0)
            down[0:128, :] = block(1)
            down[128:256, :] = block(2)


VM = pl.BlockSpec(memory_space=pltpu.VMEM)
SM = pl.BlockSpec(memory_space=pltpu.SMEM)


def call(kernel, shapes, scalars, arrays, scratch=(), flops=1e6, space=VM, limit=20, name=None):
    moved = sum(x.size * x.dtype.itemsize for x in arrays)
    moved += sum(int(np.prod(s.shape)) * s.dtype.itemsize for s in shapes)
    return pl.pallas_call(
        kernel,
        out_shape=shapes,
        in_specs=[SM] * len(scalars) + [space] * len(arrays),
        out_specs=[VM] * len(shapes),
        scratch_shapes=list(scratch),
        compiler_params=pltpu.CompilerParams(vmem_limit_bytes=limit * 2**20),
        cost_estimate=pl.CostEstimate(
            flops=int(flops), bytes_accessed=int(moved), transcendentals=0
        ),
        name=name,
    )(*scalars, *arrays)


def shape(dims, dtype):
    return jax.ShapeDtypeStruct(dims, dtype)


def on_device(
    features,
    grad_out,
    conv_weight,
    coarse_up,
    coarse_down,
    counts,
    neighbour_owner,
    neighbour_slot,
    parent,
    child_slot,
):
    grp = lax.axis_index("grp").astype(jnp.int32)
    core = (grp & 1).reshape(1)
    line = (grp >> 1).reshape(1)
    pool = jnp.asarray(POOL, BF)
    swap = [(i, i ^ 1) for i in range(8)]
    (msg,) = call(
        ask_kernel,
        [shape((32, 48, 128), BF)],
        [counts],
        [features, neighbour_owner, neighbour_slot, jnp.asarray(TAKE, BF), jnp.asarray(ASK, BF)],
        [
            pltpu.VMEM((2, 128, 512), BF),
            pltpu.VMEM((2, 26), jnp.int32),
            pltpu.VMEM((2, 26), jnp.int32),
            pltpu.VMEM((512, 512), BF),
            pltpu.VMEM((512, 128), BF),
            pltpu.VMEM((128, 128), F32),
            pltpu.SemaphoreType.DMA((5,)),
        ],
        flops=2e8,
        space=pl.BlockSpec(memory_space=pltpu.HBM),
        name="ask",
    )
    first = lax.all_to_all(msg, "dev", split_axis=0, concat_axis=0, tiled=True)
    (answer,) = call(
        route_kernel,
        [shape((32, 32, 128), BF)],
        [],
        [first],
        [pltpu.VMEM((512, 1024), BF)],
        flops=3e8,
        name="route",
    )
    halo = lax.all_to_all(answer, "dev", split_axis=0, concat_axis=0, tiled=True)
    table = first[:, 32:48, 0:2].transpose(0, 2, 1).reshape(1, 1024)
    table = jnp.broadcast_to(table, (16, 1024))
    mine, grad_coarse, grad_mid = call(
        prepare_kernel,
        [shape((2, 512, 128), F32), shape((16, 128), BF), shape((16, 256), F32)],
        [counts],
        [features, grad_out, coarse_down, pool],
        flops=1e8,
        name="prepare",
    )
    output, grad_pre, wsum = call(
        forward_kernel,
        [shape((2, 128, 512), BF), shape((2, 512, 128), BF), shape((2, 2048, 128), BF)],
        [counts, parent, child_slot, core],
        [
            features,
            mine,
            grad_coarse,
            grad_mid,
            halo,
            grad_out,
            conv_weight.reshape(3, 1152, 128),
            coarse_up,
            coarse_down,
            jnp.asarray(UNPACK, BF),
            pool,
        ],
        [
            pltpu.VMEM((512, 128), F32),
            pltpu.VMEM((800, 128), F32),
            pltpu.VMEM((816, 128), F32),
            pltpu.VMEM((800, 128), F32),
            pltpu.VMEM((2, 640, 1152), BF),
            pltpu.VMEM((2, 128, 512), BF),
            pltpu.VMEM((2, 128, 512), F32),
            pltpu.VMEM((2, 128, 512), F32),
            pltpu.VMEM((16, 128), F32),
        ],
        flops=2e9,
        name="forward",
    )

    def backward(s, grad):
        return call(
            functools.partial(backward_kernel, s),
            [shape((512, 128), F32), shape((32, 16, 128), BF)],
            [],
            [grad, conv_weight, jnp.asarray(PACK, BF)],
            [
                pltpu.VMEM((768, 128), BF),
                pltpu.VMEM((3, 816, 128), F32),
                pltpu.VMEM((512, 128), F32),
            ],
            flops=2e9,
            name="backward",
        )

    other = lax.ppermute(wsum[1], "grp", swap)
    own0, terms0 = backward(0, grad_pre)
    own_sum, *away = call(
        pair_kernel,
        [shape((512, 128), F32)] + [shape((512, 128), BF)] * 3,
        [line],
        [wsum, other],
        name="pair",
    )
    grad_pre, own_sum = lax.optimization_barrier((grad_pre, own_sum))
    away = [
        lax.ppermute(x, "grp", [(i, (i + 2 * step) % 8) for i in range(8)])
        for step, x in zip((1, 2, 3), away)
    ]
    own1, terms1 = backward(1, grad_pre)
    (terms,) = call(
        join_kernel,
        [shape((32, 48, 128), BF)],
        [],
        [terms0, terms1, own_sum, *away],
        name="join",
    )
    terms = lax.all_to_all(terms, "dev", split_axis=0, concat_axis=0, tiled=True)
    (sums,) = call(
        merge_kernel,
        [shape((32, 48, 128), BF)],
        [],
        [terms, table],
        [pltpu.VMEM((1024, 1024), BF)],
        flops=3e8,
        name="merge",
    )
    back = lax.all_to_all(sums, "dev", split_axis=0, concat_axis=0, tiled=True)
    chunk = back[:, 32:48, :].reshape(512, 128)
    parts = [chunk] + [
        lax.ppermute(chunk, "grp", [(i, (i - 2 * step) % 8) for i in range(8)])
        for step in (1, 2, 3)
    ]
    parts = parts + [lax.ppermute(x, "grp", swap) for x in parts]
    (grad_features,) = call(
        finish_kernel,
        [shape((2, 128, 512), BF)],
        [counts],
        [back, own0, own1, grad_out, jnp.asarray(GIVE, BF)],
        flops=3e8,
        name="finish",
    )
    grad_conv, grad_up, grad_down = call(
        assemble_kernel,
        [shape((27, 128, 128), F32), shape((128, 256), F32), shape((256, 128), F32)],
        [core, line],
        parts,
        name="assemble",
    )
    return (output, grad_features, grad_conv, grad_up, grad_down)


def solution(mesh):
    return jax.shard_map(
        on_device,
        mesh=mesh,
        in_specs=(
            P(("grp", "dev"), None, None),
            P(("grp", "dev"), None, None),
            P(),
            P(),
            P(),
            P(("grp", "dev")),
            P(("grp", "dev"), None),
            P(("grp", "dev"), None),
            P(("grp", "dev")),
            P(("grp", "dev")),
        ),
        out_specs=(P(("grp", "dev"), None, None), P(("grp", "dev"), None, None), P(), P(), P()),
        check_vma=False,
    )
```

```python
import functools

import jax
import jax.numpy as jnp
import numpy as np
from jax import lax
from jax.experimental import pallas as pl
from jax.experimental.pallas import tpu as pltpu
from jax.sharding import PartitionSpec as P

BF = jnp.bfloat16
F32 = jnp.float32

OFFSETS = [
    (a, b, c) for a in (-1, 0, 1) for b in (-1, 0, 1) for c in (-1, 0, 1) if (a, b, c) != (0, 0, 0)
]
FACES = [d for d in OFFSETS if sum(map(abs, d)) == 1]
EDGES = [d for d in OFFSETS if sum(map(abs, d)) == 2]
CORNERS = [d for d in OFFSETS if sum(map(abs, d)) == 3]
PIECE = {d: 64 * n for n, d in enumerate(FACES)}
PIECE.update({d: 384 + 8 * n for n, d in enumerate(EDGES)})
PIECE.update({d: 480 + n for n, d in enumerate(CORNERS)})


def voxel_runs(d):
    a, b, c = (7 if x < 0 else 0 for x in d)
    free = [x == 0 for x in d]
    if free == [True, True, False]:
        return [(0, c, 64, 8)]
    if free == [True, False, True]:
        return [(8 * x, x * 64 + b * 8, 8, 1) for x in range(8)]
    if free == [False, True, True]:
        return [(0, a * 64, 64, 1)]
    size = 8 if any(free) else 1
    stride = (64 if free[0] else 1) * (8 if free[1] else 1)
    return [(0, a * 64 + b * 8 + c, size, stride)]


def run(start, size, stride):
    return pl.ds(start, size) if stride == 1 else pl.ds(start, size, stride=stride)


SHARES = [((64 * f + p, 32, 2), (2 * f + p, 32, 16)) for f in range(6) for p in range(2)]
SHARES += [((384 + 32 * m, 32, 1), (12 + m, 32, 16)) for m in range(3)]
SHARES += [((480, 8, 1), (15 + 16 * n, 8, 64)) for n in range(4)]


def to_pieces(rows, pieces):
    for there, here in SHARES[:16]:
        pieces[run(*there), :] = rows[run(*here), :]


def to_shares(pieces, rows):
    for there, here in SHARES:
        rows[run(*here), :] = pieces[run(*there), :]


def nn(x, y):
    return lax.dot_general(x, y, (((1,), (0,)), ((), ())), preferred_element_type=F32)


def nt(x, y):
    return lax.dot_general(x, y, (((1,), (1,)), ((), ())), preferred_element_type=F32)


def identity():
    rows = lax.broadcasted_iota(jnp.int32, (128, 128), 0)
    lanes = lax.broadcasted_iota(jnp.int32, (128, 128), 1)
    return (rows == lanes).astype(F32).astype(BF)


def pool_rows(s):
    rows = lax.broadcasted_iota(jnp.int32, (16, 512), 0) - 8 * s
    lanes = lax.broadcasted_iota(jnp.int32, (16, 512), 1)
    block = ((lanes >> 8) & 1) * 4 + ((lanes >> 5) & 1) * 2 + ((lanes >> 2) & 1)
    return (rows == block).astype(F32).astype(BF)


def ask_kernel(
    counts, feat, owner, slot, msg, feat_v, owner_v, slot_v, bricks, voxels, pc, rows, sems
):
    pairs = ((owner, owner_v), (slot, slot_v), (feat, feat_v))
    copies = [
        pltpu.make_async_copy(src, dst, sems.at[n]) for n, (src, dst) in enumerate(pairs)
    ]
    for copy in copies:
        copy.start()
    bricks[...] = jnp.zeros((128, 128), F32)
    copies[0].wait()
    copies[1].wait()
    named = jnp.where(owner_v[...] >= 0, owner_v[...] * 2 + slot_v[...], -1)
    bricks[0:2, 0:26] = named.astype(F32)
    bricks[...] = bricks[...].T

    def ask(first, size, stride, direction):
        line = bricks[pl.ds(OFFSETS.index(direction), 1), :]
        rows[run(first, size, stride), :] = jnp.broadcast_to(line, (size, 128))

    for n, d in enumerate(FACES):
        ask(2 * n, 32, 16, d)
        ask(2 * n + 1, 32, 16, d)
    for n, d in enumerate(EDGES):
        ask(12 + n // 4 + 128 * (n % 4), 8, 16, d)
    for n, d in enumerate(CORNERS):
        ask(15 + 64 * n, 4, 16, d)
    msg[:, 32:48, :] = rows[...].astype(BF).reshape(32, 16, 128)
    copies[2].wait()
    for s in range(2):
        live = (counts[0] > s).astype(F32)
        voxels[...] = (feat_v[s].astype(F32) * live).T
        for d in OFFSETS:
            for at, first, size, stride in voxel_runs(d):
                pc[pl.ds(PIECE[d] + at, size), :] = voxels[run(first, size, stride), :]
        to_shares(pc, rows)
        msg[:, 16 * s : 16 * s + 16, :] = rows[...].astype(BF).reshape(32, 16, 128)


def same_part():
    rows = lax.broadcasted_iota(jnp.int32, (16, 128), 0)
    lanes = lax.broadcasted_iota(jnp.int32, (16, 128), 1) & 15
    return (rows == lanes).astype(F32).astype(BF)


def route_kernel(got, out, hot):
    same = jnp.broadcast_to(same_part()[None], (32, 16, 128))
    zero = jnp.zeros((32, 16, 128), BF)
    lanes = lax.broadcasted_iota(jnp.int32, (128, 128), 0)
    brick = lax.broadcasted_iota(jnp.int32, (16, 128), 1) >> 4
    table = got[:, 32:48, :].reshape(512, 128)
    data = got[:, 0:32, :].reshape(1024, 128)
    for s in range(2):
        spread = (lanes == s).astype(F32).astype(BF)
        asked = nn(table, spread).astype(BF).reshape(32, 16, 128)
        for n in range(8):
            here = (brick + 8 * n).astype(F32).astype(BF)
            hot[:, n * 128 : n * 128 + 128] = jnp.where(asked == here[None], same, zero).reshape(
                512, 128
            )
        picked = nn(hot[...], data).astype(BF)
        out[:, 16 * s : 16 * s + 16, :] = picked.reshape(32, 16, 128)


def forward_kernel(
    counts, parent, child, core, feat, got, gout, weight, up, down,
    out, grad, keep, send,
    rows, pc, mine, s0, s1, s2, cols, grad_t, acts, slopes, pooled, grad_pooled,
):
    eye = identity()
    pooled[...] = jnp.zeros((16, 128), F32)
    grad_pooled[...] = jnp.zeros((16, 128), F32)

    def brick(s, _):
        live = (counts[0] > s).astype(F32)
        pool = pool_rows(s)
        mine[...] = (feat[s].astype(F32) * live).T
        grad_pooled[...] += nt(pool, gout[s]) * live
        share = got[:, pl.ds(pl.multiple_of(s * 16, 16), 16), :]
        rows[...] = share.reshape(512, 128).astype(F32)
        to_pieces(rows, pc)
        for a in range(8):
            s1[pl.ds(8 + ((a + 1) * 10 + 1) * 8, 64), :] = mine[a * 64 : a * 64 + 64, :]
            for d, b in (((0, -1, 0), 0), ((0, 1, 0), 9)):
                s1[pl.ds(8 + ((a + 1) * 10 + b) * 8, 8), :] = pc[pl.ds(PIECE[d] + 8 * a, 8), :]
        for a, x in ((-1, 0), (1, 9)):
            s1[pl.ds(8 + (x * 10 + 1) * 8, 64), :] = pc[pl.ds(PIECE[a, 0, 0], 64), :]
            for b, y in ((-1, 0), (1, 9)):
                s1[pl.ds(8 + (x * 10 + y) * 8, 8), :] = pc[pl.ds(PIECE[a, b, 0], 8), :]
        s0[...] = s1[pl.ds(7, 800), :]
        s2[...] = s1[pl.ds(9, 800), :]
        for c, ref, lane in ((-1, s0, 0), (1, s2, 7)):
            for a in range(8):
                ref[pl.ds(((a + 1) * 10 + 1) * 8 + lane, 8, stride=8), :] = pc[
                    pl.ds(PIECE[0, 0, c] + 8 * a, 8), :
                ]
            for a, x in ((-1, 0), (1, 9)):
                ref[pl.ds((x * 10 + 1) * 8 + lane, 8, stride=8), :] = pc[
                    pl.ds(PIECE[a, 0, c], 8), :
                ]
                ref[pl.ds((10 + x) * 8 + lane, 8, stride=80), :] = pc[pl.ds(PIECE[0, a, c], 8), :]
                for b, y in ((-1, 0), (1, 9)):
                    ref[pl.ds((x * 10 + y) * 8 + lane, 1), :] = pc[pl.ds(PIECE[a, b, c], 1), :]

        def plane(a, _):
            for b in range(3):
                for c, ref in enumerate((s0, s1, s2)):
                    start = pl.multiple_of((a * 10 + b) * 8 + (8 if c == 1 else 0), 8)
                    cols[s, pl.ds(pl.multiple_of(a * 64, 64), 64), pl.ds((3 * b + c) * 128, 128)] = ref[
                        pl.ds(start, 64), :
                    ].astype(BF)
            return 0

        lax.fori_loop(0, 10, plane, 0)
        pre = nn(cols[s, 0:512, :], weight[0])
        pre = pre + nn(cols[s, 64:576, :], weight[1])
        pre = pre + nn(cols[s, 128:640, :], weight[2])
        pre = pre.T
        gate = 1.0 / (1.0 + jnp.exp(-pre))
        active = pre * gate
        acts[s] = active
        slopes[s] = gate * (1.0 + pre * (1.0 - gate))
        high = active.astype(BF)
        low = (active - high.astype(F32)).astype(BF)
        pooled[...] += nt(pool, high) + nt(pool, low)
        return 0

    lax.fori_loop(0, 2, brick, 0)
    second = lax.broadcasted_iota(jnp.int32, (16, 1), 0) >= 8
    valid = [
        (
            (counts[0] > s) & (parent[s] >= 0) & (parent[s] * 64 + child[s] >= 0)
        ).astype(F32)
        for s in range(2)
    ]
    valid = jnp.where(second, valid[1], valid[0])
    coarse_in = (pooled[...] * (1.0 / 64.0) * valid).astype(BF)
    grad_out = (grad_pooled[...] * valid).astype(BF)
    coarse_pre = nn(coarse_in, up[...])
    gate = 1.0 / (1.0 + jnp.exp(-coarse_pre))
    coarse_mid = (coarse_pre * gate).astype(BF)
    grad_pre = nt(grad_out, down[...]) * (gate * (1.0 + coarse_pre * (1.0 - gate)))
    grad_pre = grad_pre.astype(BF)
    coarse_out = nn(coarse_mid, down[...]).astype(BF)
    grad_cin = nt(grad_pre, up[...]).astype(BF)
    lift = nt(eye, coarse_out).astype(BF)
    back = nt(eye, grad_cin).astype(BF)

    def blend(s, _):
        live = (counts[0] > s).astype(F32)
        pool = pool_rows(s)
        out[s] = (feat[s].astype(F32) * live + acts[s] + nn(lift, pool)).astype(BF)
        grad_in = gout[s].astype(F32) * live + nn(back, pool) * (1.0 / 64.0)
        grad_pre_conv = grad_in * slopes[s]
        grad_t[s] = grad_pre_conv.astype(BF)
        grad[s] = grad_pre_conv.T.astype(BF)
        return 0

    lax.fori_loop(0, 2, blend, 0)

    def put(block, value):
        half, at = divmod(block, 16)
        value = value.astype(BF)

        @pl.when(core[0] == half)
        def _():
            keep[pl.ds(at * 128, 128), :] = value

        @pl.when(core[0] != half)
        def _():
            send[pl.ds(at * 128, 128), :] = value

    grad_up = nn(nt(eye, coarse_in).astype(BF), grad_pre)
    for h in range(2):
        put(27 + h, grad_up[:, h * 128 : h * 128 + 128])
        middle = nt(eye, coarse_mid[:, h * 128 : h * 128 + 128]).astype(BF)
        put(29 + h, nn(middle, grad_out))
    put(31, jnp.zeros((128, 128), F32))
    for a in range(3):
        total = nn(grad_t[0], cols[0, a * 64 : a * 64 + 512, :])
        total = total + nn(grad_t[1], cols[1, a * 64 : a * 64 + 512, :])
        total = total.astype(BF)
        for n in range(9):
            put(9 * a + n, nt(eye, total[:, n * 128 : n * 128 + 128]))


def pair_kernel(line, keep, other, own, one, two, three):
    for step, ref in enumerate((own, one, two, three)):
        at = pl.ds(pl.multiple_of(((line[0] + step) & 3) * 512, 512), 512)
        ref[...] = (keep[at, :].astype(F32) + other[at, :].astype(F32)).astype(ref.dtype)


def backward_kernel(grad, weight, own, msg, planes, acc, pc, rows):
    planes[0:128, :] = jnp.zeros((128, 128), BF)
    planes[640:768, :] = jnp.zeros((128, 128), BF)
    low = (lax.broadcasted_iota(jnp.int32, (64, 1), 0) & 7) != 0
    high = (lax.broadcasted_iota(jnp.int32, (64, 1), 0) & 7) != 7

    def brick(s, _):
        planes[128:640, :] = grad[s]
        acc[...] = jnp.zeros_like(acc)

        def tap(n, _):
            c = lax.rem(n, 3)
            b = lax.div(n, 3)
            part = nt(planes[128:768, :], weight[n])
            part = part + nt(planes[64:704, :], weight[n + 9])
            part = part + nt(planes[0:640, :], weight[n + 18])
            for a in range(10):
                at = pl.ds(pl.multiple_of(8 + (a * 10 + b) * 8, 8), 64)
                acc[c, at, :] = acc[c, at, :] + part[a * 64 : a * 64 + 64]
            return 0

        lax.fori_loop(0, 9, tap, 0)

        def middle(row, size):
            at = 8 + row
            total = acc[1, pl.ds(at, size), :]
            total = total + jnp.where(high[:size], acc[0, pl.ds(at + 1, size), :], 0.0)
            return total + jnp.where(low[:size], acc[2, pl.ds(at - 1, size), :], 0.0)

        for a in range(8):
            own[s, pl.ds(a * 64, 64), :] = middle(((a + 1) * 10 + 1) * 8, 64)
            for d, b in (((0, -1, 0), 0), ((0, 1, 0), 9)):
                pc[pl.ds(PIECE[d] + 8 * a, 8), :] = middle(((a + 1) * 10 + b) * 8, 8)
        for a, x in ((-1, 0), (1, 9)):
            pc[pl.ds(PIECE[a, 0, 0], 64), :] = middle((x * 10 + 1) * 8, 64)
            for b, y in ((-1, 0), (1, 9)):
                pc[pl.ds(PIECE[a, b, 0], 8), :] = middle((x * 10 + y) * 8, 8)
        for c, ref, lane in ((-1, acc.at[0], 8), (1, acc.at[2], 15)):
            for a in range(8):
                pc[pl.ds(PIECE[0, 0, c] + 8 * a, 8), :] = ref[
                    pl.ds(((a + 1) * 10 + 1) * 8 + lane, 8, stride=8), :
                ]
            for a, x in ((-1, 0), (1, 9)):
                pc[pl.ds(PIECE[a, 0, c], 8), :] = ref[pl.ds((x * 10 + 1) * 8 + lane, 8, stride=8), :]
                pc[pl.ds(PIECE[0, a, c], 8), :] = ref[pl.ds((10 + x) * 8 + lane, 8, stride=80), :]
                for b, y in ((-1, 0), (1, 9)):
                    pc[pl.ds(PIECE[a, b, c], 1), :] = ref[pl.ds((x * 10 + y) * 8 + lane, 1), :]
        to_shares(pc, rows)
        at = pl.ds(pl.multiple_of(s * 16, 16), 16)
        msg[:, at, :] = rows[...].astype(BF).reshape(32, 16, 128)
        return 0

    lax.fori_loop(0, 2, brick, 0)


def join_kernel(terms, own, away1, away2, away3, msg):
    msg[:, 0:32, :] = terms[...]
    total = own[...] + away1[...].astype(F32) + away2[...].astype(F32) + away3[...].astype(F32)
    msg[:, 32:48, :] = total.astype(BF).reshape(32, 16, 128)


def merge_kernel(got, table, out, hot):
    same = same_part()
    zero = jnp.zeros((16, 128), BF)
    share = jnp.sum(got[:, 32:48, :].astype(F32), axis=0).astype(BF)
    out[:, 32:48, :] = jnp.broadcast_to(share[None], (32, 16, 128))
    for n in range(8):
        asked = table[:, n * 128 : n * 128 + 128]
        for brick in range(64):
            hot[brick * 16 : brick * 16 + 16, n * 128 : n * 128 + 128] = jnp.where(
                asked == jnp.full((16, 128), brick, BF), same, zero
            )
    total = nn(hot[...], got[:, 0:32, :].reshape(1024, 128))
    out[:, 0:32, :] = total.astype(BF).reshape(32, 32, 128)


def finish_kernel(counts, got, own, gout, out, rows, pc, total):
    for s in range(2):
        live = (counts[0] > s).astype(F32)
        rows[...] = got[:, 16 * s : 16 * s + 16, :].reshape(512, 128).astype(F32)
        to_pieces(rows, pc)
        total[...] = own[s]
        for d in OFFSETS:
            for at, first, size, stride in voxel_runs(d):
                where = run(first, size, stride)
                total[where, :] = total[where, :] + pc[pl.ds(PIECE[d] + at, size), :]
        out[s] = (total[...].T + gout[s].astype(F32) * live).astype(BF)


def assemble_kernel(core, line, *refs):
    parts, (conv, up, down) = refs[:8], refs[8:]
    for n, part in enumerate(parts):
        half = core[0] ^ (n // 4)
        first = half * 16 + ((line[0] + n % 4) & 3) * 4

        def block(at):
            return part[at * 128 : at * 128 + 128, :].astype(F32)

        @pl.when(first < 24)
        def _():
            for at in range(4):
                conv[first + at] = block(at)

        @pl.when(first == 24)
        def _():
            for at in range(3):
                conv[24 + at] = block(at)
            up[:, 0:128] = block(3)

        @pl.when(first == 28)
        def _():
            up[:, 128:256] = block(0)
            down[0:128, :] = block(1)
            down[128:256, :] = block(2)


VM = pl.BlockSpec(memory_space=pltpu.VMEM)
SM = pl.BlockSpec(memory_space=pltpu.SMEM)


def call(kernel, shapes, scalars, arrays, scratch=(), flops=1e6, space=VM, limit=20, name=None):
    moved = sum(x.size * x.dtype.itemsize for x in arrays)
    moved += sum(int(np.prod(s.shape)) * s.dtype.itemsize for s in shapes)
    return pl.pallas_call(
        kernel,
        out_shape=shapes,
        in_specs=[SM] * len(scalars) + [space] * len(arrays),
        out_specs=[VM] * len(shapes),
        scratch_shapes=list(scratch),
        compiler_params=pltpu.CompilerParams(vmem_limit_bytes=limit * 2**20),
        cost_estimate=pl.CostEstimate(
            flops=int(flops), bytes_accessed=int(moved), transcendentals=0
        ),
        name=name,
    )(*scalars, *arrays)


def shape(dims, dtype):
    return jax.ShapeDtypeStruct(dims, dtype)


def on_device(
    features,
    grad_out,
    conv_weight,
    coarse_up,
    coarse_down,
    counts,
    neighbour_owner,
    neighbour_slot,
    parent,
    child_slot,
):
    grp = lax.axis_index("grp").astype(jnp.int32)
    core = (grp & 1).reshape(1)
    line = (grp >> 1).reshape(1)
    swap = [(i, i ^ 1) for i in range(8)]
    (msg,) = call(
        ask_kernel,
        [shape((32, 48, 128), BF)],
        [counts],
        [features, neighbour_owner, neighbour_slot],
        [
            pltpu.VMEM((2, 128, 512), BF),
            pltpu.VMEM((2, 26), jnp.int32),
            pltpu.VMEM((2, 26), jnp.int32),
            pltpu.VMEM((128, 128), F32),
            pltpu.VMEM((512, 128), F32),
            pltpu.VMEM((512, 128), F32),
            pltpu.VMEM((512, 128), F32),
            pltpu.SemaphoreType.DMA((3,)),
        ],
        flops=2e6,
        space=pl.BlockSpec(memory_space=pltpu.HBM),
        limit=60,
        name="ask",
    )
    first = lax.all_to_all(msg, "dev", split_axis=0, concat_axis=0, tiled=True)
    (answer,) = call(
        route_kernel,
        [shape((32, 32, 128), BF)],
        [],
        [first],
        [pltpu.VMEM((512, 1024), BF)],
        flops=3e8,
        name="route",
    )
    halo = lax.all_to_all(answer, "dev", split_axis=0, concat_axis=0, tiled=True)
    table = first[:, 32:48, 0:2].transpose(0, 2, 1).reshape(1, 1024)
    table = jnp.broadcast_to(table, (16, 1024))
    output, grad_pre, keep, send = call(
        forward_kernel,
        [
            shape((2, 128, 512), BF),
            shape((2, 512, 128), BF),
            shape((2048, 128), BF),
            shape((2048, 128), BF),
        ],
        [counts, parent, child_slot, core],
        [
            features,
            halo,
            grad_out,
            conv_weight.reshape(3, 1152, 128),
            coarse_up,
            coarse_down,
        ],
        [
            pltpu.VMEM((512, 128), F32),
            pltpu.VMEM((512, 128), F32),
            pltpu.VMEM((512, 128), F32),
            pltpu.VMEM((800, 128), F32),
            pltpu.VMEM((816, 128), F32),
            pltpu.VMEM((800, 128), F32),
            pltpu.VMEM((2, 640, 1152), BF),
            pltpu.VMEM((2, 128, 512), BF),
            pltpu.VMEM((2, 128, 512), F32),
            pltpu.VMEM((2, 128, 512), F32),
            pltpu.VMEM((16, 128), F32),
            pltpu.VMEM((16, 128), F32),
        ],
        flops=2e9,
        name="forward",
    )

    other = lax.ppermute(send, "grp", swap)
    own_sum, *away = call(
        pair_kernel,
        [shape((512, 128), F32)] + [shape((512, 128), BF)] * 3,
        [line],
        [keep, other],
        name="pair",
    )
    away = [
        lax.ppermute(x, "grp", [(i, (i + 2 * step) % 8) for i in range(8)])
        for step, x in zip((1, 2, 3), away)
    ]
    grad_pre, own_sum = lax.optimization_barrier((grad_pre, own_sum))
    own, terms = call(
        backward_kernel,
        [shape((2, 512, 128), F32), shape((32, 32, 128), BF)],
        [],
        [grad_pre, conv_weight],
        [
            pltpu.VMEM((768, 128), BF),
            pltpu.VMEM((3, 816, 128), F32),
            pltpu.VMEM((512, 128), F32),
            pltpu.VMEM((512, 128), F32),
        ],
        flops=4e9,
        name="backward",
    )
    (terms,) = call(
        join_kernel, [shape((32, 48, 128), BF)], [], [terms, own_sum, *away], name="join"
    )
    terms = lax.all_to_all(terms, "dev", split_axis=0, concat_axis=0, tiled=True)
    (sums,) = call(
        merge_kernel,
        [shape((32, 48, 128), BF)],
        [],
        [terms, table],
        [pltpu.VMEM((1024, 1024), BF)],
        flops=3e8,
        name="merge",
    )
    back = lax.all_to_all(sums, "dev", split_axis=0, concat_axis=0, tiled=True)
    chunk = back[:, 32:48, :].reshape(512, 128)
    parts = [chunk] + [
        lax.ppermute(chunk, "grp", [(i, (i - 2 * step) % 8) for i in range(8)])
        for step in (1, 2, 3)
    ]
    (grad_features,) = call(
        finish_kernel,
        [shape((2, 128, 512), BF)],
        [counts],
        [back, own, grad_out],
        [pltpu.VMEM((512, 128), F32)] * 3,
        flops=3e8,
        name="finish",
    )
    chunk = lax.ppermute(chunk, "grp", swap)
    parts, grad_features = lax.optimization_barrier((parts, grad_features))
    parts = parts + [chunk] + [lax.ppermute(x, "grp", swap) for x in parts[1:]]
    grad_conv, grad_up, grad_down = call(
        assemble_kernel,
        [shape((27, 128, 128), F32), shape((128, 256), F32), shape((256, 128), F32)],
        [core, line],
        parts,
        name="assemble",
    )
    return (output, grad_features, grad_conv, grad_up, grad_down)


def solution(mesh):
    return jax.shard_map(
        on_device,
        mesh=mesh,
        in_specs=(
            P(("grp", "dev"), None, None),
            P(("grp", "dev"), None, None),
            P(),
            P(),
            P(),
            P(("grp", "dev")),
            P(("grp", "dev"), None),
            P(("grp", "dev"), None),
            P(("grp", "dev")),
            P(("grp", "dev")),
        ),
        out_specs=(P(("grp", "dev"), None, None), P(("grp", "dev"), None, None), P(), P(), P()),
        check_vma=False,
    )
```

```python
import functools

import jax
import jax.numpy as jnp
import numpy as np
from jax import lax
from jax.experimental import pallas as pl
from jax.experimental.pallas import tpu as pltpu
from jax.sharding import PartitionSpec as P

BF = jnp.bfloat16
F32 = jnp.float32

OFFSETS = [
    (a, b, c) for a in (-1, 0, 1) for b in (-1, 0, 1) for c in (-1, 0, 1) if (a, b, c) != (0, 0, 0)
]
FACES = [d for d in OFFSETS if sum(map(abs, d)) == 1]
EDGES = [d for d in OFFSETS if sum(map(abs, d)) == 2]
CORNERS = [d for d in OFFSETS if sum(map(abs, d)) == 3]
PIECE = {d: 64 * n for n, d in enumerate(FACES)}
PIECE.update({d: 384 + 8 * n for n, d in enumerate(EDGES)})
PIECE.update({d: 480 + n for n, d in enumerate(CORNERS)})


def voxel_runs(d):
    a, b, c = (7 if x < 0 else 0 for x in d)
    free = [x == 0 for x in d]
    if free == [True, True, False]:
        return [(0, c, 64, 8)]
    if free == [True, False, True]:
        return [(8 * x, x * 64 + b * 8, 8, 1) for x in range(8)]
    if free == [False, True, True]:
        return [(0, a * 64, 64, 1)]
    size = 8 if any(free) else 1
    stride = (64 if free[0] else 1) * (8 if free[1] else 1)
    return [(0, a * 64 + b * 8 + c, size, stride)]


def run(start, size, stride):
    return pl.ds(start, size) if stride == 1 else pl.ds(start, size, stride=stride)


SHARES = [((64 * f + p, 32, 2), (2 * f + p, 32, 16)) for f in range(6) for p in range(2)]
SHARES += [((384 + 32 * m, 32, 1), (12 + m, 32, 16)) for m in range(3)]
SHARES += [((480, 8, 1), (15 + 16 * n, 8, 64)) for n in range(4)]


def to_pieces(rows, pieces):
    for there, here in SHARES[:16]:
        pieces[run(*there), :] = rows[run(*here), :]


def to_shares(pieces, rows):
    for there, here in SHARES:
        rows[run(*here), :] = pieces[run(*there), :]


def nn(x, y):
    return lax.dot_general(x, y, (((1,), (0,)), ((), ())), preferred_element_type=F32)


def nt(x, y):
    return lax.dot_general(x, y, (((1,), (1,)), ((), ())), preferred_element_type=F32)


def identity():
    rows = lax.broadcasted_iota(jnp.int32, (128, 128), 0)
    lanes = lax.broadcasted_iota(jnp.int32, (128, 128), 1)
    return (rows == lanes).astype(F32).astype(BF)


def pool_rows(s):
    rows = lax.broadcasted_iota(jnp.int32, (16, 512), 0) - 8 * s
    lanes = lax.broadcasted_iota(jnp.int32, (16, 512), 1)
    block = ((lanes >> 8) & 1) * 4 + ((lanes >> 5) & 1) * 2 + ((lanes >> 2) & 1)
    return (rows == block).astype(F32).astype(BF)


def ask_kernel(
    counts, feat, owner, slot, msg, feat_v, owner_v, slot_v, bricks, voxels, pc, rows, sems
):
    pairs = ((owner, owner_v), (slot, slot_v), (feat, feat_v))
    copies = [
        pltpu.make_async_copy(src, dst, sems.at[n]) for n, (src, dst) in enumerate(pairs)
    ]
    for copy in copies:
        copy.start()
    bricks[...] = jnp.zeros((128, 128), F32)
    copies[0].wait()
    copies[1].wait()
    named = jnp.where(owner_v[...] >= 0, owner_v[...] * 2 + slot_v[...], -1)
    bricks[0:2, 0:26] = named.astype(F32)
    bricks[...] = bricks[...].T

    def ask(first, size, stride, direction):
        line = bricks[pl.ds(OFFSETS.index(direction), 1), :]
        rows[run(first, size, stride), :] = jnp.broadcast_to(line, (size, 128))

    for n, d in enumerate(FACES):
        ask(2 * n, 32, 16, d)
        ask(2 * n + 1, 32, 16, d)
    for n, d in enumerate(EDGES):
        ask(12 + n // 4 + 128 * (n % 4), 8, 16, d)
    for n, d in enumerate(CORNERS):
        ask(15 + 64 * n, 4, 16, d)
    msg[:, 32:48, :] = rows[...].astype(BF).reshape(32, 16, 128)
    copies[2].wait()
    for s in range(2):
        live = (counts[0] > s).astype(F32)
        voxels[...] = (feat_v[s].astype(F32) * live).T
        for d in OFFSETS:
            for at, first, size, stride in voxel_runs(d):
                pc[pl.ds(PIECE[d] + at, size), :] = voxels[run(first, size, stride), :]
        to_shares(pc, rows)
        msg[:, 16 * s : 16 * s + 16, :] = rows[...].astype(BF).reshape(32, 16, 128)


def same_part():
    rows = lax.broadcasted_iota(jnp.int32, (16, 128), 0)
    lanes = lax.broadcasted_iota(jnp.int32, (16, 128), 1) & 15
    return (rows == lanes).astype(F32).astype(BF)


def route_kernel(got, out, hot):
    same = jnp.broadcast_to(same_part()[None], (32, 16, 128))
    zero = jnp.zeros((32, 16, 128), BF)
    lanes = lax.broadcasted_iota(jnp.int32, (128, 128), 0)
    brick = lax.broadcasted_iota(jnp.int32, (16, 128), 1) >> 4
    table = got[:, 32:48, :].reshape(512, 128)
    for s in range(2):
        spread = (lanes == s).astype(F32).astype(BF)
        asked = nn(table, spread).astype(BF).reshape(32, 16, 128)
        for n in range(8):
            here = (brick + 8 * n).astype(F32).astype(BF)
            picked = jnp.where(asked == here[None], same, zero)
            hot[s * 512 : s * 512 + 512, n * 128 : n * 128 + 128] = picked.reshape(512, 128)
    answer = nn(hot[...], got[:, 0:32, :].reshape(1024, 128)).astype(BF)
    for s in range(2):
        out[:, 16 * s : 16 * s + 16, :] = answer[s * 512 : s * 512 + 512].reshape(32, 16, 128)


def forward_kernel(
    counts, parent, child, core, feat, got, gout, weight, up, down,
    out, grad, wsum, send,
    rows_all, pc_all, mine_all, s0_all, s1_all, s2_all, cols, grad_t, pooled, grad_pooled,
    out_v, sem,
):
    eye = identity()
    acts, slopes = [], []
    for s in range(2):
        rows, pc, mine, s0, s1, s2 = (
            x.at[s] for x in (rows_all, pc_all, mine_all, s0_all, s1_all, s2_all)
        )
        live = (counts[0] > s).astype(F32)
        pool = pool_rows(s)
        mine[...] = (feat[s].astype(F32) * live).T
        grad_pooled[s] = nt(pool, gout[s]) * live
        rows[...] = got[:, 16 * s : 16 * s + 16, :].reshape(512, 128).astype(F32)
        to_pieces(rows, pc)
        for a in range(8):
            s1[pl.ds(8 + ((a + 1) * 10 + 1) * 8, 64), :] = mine[a * 64 : a * 64 + 64, :]
            for d, b in (((0, -1, 0), 0), ((0, 1, 0), 9)):
                s1[pl.ds(8 + ((a + 1) * 10 + b) * 8, 8), :] = pc[pl.ds(PIECE[d] + 8 * a, 8), :]
        for a, x in ((-1, 0), (1, 9)):
            s1[pl.ds(8 + (x * 10 + 1) * 8, 64), :] = pc[pl.ds(PIECE[a, 0, 0], 64), :]
            for b, y in ((-1, 0), (1, 9)):
                s1[pl.ds(8 + (x * 10 + y) * 8, 8), :] = pc[pl.ds(PIECE[a, b, 0], 8), :]
        s0[...] = s1[pl.ds(7, 800), :]
        s2[...] = s1[pl.ds(9, 800), :]
        for c, ref, lane in ((-1, s0, 0), (1, s2, 7)):
            for a in range(8):
                ref[pl.ds(((a + 1) * 10 + 1) * 8 + lane, 8, stride=8), :] = pc[
                    pl.ds(PIECE[0, 0, c] + 8 * a, 8), :
                ]
            for a, x in ((-1, 0), (1, 9)):
                ref[pl.ds((x * 10 + 1) * 8 + lane, 8, stride=8), :] = pc[
                    pl.ds(PIECE[a, 0, c], 8), :
                ]
                ref[pl.ds((10 + x) * 8 + lane, 8, stride=80), :] = pc[pl.ds(PIECE[0, a, c], 8), :]
                for b, y in ((-1, 0), (1, 9)):
                    ref[pl.ds((x * 10 + y) * 8 + lane, 1), :] = pc[pl.ds(PIECE[a, b, c], 1), :]
        for a in range(10):
            for b in range(3):
                for c, ref in enumerate((s0, s1, s2)):
                    start = (a * 10 + b) * 8 + (8 if c == 1 else 0)
                    at = 640 * s + 64 * a
                    cols[at : at + 64, (3 * b + c) * 128 : (3 * b + c) * 128 + 128] = ref[
                        pl.ds(start, 64), :
                    ].astype(BF)
        taps = nn(cols[640 * s : 640 * s + 640, :], weight[...])
        pre = taps[0:512, 0:128] + taps[64:576, 128:256] + taps[128:640, 256:384]
        pre = pre.T
        gate = 1.0 / (1.0 + jnp.exp(-pre))
        active = pre * gate
        acts.append(active)
        slopes.append(gate * (1.0 + pre * (1.0 - gate)))
        high = active.astype(BF)
        low = (active - high.astype(F32)).astype(BF)
        pooled[s] = nt(pool, high) + nt(pool, low)
    second = lax.broadcasted_iota(jnp.int32, (16, 1), 0) >= 8
    valid = [
        (
            (counts[0] > s) & (parent[s] >= 0) & (parent[s] * 64 + child[s] >= 0)
        ).astype(F32)
        for s in range(2)
    ]
    valid = jnp.where(second, valid[1], valid[0])
    coarse_in = ((pooled[0] + pooled[1]) * (1.0 / 64.0) * valid).astype(BF)
    grad_out = ((grad_pooled[0] + grad_pooled[1]) * valid).astype(BF)
    coarse_pre = nn(coarse_in, up[...])
    gate = 1.0 / (1.0 + jnp.exp(-coarse_pre))
    coarse_mid = (coarse_pre * gate).astype(BF)
    grad_pre = nt(grad_out, down[...]) * (gate * (1.0 + coarse_pre * (1.0 - gate)))
    grad_pre = grad_pre.astype(BF)
    coarse_out = nn(coarse_mid, down[...]).astype(BF)
    grad_cin = nt(grad_pre, up[...]).astype(BF)
    lift = nt(eye, coarse_out).astype(BF)
    back = nt(eye, grad_cin).astype(BF)
    for s in range(2):
        live = (counts[0] > s).astype(F32)
        pool = pool_rows(s)
        out_v[s] = (feat[s].astype(F32) * live + acts[s] + nn(lift, pool)).astype(BF)
        grad_in = gout[s].astype(F32) * live + nn(back, pool) * (1.0 / 64.0)
        grad_pre_conv = grad_in * slopes[s]
        grad_t[s] = grad_pre_conv.astype(BF)
        grad[s] = grad_pre_conv.T.astype(BF)
    copy = pltpu.make_async_copy(out_v, out, sem.at[0])
    copy.start()

    def put(block, value):
        wsum[pl.ds(block * 128, 128), :] = value.astype(BF)

    grad_up = nn(nt(eye, coarse_in).astype(BF), grad_pre)
    for h in range(2):
        put(27 + h, grad_up[:, h * 128 : h * 128 + 128])
        middle = nt(eye, coarse_mid[:, h * 128 : h * 128 + 128]).astype(BF)
        put(29 + h, nn(middle, grad_out))
    put(31, jnp.zeros((128, 128), F32))
    for a in range(3):
        total = nn(grad_t[0], cols[64 * a : 64 * a + 512, :])
        total = total + nn(grad_t[1], cols[64 * a + 640 : 64 * a + 1152, :])
        total = total.astype(BF)
        for n in range(9):
            put(9 * a + n, nt(eye, total[:, n * 128 : n * 128 + 128]))
    send[...] = wsum[pl.ds(pl.multiple_of((1 - core[0]) * 2048, 2048), 2048), :]
    copy.wait()


def pair_kernel(core, line, wsum, other, own, one, two, three):
    for step, ref in enumerate((own, one, two, three)):
        at = pl.multiple_of(((line[0] + step) & 3) * 512, 512)
        kept = wsum[pl.ds(pl.multiple_of(core[0] * 2048 + at, 512), 512), :].astype(F32)
        ref[...] = (kept + other[pl.ds(at, 512), :].astype(F32)).astype(ref.dtype)


def backward_kernel(grad, weight, own, msg, lhs, acc_all, pc_all, rows_all):
    zero = jnp.zeros((64, 128), BF)
    for a in range(3):
        for n in [*range(a), *range(8 + a, 10)]:
            for s in range(2):
                lhs[s, n * 64 : n * 64 + 64, a * 128 : a * 128 + 128] = zero
    low = (lax.broadcasted_iota(jnp.int32, (64, 1), 0) & 7) != 0
    high = (lax.broadcasted_iota(jnp.int32, (64, 1), 0) & 7) != 7

    for s in range(2):
        acc, pc, rows = acc_all.at[s], pc_all.at[s], rows_all.at[s]
        for a in range(3):
            lhs[s, a * 64 : a * 64 + 512, a * 128 : a * 128 + 128] = grad[s]
        acc[...] = jnp.zeros_like(acc)
        for b in range(3):
            part = nt(lhs[s], weight[b * 384 : b * 384 + 384, :])
            for c in range(3):
                for a in range(10):
                    at = pl.ds(8 + (a * 10 + b) * 8, 64)
                    acc[c, at, :] += part[a * 64 : a * 64 + 64, c * 128 : c * 128 + 128]

        def middle(row, size):
            at = 8 + row
            total = acc[1, pl.ds(at, size), :]
            total = total + jnp.where(high[:size], acc[0, pl.ds(at + 1, size), :], 0.0)
            return total + jnp.where(low[:size], acc[2, pl.ds(at - 1, size), :], 0.0)

        for a in range(8):
            own[s, pl.ds(a * 64, 64), :] = middle(((a + 1) * 10 + 1) * 8, 64)
            for d, b in (((0, -1, 0), 0), ((0, 1, 0), 9)):
                pc[pl.ds(PIECE[d] + 8 * a, 8), :] = middle(((a + 1) * 10 + b) * 8, 8)
        for a, x in ((-1, 0), (1, 9)):
            pc[pl.ds(PIECE[a, 0, 0], 64), :] = middle((x * 10 + 1) * 8, 64)
            for b, y in ((-1, 0), (1, 9)):
                pc[pl.ds(PIECE[a, b, 0], 8), :] = middle((x * 10 + y) * 8, 8)
        for c, ref, lane in ((-1, acc.at[0], 8), (1, acc.at[2], 15)):
            for a in range(8):
                pc[pl.ds(PIECE[0, 0, c] + 8 * a, 8), :] = ref[
                    pl.ds(((a + 1) * 10 + 1) * 8 + lane, 8, stride=8), :
                ]
            for a, x in ((-1, 0), (1, 9)):
                pc[pl.ds(PIECE[a, 0, c], 8), :] = ref[pl.ds((x * 10 + 1) * 8 + lane, 8, stride=8), :]
                pc[pl.ds(PIECE[0, a, c], 8), :] = ref[pl.ds((10 + x) * 8 + lane, 8, stride=80), :]
                for b, y in ((-1, 0), (1, 9)):
                    pc[pl.ds(PIECE[a, b, c], 1), :] = ref[pl.ds((x * 10 + y) * 8 + lane, 1), :]
        to_shares(pc, rows)
        msg[:, 16 * s : 16 * s + 16, :] = rows[...].astype(BF).reshape(32, 16, 128)


def join_kernel(terms, own, away1, away2, away3, msg):
    msg[:, 0:32, :] = terms[...]
    total = own[...] + away1[...].astype(F32) + away2[...].astype(F32) + away3[...].astype(F32)
    msg[:, 32:48, :] = total.astype(BF).reshape(32, 16, 128)


def merge_kernel(got, table, out, hot):
    same = same_part()
    zero = jnp.zeros((16, 128), BF)
    share = jnp.sum(got[:, 32:48, :].astype(F32), axis=0).astype(BF)
    out[:, 32:48, :] = jnp.broadcast_to(share[None], (32, 16, 128))
    for n in range(8):
        asked = table[:, n * 128 : n * 128 + 128]
        for brick in range(64):
            hot[brick * 16 : brick * 16 + 16, n * 128 : n * 128 + 128] = jnp.where(
                asked == jnp.full((16, 128), brick, BF), same, zero
            )
    total = nn(hot[...], got[:, 0:32, :].reshape(1024, 128))
    out[:, 0:32, :] = total.astype(BF).reshape(32, 32, 128)


def finish_kernel(counts, got, own, gout, out, rows, pc, total):
    for s in range(2):
        live = (counts[0] > s).astype(F32)
        rows[...] = got[:, 16 * s : 16 * s + 16, :].reshape(512, 128).astype(F32)
        to_pieces(rows, pc)
        total[...] = own[s]
        for d in OFFSETS:
            for at, first, size, stride in voxel_runs(d):
                where = run(first, size, stride)
                total[where, :] = total[where, :] + pc[pl.ds(PIECE[d] + at, size), :]
        out[s] = (total[...].T + gout[s].astype(F32) * live).astype(BF)


def assemble_kernel(core, line, *refs):
    parts, (conv, up, down) = refs[:8], refs[8:]
    for n, part in enumerate(parts):
        half = core[0] ^ (n // 4)
        first = half * 16 + ((line[0] + n % 4) & 3) * 4

        def block(at):
            return part[at * 128 : at * 128 + 128, :].astype(F32)

        @pl.when(first < 24)
        def _():
            for at in range(4):
                conv[first + at] = block(at)

        @pl.when(first == 24)
        def _():
            for at in range(3):
                conv[24 + at] = block(at)
            up[:, 0:128] = block(3)

        @pl.when(first == 28)
        def _():
            up[:, 128:256] = block(0)
            down[0:128, :] = block(1)
            down[128:256, :] = block(2)


VM = pl.BlockSpec(memory_space=pltpu.VMEM)
SM = pl.BlockSpec(memory_space=pltpu.SMEM)


def call(kernel, shapes, scalars, arrays, scratch=(), flops=1e6, space=VM, limit=24, first=VM, name=None):
    moved = sum(x.size * x.dtype.itemsize for x in arrays)
    moved += sum(int(np.prod(s.shape)) * s.dtype.itemsize for s in shapes)
    return pl.pallas_call(
        kernel,
        out_shape=shapes,
        in_specs=[SM] * len(scalars) + [space] * len(arrays),
        out_specs=[first] + [VM] * (len(shapes) - 1),
        scratch_shapes=list(scratch),
        compiler_params=pltpu.CompilerParams(vmem_limit_bytes=limit * 2**20),
        cost_estimate=pl.CostEstimate(
            flops=int(flops), bytes_accessed=int(moved), transcendentals=0
        ),
        name=name,
    )(*scalars, *arrays)


def shape(dims, dtype):
    return jax.ShapeDtypeStruct(dims, dtype)


def on_device(
    features,
    grad_out,
    conv_weight,
    coarse_up,
    coarse_down,
    counts,
    neighbour_owner,
    neighbour_slot,
    parent,
    child_slot,
):
    grp = lax.axis_index("grp").astype(jnp.int32)
    core = (grp & 1).reshape(1)
    line = (grp >> 1).reshape(1)
    swap = [(i, i ^ 1) for i in range(8)]
    (msg,) = call(
        ask_kernel,
        [shape((32, 48, 128), BF)],
        [counts],
        [features, neighbour_owner, neighbour_slot],
        [
            pltpu.VMEM((2, 128, 512), BF),
            pltpu.VMEM((2, 26), jnp.int32),
            pltpu.VMEM((2, 26), jnp.int32),
            pltpu.VMEM((128, 128), F32),
            pltpu.VMEM((512, 128), F32),
            pltpu.VMEM((512, 128), F32),
            pltpu.VMEM((512, 128), F32),
            pltpu.SemaphoreType.DMA((3,)),
        ],
        flops=2e6,
        space=pl.BlockSpec(memory_space=pltpu.HBM),
        limit=60,
        name="ask",
    )
    first = lax.all_to_all(msg, "dev", split_axis=0, concat_axis=0, tiled=True)
    (answer,) = call(
        route_kernel,
        [shape((32, 32, 128), BF)],
        [],
        [first],
        [pltpu.VMEM((1024, 1024), BF)],
        flops=3e8,
        name="route",
    )
    halo = lax.all_to_all(answer, "dev", split_axis=0, concat_axis=0, tiled=True)
    table = first[:, 32:48, 0:2].transpose(0, 2, 1).reshape(1, 1024)
    table = jnp.broadcast_to(table, (16, 1024))
    taps = conv_weight.reshape(3, 1152, 128)
    taps = jnp.concatenate([taps[0], taps[1], taps[2]], axis=1)
    output, grad_pre, wsum, send = call(
        forward_kernel,
        [
            shape((2, 128, 512), BF),
            shape((2, 512, 128), BF),
            shape((4096, 128), BF),
            shape((2048, 128), BF),
        ],
        [counts, parent, child_slot, core],
        [
            features,
            halo,
            grad_out,
            taps,
            coarse_up,
            coarse_down,
        ],
        [
            pltpu.VMEM((2, 512, 128), F32),
            pltpu.VMEM((2, 512, 128), F32),
            pltpu.VMEM((2, 512, 128), F32),
            pltpu.VMEM((2, 800, 128), F32),
            pltpu.VMEM((2, 816, 128), F32),
            pltpu.VMEM((2, 800, 128), F32),
            pltpu.VMEM((1280, 1152), BF),
            pltpu.VMEM((2, 128, 512), BF),
            pltpu.VMEM((2, 16, 128), F32),
            pltpu.VMEM((2, 16, 128), F32),
            pltpu.VMEM((2, 128, 512), BF),
            pltpu.SemaphoreType.DMA((1,)),
        ],
        first=pl.BlockSpec(memory_space=pltpu.HBM),
        flops=2e9,
        name="forward",
    )

    other = lax.ppermute(send, "grp", swap)
    own_sum, *away = call(
        pair_kernel,
        [shape((512, 128), F32)] + [shape((512, 128), BF)] * 3,
        [core, line],
        [wsum, other],
        name="pair",
    )
    away = [
        lax.ppermute(x, "grp", [(i, (i + 2 * step) % 8) for i in range(8)])
        for step, x in zip((1, 2, 3), away)
    ]
    grad_pre, own_sum = lax.optimization_barrier((grad_pre, own_sum))
    own, terms = call(
        backward_kernel,
        [shape((2, 512, 128), F32), shape((32, 32, 128), BF)],
        [],
        [grad_pre, taps],
        [
            pltpu.VMEM((2, 640, 384), BF),
            pltpu.VMEM((2, 3, 816, 128), F32),
            pltpu.VMEM((2, 512, 128), F32),
            pltpu.VMEM((2, 512, 128), F32),
        ],
        flops=4e9,
        name="backward",
    )
    (terms,) = call(
        join_kernel,
        [shape((32, 48, 128), BF)],
        [],
        [terms, own_sum, *away],
        name="join",
    )
    terms = lax.all_to_all(terms, "dev", split_axis=0, concat_axis=0, tiled=True)
    (sums,) = call(
        merge_kernel,
        [shape((32, 48, 128), BF)],
        [],
        [terms, table],
        [pltpu.VMEM((1024, 1024), BF)],
        flops=3e8,
        name="merge",
    )
    back = lax.all_to_all(sums, "dev", split_axis=0, concat_axis=0, tiled=True)
    chunk = back[:, 32:48, :].reshape(512, 128)
    parts = [chunk] + [
        lax.ppermute(chunk, "grp", [(i, (i - 2 * step) % 8) for i in range(8)])
        for step in (1, 2, 3)
    ]
    (grad_features,) = call(
        finish_kernel,
        [shape((2, 128, 512), BF)],
        [counts],
        [back, own, grad_out],
        [pltpu.VMEM((512, 128), F32)] * 3,
        flops=3e8,
        name="finish",
    )
    chunk = lax.ppermute(chunk, "grp", swap)
    parts, grad_features = lax.optimization_barrier((parts, grad_features))
    parts = parts + [chunk] + [lax.ppermute(x, "grp", swap) for x in parts[1:]]
    grad_conv, grad_up, grad_down = call(
        assemble_kernel,
        [shape((27, 128, 128), F32), shape((128, 256), F32), shape((256, 128), F32)],
        [core, line],
        parts,
        name="assemble",
    )
    return (output, grad_features, grad_conv, grad_up, grad_down)


def solution(mesh):
    return jax.shard_map(
        on_device,
        mesh=mesh,
        in_specs=(
            P(("grp", "dev"), None, None),
            P(("grp", "dev"), None, None),
            P(),
            P(),
            P(),
            P(("grp", "dev")),
            P(("grp", "dev"), None),
            P(("grp", "dev"), None),
            P(("grp", "dev")),
            P(("grp", "dev")),
        ),
        out_specs=(P(("grp", "dev"), None, None), P(("grp", "dev"), None, None), P(), P(), P()),
        check_vma=False,
    )
```

```python
import functools

import jax
import jax.numpy as jnp
import numpy as np
from jax import lax
from jax.experimental import pallas as pl
from jax.experimental.pallas import tpu as pltpu
from jax.sharding import PartitionSpec as P

BF = jnp.bfloat16
F32 = jnp.float32

OFFSETS = [
    (a, b, c) for a in (-1, 0, 1) for b in (-1, 0, 1) for c in (-1, 0, 1) if (a, b, c) != (0, 0, 0)
]
FACES = [d for d in OFFSETS if sum(map(abs, d)) == 1]
EDGES = [d for d in OFFSETS if sum(map(abs, d)) == 2]
CORNERS = [d for d in OFFSETS if sum(map(abs, d)) == 3]
PIECE = {d: 64 * n for n, d in enumerate(FACES)}
PIECE.update({d: 384 + 8 * n for n, d in enumerate(EDGES)})
PIECE.update({d: 480 + n for n, d in enumerate(CORNERS)})


def voxel_runs(d):
    a, b, c = (7 if x < 0 else 0 for x in d)
    free = [x == 0 for x in d]
    if free == [True, True, False]:
        return [(0, c, 64, 8)]
    if free == [True, False, True]:
        return [(8 * x, x * 64 + b * 8, 8, 1) for x in range(8)]
    if free == [False, True, True]:
        return [(0, a * 64, 64, 1)]
    size = 8 if any(free) else 1
    stride = (64 if free[0] else 1) * (8 if free[1] else 1)
    return [(0, a * 64 + b * 8 + c, size, stride)]


def run(start, size, stride):
    return pl.ds(start, size) if stride == 1 else pl.ds(start, size, stride=stride)


SHARES = [((64 * f + p, 32, 2), (2 * f + p, 32, 16)) for f in range(6) for p in range(2)]
SHARES += [((384 + 32 * m, 32, 1), (12 + m, 32, 16)) for m in range(3)]


def share_directions(group):
    edges = [EDGES[4 * m + group // 2] for m in range(3)]
    return [OFFSETS.index(d) for d in [FACES[q // 2] for q in range(12)] + edges + [CORNERS[group]]]


def choice_table():
    table = np.zeros((128, 8, 128), np.float32)
    for group in range(8):
        for q, direction in enumerate(share_directions(group)):
            table[direction, group, 32 + q] = 1
    return table.reshape(128, 1024)


def few_lanes(rows):
    return lax.broadcasted_iota(jnp.int32, (rows, 128), 1) < 32


def to_pieces(rows, pieces):
    for there, here in SHARES:
        pieces[run(*there), :] = rows[run(*here), :]
    total = jnp.zeros((8, 128), F32)
    for n in range(4):
        part = jnp.where(few_lanes(8), rows[pl.ds(15 + 16 * n, 8, stride=64), :], 0.0)
        total = total + (pltpu.roll(part, 32 * n, 1) if n else part)
    pieces[pl.ds(480, 8), :] = total


def to_shares(pieces, rows, extra=None):
    for there, here in SHARES:
        rows[run(*here), :] = pieces[run(*there), :]
    for n in range(4):
        part = pieces[pl.ds(480, 8), :]
        part = pltpu.roll(part, 128 - 32 * n, 1) if n else part
        if extra is not None:
            part = jnp.where(few_lanes(8), part, extra)
        rows[pl.ds(15 + 16 * n, 8, stride=64), :] = part


def nn(x, y):
    return lax.dot_general(x, y, (((1,), (0,)), ((), ())), preferred_element_type=F32)


def nt(x, y):
    return lax.dot_general(x, y, (((1,), (1,)), ((), ())), preferred_element_type=F32)


def identity():
    rows = lax.broadcasted_iota(jnp.int32, (128, 128), 0)
    lanes = lax.broadcasted_iota(jnp.int32, (128, 128), 1)
    return (rows == lanes).astype(F32).astype(BF)


def pool_rows(s):
    rows = lax.broadcasted_iota(jnp.int32, (16, 512), 0) - 8 * s
    lanes = lax.broadcasted_iota(jnp.int32, (16, 512), 1)
    block = ((lanes >> 8) & 1) * 4 + ((lanes >> 5) & 1) * 2 + ((lanes >> 2) & 1)
    return (rows == block).astype(F32).astype(BF)


def ask_kernel(
    counts, feat, owner, slot, choice, msg,
    feat_v, owner_v, slot_v, choice_v, bricks, tables, voxels, pc, rows, msg_v, sems,
):
    pairs = (
        (owner, owner_v), (slot, slot_v), (choice, choice_v),
        (feat.at[0], feat_v.at[0]), (feat.at[1], feat_v.at[1]),
    )
    copies = [
        pltpu.make_async_copy(src, dst, sems.at[n]) for n, (src, dst) in enumerate(pairs)
    ]
    for copy in copies:
        copy.start()
    bricks[...] = jnp.zeros((16, 128), F32)
    for copy in copies[:3]:
        copy.wait()
    named = jnp.where(owner_v[...] >= 0, owner_v[...] * 2 + slot_v[...], -1)
    bricks[0:2, 0:26] = named.astype(F32)
    asked = nn(bricks[...].astype(BF), choice_v[...])
    for group in range(8):
        for s in range(2):
            tables[s, group : group + 1, :] = asked[s : s + 1, group * 128 : group * 128 + 128]
    sent = []
    for s in range(2):
        copies[3 + s].wait()
        live = (counts[0] > s).astype(F32)
        voxels[s] = (feat_v[s].astype(F32) * live).T
        for d in OFFSETS:
            for at, first, size, stride in voxel_runs(d):
                pc[s, pl.ds(PIECE[d] + at, size), :] = voxels.at[s][run(first, size, stride), :]
        to_shares(pc.at[s], rows.at[s], tables[s])
        at = pl.ds(16 * s, 16)
        msg_v[:, at, :] = rows[s].astype(BF).reshape(32, 16, 128)
        sent.append(pltpu.make_async_copy(msg_v.at[:, at, :], msg.at[:, at, :], sems.at[5 + s]))
        sent[s].start()
    for copy in sent:
        copy.wait()


def same_part():
    rows = lax.broadcasted_iota(jnp.int32, (16, 128), 0)
    lanes = lax.broadcasted_iota(jnp.int32, (16, 128), 1) & 15
    return (rows == lanes).astype(F32).astype(BF)


def route_kernel(got, out, hot, out_v, sems):
    same = jnp.broadcast_to(same_part()[None], (32, 16, 128))
    zero = jnp.zeros((32, 16, 128), BF)
    ones = jnp.ones((128, 128), BF)
    part = lax.broadcasted_iota(jnp.int32, (16, 128), 0)
    lanes = lax.broadcasted_iota(jnp.int32, (16, 128), 1)
    place = (lanes == part + 32)[None]
    sent = []
    for s in range(2):
        at = pl.ds(16 * s, 16)
        table = got[:, at, :].astype(F32)[:, 15:16, :]
        table = jnp.where(place, jnp.broadcast_to(table, (32, 16, 128)), 0.0)
        asked = nn(table.astype(BF).reshape(512, 128), ones).astype(BF).reshape(32, 16, 128)
        for n in range(8):
            here = ((lanes >> 4) + 8 * n).astype(F32).astype(BF)
            picked = jnp.where(asked == here[None], same, zero)
            hot[s, :, n * 128 : n * 128 + 128] = picked.reshape(512, 128)
        answer = nn(hot[s], got[...].reshape(1024, 128)).astype(BF)
        out_v[:, at, :] = answer.reshape(32, 16, 128)
        sent.append(pltpu.make_async_copy(out_v.at[:, at, :], out.at[:, at, :], sems.at[s]))
        sent[s].start()
    for copy in sent:
        copy.wait()


def forward_kernel(
    counts, parent, child, core, feat, got, gout, weight, up, down,
    grad_t, acts, lift, wsum, send,
    rows_all, pc_all, mine_all, s0_all, s1_all, s2_all, cols, pooled, grad_pooled,
):
    eye = identity()
    slopes = []
    for s in range(2):
        rows, pc, mine, s0, s1, s2 = (
            x.at[s] for x in (rows_all, pc_all, mine_all, s0_all, s1_all, s2_all)
        )
        live = (counts[0] > s).astype(F32)
        pool = pool_rows(s)
        mine[...] = (feat[s].astype(F32) * live).T
        grad_pooled[s] = nt(pool, gout[s]) * live
        rows[...] = got[:, 16 * s : 16 * s + 16, :].reshape(512, 128).astype(F32)
        to_pieces(rows, pc)
        for a in range(8):
            s1[pl.ds(8 + ((a + 1) * 10 + 1) * 8, 64), :] = mine[a * 64 : a * 64 + 64, :]
            for d, b in (((0, -1, 0), 0), ((0, 1, 0), 9)):
                s1[pl.ds(8 + ((a + 1) * 10 + b) * 8, 8), :] = pc[pl.ds(PIECE[d] + 8 * a, 8), :]
        for a, x in ((-1, 0), (1, 9)):
            s1[pl.ds(8 + (x * 10 + 1) * 8, 64), :] = pc[pl.ds(PIECE[a, 0, 0], 64), :]
            for b, y in ((-1, 0), (1, 9)):
                s1[pl.ds(8 + (x * 10 + y) * 8, 8), :] = pc[pl.ds(PIECE[a, b, 0], 8), :]
        s0[...] = s1[pl.ds(7, 800), :]
        s2[...] = s1[pl.ds(9, 800), :]
        for c, ref, lane in ((-1, s0, 0), (1, s2, 7)):
            for a in range(8):
                ref[pl.ds(((a + 1) * 10 + 1) * 8 + lane, 8, stride=8), :] = pc[
                    pl.ds(PIECE[0, 0, c] + 8 * a, 8), :
                ]
            for a, x in ((-1, 0), (1, 9)):
                ref[pl.ds((x * 10 + 1) * 8 + lane, 8, stride=8), :] = pc[
                    pl.ds(PIECE[a, 0, c], 8), :
                ]
                ref[pl.ds((10 + x) * 8 + lane, 8, stride=80), :] = pc[pl.ds(PIECE[0, a, c], 8), :]
                for b, y in ((-1, 0), (1, 9)):
                    ref[pl.ds((x * 10 + y) * 8 + lane, 1), :] = pc[pl.ds(PIECE[a, b, c], 1), :]
        for a in range(10):
            for b in range(3):
                for c, ref in enumerate((s0, s1, s2)):
                    start = (a * 10 + b) * 8 + (8 if c == 1 else 0)
                    at = 640 * s + 64 * a
                    cols[at : at + 64, (3 * b + c) * 128 : (3 * b + c) * 128 + 128] = ref[
                        pl.ds(start, 64), :
                    ].astype(BF)
        taps = nn(cols[640 * s : 640 * s + 640, :], weight[...])
        pre = taps[0:512, 0:128] + taps[64:576, 128:256] + taps[128:640, 256:384]
        pre = pre.T
        gate = 1.0 / (1.0 + jnp.exp(-pre))
        active = pre * gate
        acts[s] = active
        slopes.append(gate * (1.0 + pre * (1.0 - gate)))
        high = active.astype(BF)
        low = (active - high.astype(F32)).astype(BF)
        pooled[s] = nt(pool, high) + nt(pool, low)
    second = lax.broadcasted_iota(jnp.int32, (16, 1), 0) >= 8
    valid = [
        (
            (counts[0] > s) & (parent[s] >= 0) & (parent[s] * 64 + child[s] >= 0)
        ).astype(F32)
        for s in range(2)
    ]
    valid = jnp.where(second, valid[1], valid[0])
    coarse_in = ((pooled[0] + pooled[1]) * (1.0 / 64.0) * valid).astype(BF)
    grad_out = ((grad_pooled[0] + grad_pooled[1]) * valid).astype(BF)
    coarse_pre = nn(coarse_in, up[...])
    gate = 1.0 / (1.0 + jnp.exp(-coarse_pre))
    coarse_mid = (coarse_pre * gate).astype(BF)
    grad_pre = nt(grad_out, down[...]) * (gate * (1.0 + coarse_pre * (1.0 - gate)))
    grad_pre = grad_pre.astype(BF)
    coarse_out = nn(coarse_mid, down[...]).astype(BF)
    grad_cin = nt(grad_pre, up[...]).astype(BF)
    lift[...] = nt(eye, coarse_out).astype(BF)
    back = nt(eye, grad_cin).astype(BF)
    for s in range(2):
        live = (counts[0] > s).astype(F32)
        grad_in = gout[s].astype(F32) * live + nn(back, pool_rows(s)) * (1.0 / 64.0)
        grad_t[s] = (grad_in * slopes[s]).astype(BF)

    def put(block, value):
        wsum[pl.ds(block * 128, 128), :] = value.astype(BF)

    grad_up = nn(nt(eye, coarse_in).astype(BF), grad_pre)
    for h in range(2):
        put(27 + h, grad_up[:, h * 128 : h * 128 + 128])
        middle = nt(eye, coarse_mid[:, h * 128 : h * 128 + 128]).astype(BF)
        put(29 + h, nn(middle, grad_out))
    put(31, jnp.zeros((128, 128), F32))
    for a in range(3):
        total = nn(grad_t[0], cols[64 * a : 64 * a + 512, :])
        total = total + nn(grad_t[1], cols[64 * a + 640 : 64 * a + 1152, :])
        total = total.astype(BF)
        for n in range(9):
            put(9 * a + n, nt(eye, total[:, n * 128 : n * 128 + 128]))
    send[...] = wsum[pl.ds(pl.multiple_of((1 - core[0]) * 2048, 2048), 2048), :]


def pair_kernel(core, line, wsum, other, own, one, two, three):
    for step, ref in enumerate((own, one, two, three)):
        at = pl.multiple_of(((line[0] + step) & 3) * 512, 512)
        kept = wsum[pl.ds(pl.multiple_of(core[0] * 2048 + at, 512), 512), :].astype(F32)
        ref[...] = (kept + other[pl.ds(at, 512), :].astype(F32)).astype(ref.dtype)


def backward_kernel(
    counts, feat, grad_t, acts, lift, weight,
    own, out, msg,
    lhs, acc_all, pc_all, rows_all, out_v, msg_v, sems,
):
    sent = []

    def send(src, dst):
        sent.append(pltpu.make_async_copy(src, dst, sems.at[len(sent)]))
        sent[-1].start()

    for s in range(2):
        live = (counts[0] > s).astype(F32)
        value = feat[s].astype(F32) * live + acts[s] + nn(lift[...], pool_rows(s))
        out_v[s] = value.astype(BF)
    send(out_v, out)
    zero = jnp.zeros((64, 128), BF)
    for a in range(3):
        for n in [*range(a), *range(8 + a, 10)]:
            for s in range(2):
                lhs[s, n * 64 : n * 64 + 64, a * 128 : a * 128 + 128] = zero
    low = (lax.broadcasted_iota(jnp.int32, (64, 1), 0) & 7) != 0
    high = (lax.broadcasted_iota(jnp.int32, (64, 1), 0) & 7) != 7

    for s in range(2):
        acc, pc, rows = acc_all.at[s], pc_all.at[s], rows_all.at[s]
        grad = grad_t[s].astype(F32).T.astype(BF)
        for a in range(3):
            lhs[s, a * 64 : a * 64 + 512, a * 128 : a * 128 + 128] = grad
        acc[...] = jnp.zeros_like(acc)
        for b in range(3):
            part = nt(lhs[s], weight[b * 384 : b * 384 + 384, :])
            for c in range(3):
                for a in range(10):
                    at = pl.ds(8 + (a * 10 + b) * 8, 64)
                    acc[c, at, :] += part[a * 64 : a * 64 + 64, c * 128 : c * 128 + 128]

        def middle(row, size):
            at = 8 + row
            total = acc[1, pl.ds(at, size), :]
            total = total + jnp.where(high[:size], acc[0, pl.ds(at + 1, size), :], 0.0)
            return total + jnp.where(low[:size], acc[2, pl.ds(at - 1, size), :], 0.0)

        for a in range(8):
            own[s, pl.ds(a * 64, 64), :] = middle(((a + 1) * 10 + 1) * 8, 64)
            for d, b in (((0, -1, 0), 0), ((0, 1, 0), 9)):
                pc[pl.ds(PIECE[d] + 8 * a, 8), :] = middle(((a + 1) * 10 + b) * 8, 8)
        for a, x in ((-1, 0), (1, 9)):
            pc[pl.ds(PIECE[a, 0, 0], 64), :] = middle((x * 10 + 1) * 8, 64)
            for b, y in ((-1, 0), (1, 9)):
                pc[pl.ds(PIECE[a, b, 0], 8), :] = middle((x * 10 + y) * 8, 8)
        for c, ref, lane in ((-1, acc.at[0], 8), (1, acc.at[2], 15)):
            for a in range(8):
                pc[pl.ds(PIECE[0, 0, c] + 8 * a, 8), :] = ref[
                    pl.ds(((a + 1) * 10 + 1) * 8 + lane, 8, stride=8), :
                ]
            for a, x in ((-1, 0), (1, 9)):
                pc[pl.ds(PIECE[a, 0, c], 8), :] = ref[pl.ds((x * 10 + 1) * 8 + lane, 8, stride=8), :]
                pc[pl.ds(PIECE[0, a, c], 8), :] = ref[pl.ds((10 + x) * 8 + lane, 8, stride=80), :]
                for b, y in ((-1, 0), (1, 9)):
                    pc[pl.ds(PIECE[a, b, c], 1), :] = ref[pl.ds((x * 10 + y) * 8 + lane, 1), :]
        to_shares(pc, rows)
        at = pl.ds(16 * s, 16)
        msg_v[:, at, :] = rows[...].astype(BF).reshape(32, 16, 128)
        send(msg_v.at[:, at, :], msg.at[:, at, :])
    for copy in sent:
        copy.wait()


def join_kernel(terms, own, away1, away2, away3, msg, share, sem):
    total = own[...] + away1[...].astype(F32) + away2[...].astype(F32) + away3[...].astype(F32)
    share[...] = total.astype(BF).reshape(32, 16, 128)
    copy = pltpu.make_async_copy(share, msg.at[:, pl.ds(32, 16), :], sem.at[0])
    copy.start()
    copy.wait()


def merge_kernel(got, table, out, hot):
    same = same_part()
    zero = jnp.zeros((16, 128), BF)
    share = jnp.sum(got[:, 32:48, :].astype(F32), axis=0).astype(BF)
    out[:, 32:48, :] = jnp.broadcast_to(share[None], (32, 16, 128))
    for n in range(8):
        asked = table[:, n * 128 : n * 128 + 128]
        for brick in range(64):
            hot[brick * 16 : brick * 16 + 16, n * 128 : n * 128 + 128] = jnp.where(
                asked == jnp.full((16, 128), brick, BF), same, zero
            )
    total = nn(hot[...], got[:, 0:32, :].reshape(1024, 128))
    out[:, 0:32, :] = total.astype(BF).reshape(32, 32, 128)


def finish_kernel(counts, got, own, gout, out, rows, pc, total):
    for s in range(2):
        live = (counts[0] > s).astype(F32)
        rows[...] = got[:, 16 * s : 16 * s + 16, :].reshape(512, 128).astype(F32)
        to_pieces(rows, pc)
        total[...] = own[s]
        for d in OFFSETS:
            for at, first, size, stride in voxel_runs(d):
                where = run(first, size, stride)
                total[where, :] = total[where, :] + pc[pl.ds(PIECE[d] + at, size), :]
        out[s] = (total[...].T + gout[s].astype(F32) * live).astype(BF)


def assemble_kernel(flip, core, line, *refs):
    parts, (conv, up, down, held, sems) = refs[:4], refs[-5:]
    half = core[0] ^ flip

    def moves(n, first):
        def copy(src, dst, k):
            return pltpu.make_async_copy(src, dst, sems.at[n, k])

        block = held.at[n]
        return (
            (first < 24, lambda: [copy(block, conv.at[pl.ds(first, 4)], 0)]),
            (
                first == 24,
                lambda: [
                    copy(block.at[0:3], conv.at[pl.ds(24, 3)], 0),
                    copy(block.at[3], up.at[:, pl.ds(0, 128)], 1),
                ],
            ),
            (
                first == 28,
                lambda: [
                    copy(block.at[0], up.at[:, pl.ds(128, 128)], 0),
                    copy(block.at[1], down.at[pl.ds(0, 128), :], 1),
                    copy(block.at[2], down.at[pl.ds(128, 128), :], 2),
                ],
            ),
        )

    firsts = [half * 16 + ((line[0] + n) & 3) * 4 for n in range(4)]
    for n, part in enumerate(parts):
        held[n] = part[...].astype(F32).reshape(4, 128, 128)
        for when, copies in moves(n, firsts[n]):

            @pl.when(when)
            def _():
                for copy in copies():
                    copy.start()

    for n in range(4):
        for when, copies in moves(n, firsts[n]):

            @pl.when(when)
            def _():
                for copy in copies():
                    copy.wait()


VM = pl.BlockSpec(memory_space=pltpu.VMEM)
SM = pl.BlockSpec(memory_space=pltpu.SMEM)


HB = pl.BlockSpec(memory_space=pltpu.HBM)


def call(
    kernel, shapes, scalars, arrays, scratch=(), flops=1e6, limit=24, ins=None, outs=None,
    alias=None, name=None,
):
    moved = sum(x.size * x.dtype.itemsize for x in arrays)
    moved += sum(int(np.prod(s.shape)) * s.dtype.itemsize for s in shapes)
    return pl.pallas_call(
        kernel,
        out_shape=shapes,
        in_specs=[SM] * len(scalars) + (ins or [VM] * len(arrays)),
        out_specs=outs or [VM] * len(shapes),
        input_output_aliases=alias or {},
        scratch_shapes=list(scratch),
        compiler_params=pltpu.CompilerParams(vmem_limit_bytes=limit * 2**20),
        cost_estimate=pl.CostEstimate(
            flops=int(flops), bytes_accessed=int(moved), transcendentals=0
        ),
        name=name,
    )(*scalars, *arrays)


def shape(dims, dtype):
    return jax.ShapeDtypeStruct(dims, dtype)


def on_device(
    features,
    grad_out,
    conv_weight,
    coarse_up,
    coarse_down,
    counts,
    neighbour_owner,
    neighbour_slot,
    parent,
    child_slot,
):
    grp = lax.axis_index("grp").astype(jnp.int32)
    core = (grp & 1).reshape(1)
    line = (grp >> 1).reshape(1)
    swap = [(i, i ^ 1) for i in range(8)]
    (msg,) = call(
        ask_kernel,
        [shape((32, 32, 128), BF)],
        [counts],
        [features, neighbour_owner, neighbour_slot, jnp.asarray(choice_table(), BF)],
        [
            pltpu.VMEM((2, 128, 512), BF),
            pltpu.VMEM((2, 26), jnp.int32),
            pltpu.VMEM((2, 26), jnp.int32),
            pltpu.VMEM((128, 1024), BF),
            pltpu.VMEM((16, 128), F32),
            pltpu.VMEM((2, 8, 128), F32),
            pltpu.VMEM((2, 512, 128), F32),
            pltpu.VMEM((2, 512, 128), F32),
            pltpu.VMEM((2, 512, 128), F32),
            pltpu.VMEM((32, 32, 128), BF),
            pltpu.SemaphoreType.DMA((7,)),
        ],
        flops=2e6,
        limit=60,
        ins=[HB] * 3 + [pl.BlockSpec(memory_space=pl.ANY)],
        outs=[HB],
        name="ask",
    )
    first = lax.all_to_all(msg, "dev", split_axis=0, concat_axis=0, tiled=True)
    (answer,) = call(
        route_kernel,
        [shape((32, 32, 128), BF)],
        [],
        [first],
        [
            pltpu.VMEM((2, 512, 1024), BF),
            pltpu.VMEM((32, 32, 128), BF),
            pltpu.SemaphoreType.DMA((2,)),
        ],
        flops=3e8,
        outs=[HB],
        name="route",
    )
    halo = lax.all_to_all(answer, "dev", split_axis=0, concat_axis=0, tiled=True)
    table = first.reshape(32, 2, 16, 128)[:, :, 15, 32:48].reshape(1, 1024)
    table = jnp.broadcast_to(table, (16, 1024))
    taps = conv_weight.reshape(3, 1152, 128)
    taps = jnp.concatenate([taps[0], taps[1], taps[2]], axis=1)
    grad_pre, acts, lift, wsum, send = call(
        forward_kernel,
        [
            shape((2, 128, 512), BF),
            shape((2, 128, 512), F32),
            shape((128, 16), BF),
            shape((4096, 128), BF),
            shape((2048, 128), BF),
        ],
        [counts, parent, child_slot, core],
        [features, halo, grad_out, taps, coarse_up, coarse_down],
        [
            pltpu.VMEM((2, 512, 128), F32),
            pltpu.VMEM((2, 512, 128), F32),
            pltpu.VMEM((2, 512, 128), F32),
            pltpu.VMEM((2, 800, 128), F32),
            pltpu.VMEM((2, 816, 128), F32),
            pltpu.VMEM((2, 800, 128), F32),
            pltpu.VMEM((1280, 1152), BF),
            pltpu.VMEM((2, 16, 128), F32),
            pltpu.VMEM((2, 16, 128), F32),
        ],
        flops=2e9,
        name="forward",
    )
    other = lax.ppermute(send, "grp", swap)
    own_sum, *away = call(
        pair_kernel,
        [shape((512, 128), F32)] + [shape((512, 128), BF)] * 3,
        [core, line],
        [wsum, other],
        name="pair",
    )
    away = [
        lax.ppermute(away[step - 1], "grp", [(i, (i + 2 * step) % 8) for i in range(8)])
        for step in (2, 1, 3)
    ]
    grad_pre, own_sum = lax.optimization_barrier((grad_pre, own_sum))
    own, output, terms = call(
        backward_kernel,
        [shape((2, 512, 128), F32), shape((2, 128, 512), BF), shape((32, 48, 128), BF)],
        [counts],
        [features, grad_pre, acts, lift, taps],
        [
            pltpu.VMEM((2, 640, 384), BF),
            pltpu.VMEM((2, 3, 816, 128), F32),
            pltpu.VMEM((2, 512, 128), F32),
            pltpu.VMEM((2, 512, 128), F32),
            pltpu.VMEM((2, 128, 512), BF),
            pltpu.VMEM((32, 32, 128), BF),
            pltpu.SemaphoreType.DMA((3,)),
        ],
        flops=4e9,
        outs=[VM, HB, HB],
        name="backward",
    )
    (terms,) = call(
        join_kernel,
        [shape((32, 48, 128), BF)],
        [],
        [terms, own_sum, *away],
        [pltpu.VMEM((32, 16, 128), BF), pltpu.SemaphoreType.DMA((1,))],
        ins=[HB] + [VM] * 4,
        outs=[HB],
        alias={0: 0},
        name="join",
    )
    terms = lax.all_to_all(terms, "dev", split_axis=0, concat_axis=0, tiled=True)
    (sums,) = call(
        merge_kernel,
        [shape((32, 48, 128), BF)],
        [],
        [terms, table],
        [pltpu.VMEM((1024, 1024), BF)],
        flops=3e8,
        name="merge",
    )
    back = lax.all_to_all(sums, "dev", split_axis=0, concat_axis=0, tiled=True)
    chunk = back[:, 32:48, :].reshape(512, 128)
    parts = {
        step: lax.ppermute(chunk, "grp", [(i, (i - 2 * step) % 8) for i in range(8)])
        for step in (2, 1, 3)
    }
    (grad_features,) = call(
        finish_kernel,
        [shape((2, 128, 512), BF)],
        [counts],
        [back, own, grad_out],
        [pltpu.VMEM((512, 128), F32)] * 3,
        flops=3e8,
        name="finish",
    )
    parts, grad_features = lax.optimization_barrier((parts, grad_features))
    mine = [chunk, parts[1], parts[2], parts[3]]
    others = [lax.ppermute(x, "grp", swap) for x in mine]

    def assemble(flip, pieces, held):
        return call(
            functools.partial(assemble_kernel, flip),
            [shape((27, 128, 128), F32), shape((128, 256), F32), shape((256, 128), F32)],
            [core, line],
            pieces + held,
            [pltpu.VMEM((4, 4, 128, 128), F32), pltpu.SemaphoreType.DMA((4, 3))],
            ins=[VM] * 4 + [HB] * len(held),
            outs=[HB] * 3,
            alias={6 + n: n for n in range(len(held))},
            name="assemble",
        )

    grad_conv, grad_up, grad_down = assemble(1, others, list(assemble(0, mine, [])))
    return (output, grad_features, grad_conv, grad_up, grad_down)


def solution(mesh):
    return jax.shard_map(
        on_device,
        mesh=mesh,
        in_specs=(
            P(("grp", "dev"), None, None),
            P(("grp", "dev"), None, None),
            P(),
            P(),
            P(),
            P(("grp", "dev")),
            P(("grp", "dev"), None),
            P(("grp", "dev"), None),
            P(("grp", "dev")),
            P(("grp", "dev")),
        ),
        out_specs=(P(("grp", "dev"), None, None), P(("grp", "dev"), None, None), P(), P(), P()),
        check_vma=False,
    )
```

```python
import functools

import jax
import jax.numpy as jnp
import numpy as np
from jax import lax
from jax.experimental import pallas as pl
from jax.experimental.pallas import tpu as pltpu
from jax.sharding import PartitionSpec as P

BF = jnp.bfloat16
F32 = jnp.float32

OFFSETS = [
    (a, b, c) for a in (-1, 0, 1) for b in (-1, 0, 1) for c in (-1, 0, 1) if (a, b, c) != (0, 0, 0)
]
FACES = [d for d in OFFSETS if sum(map(abs, d)) == 1]
EDGES = [d for d in OFFSETS if sum(map(abs, d)) == 2]
CORNERS = [d for d in OFFSETS if sum(map(abs, d)) == 3]
PIECE = {d: 64 * n for n, d in enumerate(FACES)}
PIECE.update({d: 384 + 8 * n for n, d in enumerate(EDGES)})
PIECE.update({d: 480 + n for n, d in enumerate(CORNERS)})


def voxel_runs(d):
    a, b, c = (7 if x < 0 else 0 for x in d)
    free = [x == 0 for x in d]
    if free == [True, True, False]:
        return [(0, c, 64, 8)]
    if free == [True, False, True]:
        return [(8 * x, x * 64 + b * 8, 8, 1) for x in range(8)]
    if free == [False, True, True]:
        return [(0, a * 64, 64, 1)]
    size = 8 if any(free) else 1
    stride = (64 if free[0] else 1) * (8 if free[1] else 1)
    return [(0, a * 64 + b * 8 + c, size, stride)]


def run(start, size, stride):
    return pl.ds(start, size) if stride == 1 else pl.ds(start, size, stride=stride)


SHARES = [((64 * f + p, 32, 2), (2 * f + p, 32, 16)) for f in range(6) for p in range(2)]
SHARES += [((384 + 32 * m, 32, 1), (12 + m, 32, 16)) for m in range(3)]


def share_directions(group):
    edges = [EDGES[4 * m + group // 2] for m in range(3)]
    return [OFFSETS.index(d) for d in [FACES[q // 2] for q in range(12)] + edges + [CORNERS[group]]]


def choice_table():
    table = np.zeros((128, 8, 128), np.float32)
    for group in range(8):
        for q, direction in enumerate(share_directions(group)):
            table[direction, group, 32 + q] = 1
    return table.reshape(128, 1024)


def few_lanes(rows):
    return lax.broadcasted_iota(jnp.int32, (rows, 128), 1) < 32


def to_pieces(rows, pieces):
    for there, here in SHARES:
        pieces[run(*there), :] = rows[run(*here), :]
    total = jnp.zeros((8, 128), F32)
    for n in range(4):
        part = jnp.where(few_lanes(8), rows[pl.ds(15 + 16 * n, 8, stride=64), :], 0.0)
        total = total + (pltpu.roll(part, 32 * n, 1) if n else part)
    pieces[pl.ds(480, 8), :] = total


def to_shares(pieces, rows, extra=None):
    for there, here in SHARES:
        rows[run(*here), :] = pieces[run(*there), :]
    for n in range(4):
        part = pieces[pl.ds(480, 8), :]
        part = pltpu.roll(part, 128 - 32 * n, 1) if n else part
        if extra is not None:
            part = jnp.where(few_lanes(8), part, extra)
        rows[pl.ds(15 + 16 * n, 8, stride=64), :] = part


def nn(x, y):
    return lax.dot_general(x, y, (((1,), (0,)), ((), ())), preferred_element_type=F32)


def nt(x, y):
    return lax.dot_general(x, y, (((1,), (1,)), ((), ())), preferred_element_type=F32)


def identity():
    rows = lax.broadcasted_iota(jnp.int32, (128, 128), 0)
    lanes = lax.broadcasted_iota(jnp.int32, (128, 128), 1)
    return (rows == lanes).astype(F32).astype(BF)


def pool_rows(s):
    rows = lax.broadcasted_iota(jnp.int32, (16, 512), 0) - 8 * s
    lanes = lax.broadcasted_iota(jnp.int32, (16, 512), 1)
    block = ((lanes >> 8) & 1) * 4 + ((lanes >> 5) & 1) * 2 + ((lanes >> 2) & 1)
    return (rows == block).astype(F32).astype(BF)


def ask_kernel(
    live_count, feat, owner, slot, choice, msg, flags,
    counts, feat_v, owner_v, slot_v, choice_v, bricks, tables, voxels, pc, rows, msg_v, flags_v, sems,
):
    pairs = (
        (owner, owner_v), (slot, slot_v), (choice, choice_v), (live_count, counts),
        (feat.at[0], feat_v.at[0]), (feat.at[1], feat_v.at[1]),
    )
    copies = [
        pltpu.make_async_copy(src, dst, sems.at[n]) for n, (src, dst) in enumerate(pairs)
    ]
    for copy in copies:
        copy.start()
    bricks[...] = jnp.zeros((16, 128), F32)
    for copy in copies[:4]:
        copy.wait()
    named = jnp.where(owner_v[...] >= 0, owner_v[...] * 2 + slot_v[...], -1)
    bricks[0:2, 0:26] = named.astype(F32)
    asked = nn(bricks[...].astype(BF), choice_v[...])
    for group in range(8):
        for s in range(2):
            tables[s, group : group + 1, :] = asked[s : s + 1, group * 128 : group * 128 + 128]
    slots = lax.broadcasted_iota(jnp.int32, (8, 128), 0)
    flags_v[...] = (slots < counts[0]).astype(F32)
    sent = [pltpu.make_async_copy(flags_v, flags, sems.at[8])]
    sent[0].start()
    for s in range(2):
        copies[4 + s].wait()
        live = (counts[0] > s).astype(F32)
        voxels[s] = (feat_v[s].astype(F32) * live).T
        for d in OFFSETS:
            for at, first, size, stride in voxel_runs(d):
                pc[s, pl.ds(PIECE[d] + at, size), :] = voxels.at[s][run(first, size, stride), :]
        to_shares(pc.at[s], rows.at[s], tables[s])
        at = pl.ds(16 * s, 16)
        msg_v[:, at, :] = rows[s].astype(BF).reshape(32, 16, 128)
        sent.append(pltpu.make_async_copy(msg_v.at[:, at, :], msg.at[:, at, :], sems.at[6 + s]))
        sent[-1].start()
    for copy in sent:
        copy.wait()


def same_part():
    rows = lax.broadcasted_iota(jnp.int32, (16, 128), 0)
    lanes = lax.broadcasted_iota(jnp.int32, (16, 128), 1) & 15
    return (rows == lanes).astype(F32).astype(BF)


def route_kernel(got, out, named, hot):
    same = jnp.broadcast_to(same_part()[None], (32, 16, 128))
    zero = jnp.zeros((32, 16, 128), BF)
    ones = jnp.ones((128, 128), BF)
    part = lax.broadcasted_iota(jnp.int32, (16, 128), 0)
    lanes = lax.broadcasted_iota(jnp.int32, (16, 128), 1)
    place = (lanes == part + 32)[None]
    for s in range(2):
        table = got[:, 16 * s : 16 * s + 16, :].astype(F32)[:, 15:16, :]
        table = jnp.where(place, jnp.broadcast_to(table, (32, 16, 128)), 0.0)
        asked = nn(table.astype(BF).reshape(512, 128), ones)
        named[s] = asked.T[0:16].astype(BF)
        asked = asked.astype(BF).reshape(32, 16, 128)
        for n in range(8):
            here = ((lanes >> 4) + 8 * n).astype(F32).astype(BF)
            picked = jnp.where(asked == here[None], same, zero)
            hot[s * 512 : s * 512 + 512, n * 128 : n * 128 + 128] = picked.reshape(512, 128)
    answer = nn(hot[...], got[...].reshape(1024, 128)).astype(BF)
    for s in range(2):
        out[:, 16 * s : 16 * s + 16, :] = answer[s * 512 : s * 512 + 512].reshape(32, 16, 128)


def forward_kernel(
    parent, child, core, flags, feat, got, gout, weight, up, down,
    out, grad_t, wsum, send,
    rows_all, pc_all, mine_all, s0_all, s1_all, s2_all, cols, pooled, grad_pooled, out_v, sem,
):
    eye = identity()
    acts, slopes = [], []
    for s in range(2):
        rows, pc, mine, s0, s1, s2 = (
            x.at[s] for x in (rows_all, pc_all, mine_all, s0_all, s1_all, s2_all)
        )
        live = flags[s : s + 1, 0:1]
        pool = pool_rows(s)
        mine[...] = (feat[s].astype(F32) * live).T
        grad_pooled[s] = nt(pool, gout[s]) * live
        rows[...] = got[:, 16 * s : 16 * s + 16, :].reshape(512, 128).astype(F32)
        to_pieces(rows, pc)
        for a in range(8):
            s1[pl.ds(8 + ((a + 1) * 10 + 1) * 8, 64), :] = mine[a * 64 : a * 64 + 64, :]
            for d, b in (((0, -1, 0), 0), ((0, 1, 0), 9)):
                s1[pl.ds(8 + ((a + 1) * 10 + b) * 8, 8), :] = pc[pl.ds(PIECE[d] + 8 * a, 8), :]
        for a, x in ((-1, 0), (1, 9)):
            s1[pl.ds(8 + (x * 10 + 1) * 8, 64), :] = pc[pl.ds(PIECE[a, 0, 0], 64), :]
            for b, y in ((-1, 0), (1, 9)):
                s1[pl.ds(8 + (x * 10 + y) * 8, 8), :] = pc[pl.ds(PIECE[a, b, 0], 8), :]
        s0[...] = s1[pl.ds(7, 800), :]
        s2[...] = s1[pl.ds(9, 800), :]
        for c, ref, lane in ((-1, s0, 0), (1, s2, 7)):
            for a in range(8):
                ref[pl.ds(((a + 1) * 10 + 1) * 8 + lane, 8, stride=8), :] = pc[
                    pl.ds(PIECE[0, 0, c] + 8 * a, 8), :
                ]
            for a, x in ((-1, 0), (1, 9)):
                ref[pl.ds((x * 10 + 1) * 8 + lane, 8, stride=8), :] = pc[
                    pl.ds(PIECE[a, 0, c], 8), :
                ]
                ref[pl.ds((10 + x) * 8 + lane, 8, stride=80), :] = pc[pl.ds(PIECE[0, a, c], 8), :]
                for b, y in ((-1, 0), (1, 9)):
                    ref[pl.ds((x * 10 + y) * 8 + lane, 1), :] = pc[pl.ds(PIECE[a, b, c], 1), :]
        for a in range(10):
            for b in range(3):
                for c, ref in enumerate((s0, s1, s2)):
                    start = (a * 10 + b) * 8 + (8 if c == 1 else 0)
                    at = 640 * s + 64 * a
                    cols[at : at + 64, (3 * b + c) * 128 : (3 * b + c) * 128 + 128] = ref[
                        pl.ds(start, 64), :
                    ].astype(BF)
        pre = nn(cols[640 * s : 640 * s + 512, :], weight[0])
        pre = pre + nn(cols[640 * s + 64 : 640 * s + 576, :], weight[1])
        pre = pre + nn(cols[640 * s + 128 : 640 * s + 640, :], weight[2])
        pre = pre.T
        gate = 1.0 / (1.0 + jnp.exp(-pre))
        active = pre * gate
        acts.append(active)
        slopes.append(gate * (1.0 + pre * (1.0 - gate)))
        high = active.astype(BF)
        low = (active - high.astype(F32)).astype(BF)
        pooled[s] = nt(pool, high) + nt(pool, low)
    second = lax.broadcasted_iota(jnp.int32, (16, 1), 0) >= 8
    valid = [
        ((parent[s] >= 0) & (parent[s] * 64 + child[s] >= 0)).astype(F32) * flags[s : s + 1, 0:1]
        for s in range(2)
    ]
    valid = jnp.where(second, valid[1], valid[0])
    coarse_in = ((pooled[0] + pooled[1]) * (1.0 / 64.0) * valid).astype(BF)
    grad_out = ((grad_pooled[0] + grad_pooled[1]) * valid).astype(BF)
    coarse_pre = nn(coarse_in, up[...])
    gate = 1.0 / (1.0 + jnp.exp(-coarse_pre))
    coarse_mid = (coarse_pre * gate).astype(BF)
    grad_pre = nt(grad_out, down[...]) * (gate * (1.0 + coarse_pre * (1.0 - gate)))
    grad_pre = grad_pre.astype(BF)
    coarse_out = nn(coarse_mid, down[...]).astype(BF)
    grad_cin = nt(grad_pre, up[...]).astype(BF)
    lift = nt(eye, coarse_out).astype(BF)
    back = nt(eye, grad_cin).astype(BF)
    for s in range(2):
        live = flags[s : s + 1, 0:1]
        pool = pool_rows(s)
        grad_in = gout[s].astype(F32) * live + nn(back, pool) * (1.0 / 64.0)
        grad_t[s] = (grad_in * slopes[s]).astype(BF)
        out_v[s] = (feat[s].astype(F32) * live + acts[s] + nn(lift, pool)).astype(BF)
    copy = pltpu.make_async_copy(out_v, out, sem.at[0])
    copy.start()

    def put(block, value):
        wsum[pl.ds(block * 128, 128), :] = value.astype(BF)

    grad_up = nn(nt(eye, coarse_in).astype(BF), grad_pre)
    for h in range(2):
        put(27 + h, grad_up[:, h * 128 : h * 128 + 128])
        middle = nt(eye, coarse_mid[:, h * 128 : h * 128 + 128]).astype(BF)
        put(29 + h, nn(middle, grad_out))
    put(31, jnp.zeros((128, 128), F32))
    for a in range(3):
        total = nn(grad_t[0], cols[64 * a : 64 * a + 512, :])
        total = total + nn(grad_t[1], cols[64 * a + 640 : 64 * a + 1152, :])
        total = total.astype(BF)
        for n in range(9):
            put(9 * a + n, nt(eye, total[:, n * 128 : n * 128 + 128]))
    send[...] = wsum[pl.ds(pl.multiple_of((1 - core[0]) * 2048, 2048), 2048), :]
    copy.wait()


def pair_kernel(core, line, wsum, other, own, one, two, three):
    for step, ref in enumerate((own, one, two, three)):
        at = pl.multiple_of(((line[0] + step) & 3) * 512, 512)
        kept = wsum[pl.ds(pl.multiple_of(core[0] * 2048 + at, 512), 512), :].astype(F32)
        ref[...] = (kept + other[pl.ds(at, 512), :].astype(F32)).astype(ref.dtype)


def backward_kernel(grad_t, weight, own, msg, lhs, rhs, acc_all, pc_all, rows_all):
    zero = jnp.zeros((64, 128), BF)
    for a in range(3):
        rhs[:, a * 128 : a * 128 + 128] = weight[a]
        for n in [*range(a), *range(8 + a, 10)]:
            for s in range(2):
                lhs[s, n * 64 : n * 64 + 64, a * 128 : a * 128 + 128] = zero
    low = (lax.broadcasted_iota(jnp.int32, (64, 1), 0) & 7) != 0
    high = (lax.broadcasted_iota(jnp.int32, (64, 1), 0) & 7) != 7

    for s in range(2):
        acc, pc, rows = acc_all.at[s], pc_all.at[s], rows_all.at[s]
        grad = grad_t[s].astype(F32).T.astype(BF)
        for a in range(3):
            lhs[s, a * 64 : a * 64 + 512, a * 128 : a * 128 + 128] = grad
        acc[...] = jnp.zeros_like(acc)
        for b in range(3):
            part = nt(lhs[s], rhs[b * 384 : b * 384 + 384, :])
            for c in range(3):
                for a in range(10):
                    at = pl.ds(8 + (a * 10 + b) * 8, 64)
                    acc[c, at, :] += part[a * 64 : a * 64 + 64, c * 128 : c * 128 + 128]

        def middle(row, size):
            at = 8 + row
            total = acc[1, pl.ds(at, size), :]
            total = total + jnp.where(high[:size], acc[0, pl.ds(at + 1, size), :], 0.0)
            return total + jnp.where(low[:size], acc[2, pl.ds(at - 1, size), :], 0.0)

        for a in range(8):
            own[s, pl.ds(a * 64, 64), :] = middle(((a + 1) * 10 + 1) * 8, 64)
            for d, b in (((0, -1, 0), 0), ((0, 1, 0), 9)):
                pc[pl.ds(PIECE[d] + 8 * a, 8), :] = middle(((a + 1) * 10 + b) * 8, 8)
        for a, x in ((-1, 0), (1, 9)):
            pc[pl.ds(PIECE[a, 0, 0], 64), :] = middle((x * 10 + 1) * 8, 64)
            for b, y in ((-1, 0), (1, 9)):
                pc[pl.ds(PIECE[a, b, 0], 8), :] = middle((x * 10 + y) * 8, 8)
        for c, ref, lane in ((-1, acc.at[0], 8), (1, acc.at[2], 15)):
            for a in range(8):
                pc[pl.ds(PIECE[0, 0, c] + 8 * a, 8), :] = ref[
                    pl.ds(((a + 1) * 10 + 1) * 8 + lane, 8, stride=8), :
                ]
            for a, x in ((-1, 0), (1, 9)):
                pc[pl.ds(PIECE[a, 0, c], 8), :] = ref[pl.ds((x * 10 + 1) * 8 + lane, 8, stride=8), :]
                pc[pl.ds(PIECE[0, a, c], 8), :] = ref[pl.ds((10 + x) * 8 + lane, 8, stride=80), :]
                for b, y in ((-1, 0), (1, 9)):
                    pc[pl.ds(PIECE[a, b, c], 1), :] = ref[pl.ds((x * 10 + y) * 8 + lane, 1), :]
        to_shares(pc, rows)
        msg[:, 16 * s : 16 * s + 16, :] = rows[...].astype(BF).reshape(32, 16, 128)


def join_kernel(terms, own, away1, away2, away3, msg):
    msg[:, 0:32, :] = terms[...]
    total = own[...] + away1[...].astype(F32) + away2[...].astype(F32) + away3[...].astype(F32)
    msg[:, 32:48, :] = total.astype(BF).reshape(32, 16, 128)


def merge_kernel(got, named, out, hot):
    same = same_part()
    zero = jnp.zeros((16, 128), BF)
    share = jnp.sum(got[:, 32:48, :].astype(F32), axis=0).astype(BF)
    out[:, 32:48, :] = jnp.broadcast_to(share[None], (32, 16, 128))
    total = jnp.zeros((1024, 128), F32)
    for s in range(2):
        for n in range(4):
            asked = named[s, :, n * 128 : n * 128 + 128]
            for brick in range(64):
                hot[s, brick * 16 : brick * 16 + 16, n * 128 : n * 128 + 128] = jnp.where(
                    asked == jnp.full((16, 128), brick, BF), same, zero
                )
        total = total + nn(hot[s], got[:, 16 * s : 16 * s + 16, :].reshape(512, 128))
    out[:, 0:32, :] = total.astype(BF).reshape(32, 32, 128)


def finish_kernel(flags, got, own, gout, out, rows, pc, total):
    for s in range(2):
        live = flags[s : s + 1, 0:1]
        rows[...] = got[:, 16 * s : 16 * s + 16, :].reshape(512, 128).astype(F32)
        to_pieces(rows, pc)
        total[...] = own[s]
        for d in OFFSETS:
            for at, first, size, stride in voxel_runs(d):
                where = run(first, size, stride)
                total[where, :] = total[where, :] + pc[pl.ds(PIECE[d] + at, size), :]
        out[s] = (total[...].T + gout[s].astype(F32) * live).astype(BF)


def assemble_kernel(flip, core, line, *refs):
    parts, (conv, up, down, held, sems) = refs[:4], refs[-5:]
    half = core[0] ^ flip

    def moves(n, first):
        def copy(src, dst, k):
            return pltpu.make_async_copy(src, dst, sems.at[n, k])

        block = held.at[n]
        return (
            (first < 24, lambda: [copy(block, conv.at[pl.ds(first, 4)], 0)]),
            (
                first == 24,
                lambda: [
                    copy(block.at[0:3], conv.at[pl.ds(24, 3)], 0),
                    copy(block.at[3], up.at[:, pl.ds(0, 128)], 1),
                ],
            ),
            (
                first == 28,
                lambda: [
                    copy(block.at[0], up.at[:, pl.ds(128, 128)], 0),
                    copy(block.at[1], down.at[pl.ds(0, 128), :], 1),
                    copy(block.at[2], down.at[pl.ds(128, 128), :], 2),
                ],
            ),
        )

    firsts = [half * 16 + ((line[0] + n) & 3) * 4 for n in range(4)]
    for n, part in enumerate(parts):
        held[n] = part[...].astype(F32).reshape(4, 128, 128)
        for when, copies in moves(n, firsts[n]):

            @pl.when(when)
            def _():
                for copy in copies():
                    copy.start()

    for n in range(4):
        for when, copies in moves(n, firsts[n]):

            @pl.when(when)
            def _():
                for copy in copies():
                    copy.wait()


VM = pl.BlockSpec(memory_space=pltpu.VMEM)
SM = pl.BlockSpec(memory_space=pltpu.SMEM)


HB = pl.BlockSpec(memory_space=pltpu.HBM)


def call(
    kernel, shapes, scalars, arrays, scratch=(), flops=1e6, limit=24, ins=None, outs=None,
    alias=None, name=None,
):
    moved = sum(x.size * x.dtype.itemsize for x in arrays)
    moved += sum(int(np.prod(s.shape)) * s.dtype.itemsize for s in shapes)
    return pl.pallas_call(
        kernel,
        out_shape=shapes,
        in_specs=[SM] * len(scalars) + (ins or [VM] * len(arrays)),
        out_specs=outs or [VM] * len(shapes),
        input_output_aliases=alias or {},
        scratch_shapes=list(scratch),
        compiler_params=pltpu.CompilerParams(vmem_limit_bytes=limit * 2**20),
        cost_estimate=pl.CostEstimate(
            flops=int(flops), bytes_accessed=int(moved), transcendentals=0
        ),
        name=name,
    )(*scalars, *arrays)


def shape(dims, dtype):
    return jax.ShapeDtypeStruct(dims, dtype)


def on_device(
    features,
    grad_out,
    conv_weight,
    coarse_up,
    coarse_down,
    counts,
    neighbour_owner,
    neighbour_slot,
    parent,
    child_slot,
):
    grp = lax.axis_index("grp").astype(jnp.int32)
    core = (grp & 1).reshape(1)
    line = (grp >> 1).reshape(1)
    swap = [(i, i ^ 1) for i in range(8)]
    msg, flags = call(
        ask_kernel,
        [shape((32, 32, 128), BF), shape((8, 128), F32)],
        [],
        [counts, features, neighbour_owner, neighbour_slot, jnp.asarray(choice_table(), BF)],
        [
            pltpu.SMEM((1,), jnp.int32),
            pltpu.VMEM((2, 128, 512), BF),
            pltpu.VMEM((2, 26), jnp.int32),
            pltpu.VMEM((2, 26), jnp.int32),
            pltpu.VMEM((128, 1024), BF),
            pltpu.VMEM((16, 128), F32),
            pltpu.VMEM((2, 8, 128), F32),
            pltpu.VMEM((2, 512, 128), F32),
            pltpu.VMEM((2, 512, 128), F32),
            pltpu.VMEM((2, 512, 128), F32),
            pltpu.VMEM((32, 32, 128), BF),
            pltpu.VMEM((8, 128), F32),
            pltpu.SemaphoreType.DMA((9,)),
        ],
        flops=2e6,
        limit=60,
        ins=[HB] * 4 + [pl.BlockSpec(memory_space=pl.ANY)],
        outs=[HB] * 2,
        name="ask",
    )
    first = lax.all_to_all(msg, "dev", split_axis=0, concat_axis=0, tiled=True)
    answer, table = call(
        route_kernel,
        [shape((32, 32, 128), BF), shape((2, 16, 512), BF)],
        [],
        [first],
        [pltpu.VMEM((1024, 1024), BF)],
        flops=3e8,
        name="route",
    )
    halo = lax.all_to_all(answer, "dev", split_axis=0, concat_axis=0, tiled=True)
    weight = conv_weight.reshape(3, 1152, 128)
    output, grad_pre, wsum, send = call(
        forward_kernel,
        [
            shape((2, 128, 512), BF),
            shape((2, 128, 512), BF),
            shape((4096, 128), BF),
            shape((2048, 128), BF),
        ],
        [parent, child_slot, core],
        [flags, features, halo, grad_out, weight, coarse_up, coarse_down],
        [
            pltpu.VMEM((2, 512, 128), F32),
            pltpu.VMEM((2, 512, 128), F32),
            pltpu.VMEM((2, 512, 128), F32),
            pltpu.VMEM((2, 800, 128), F32),
            pltpu.VMEM((2, 816, 128), F32),
            pltpu.VMEM((2, 800, 128), F32),
            pltpu.VMEM((1280, 1152), BF),
            pltpu.VMEM((2, 16, 128), F32),
            pltpu.VMEM((2, 16, 128), F32),
            pltpu.VMEM((2, 128, 512), BF),
            pltpu.SemaphoreType.DMA((1,)),
        ],
        flops=2e9,
        outs=[HB, VM, VM, VM],
        name="forward",
    )
    other = lax.ppermute(send, "grp", swap)
    own_sum, *away = call(
        pair_kernel,
        [shape((512, 128), F32)] + [shape((512, 128), BF)] * 3,
        [core, line],
        [wsum, other],
        name="pair",
    )
    away = [
        lax.ppermute(away[step - 1], "grp", [(i, (i + 2 * step) % 8) for i in range(8)])
        for step in (2, 1, 3)
    ]
    grad_pre, own_sum = lax.optimization_barrier((grad_pre, own_sum))
    own, terms = call(
        backward_kernel,
        [shape((2, 512, 128), F32), shape((32, 32, 128), BF)],
        [],
        [grad_pre, weight],
        [
            pltpu.VMEM((2, 640, 384), BF),
            pltpu.VMEM((1152, 384), BF),
            pltpu.VMEM((2, 3, 816, 128), F32),
            pltpu.VMEM((2, 512, 128), F32),
            pltpu.VMEM((2, 512, 128), F32),
        ],
        flops=4e9,
        name="backward",
    )
    (terms,) = call(
        join_kernel, [shape((32, 48, 128), BF)], [], [terms, own_sum, *away], name="join"
    )
    terms = lax.all_to_all(terms, "dev", split_axis=0, concat_axis=0, tiled=True)
    (sums,) = call(
        merge_kernel,
        [shape((32, 48, 128), BF)],
        [],
        [terms, table],
        [pltpu.VMEM((2, 1024, 512), BF)],
        flops=3e8,
        name="merge",
    )
    back = lax.all_to_all(sums, "dev", split_axis=0, concat_axis=0, tiled=True)
    chunk = back[:, 32:48, :].reshape(512, 128)
    parts = {
        step: lax.ppermute(chunk, "grp", [(i, (i - 2 * step) % 8) for i in range(8)])
        for step in (2, 1, 3)
    }
    (grad_features,) = call(
        finish_kernel,
        [shape((2, 128, 512), BF)],
        [],
        [flags, back, own, grad_out],
        [pltpu.VMEM((512, 128), F32)] * 3,
        flops=3e8,
        name="finish",
    )
    parts, grad_features = lax.optimization_barrier((parts, grad_features))
    mine = [chunk, parts[1], parts[2], parts[3]]
    others = [lax.ppermute(x, "grp", swap) for x in mine]

    def assemble(flip, pieces, held):
        return call(
            functools.partial(assemble_kernel, flip),
            [shape((27, 128, 128), F32), shape((128, 256), F32), shape((256, 128), F32)],
            [core, line],
            pieces + held,
            [pltpu.VMEM((4, 4, 128, 128), F32), pltpu.SemaphoreType.DMA((4, 3))],
            ins=[VM] * 4 + [HB] * len(held),
            outs=[HB] * 3,
            alias={6 + n: n for n in range(len(held))},
            name="assemble",
        )

    grad_conv, grad_up, grad_down = assemble(1, others, list(assemble(0, mine, [])))
    return (output, grad_features, grad_conv, grad_up, grad_down)


def solution(mesh):
    return jax.shard_map(
        on_device,
        mesh=mesh,
        in_specs=(
            P(("grp", "dev"), None, None),
            P(("grp", "dev"), None, None),
            P(),
            P(),
            P(),
            P(("grp", "dev")),
            P(("grp", "dev"), None),
            P(("grp", "dev"), None),
            P(("grp", "dev")),
            P(("grp", "dev")),
        ),
        out_specs=(P(("grp", "dev"), None, None), P(("grp", "dev"), None, None), P(), P(), P()),
        check_vma=False,
    )
```

```python
import functools

import jax
import jax.numpy as jnp
import numpy as np
from jax import lax
from jax.experimental import pallas as pl
from jax.experimental.pallas import tpu as pltpu
from jax.sharding import PartitionSpec as P

BF = jnp.bfloat16
F32 = jnp.float32

OFFSETS = [
    (a, b, c) for a in (-1, 0, 1) for b in (-1, 0, 1) for c in (-1, 0, 1) if (a, b, c) != (0, 0, 0)
]
FACES = [d for d in OFFSETS if sum(map(abs, d)) == 1]
EDGES = [d for d in OFFSETS if sum(map(abs, d)) == 2]
CORNERS = [d for d in OFFSETS if sum(map(abs, d)) == 3]
PIECE = {d: 64 * n for n, d in enumerate(FACES)}
PIECE.update({d: 384 + 8 * n for n, d in enumerate(EDGES)})
PIECE.update({d: 480 + n for n, d in enumerate(CORNERS)})


def voxel_runs(d):
    a, b, c = (7 if x < 0 else 0 for x in d)
    free = [x == 0 for x in d]
    if free == [True, True, False]:
        return [(0, c, 64, 8)]
    if free == [True, False, True]:
        return [(8 * x, x * 64 + b * 8, 8, 1) for x in range(8)]
    if free == [False, True, True]:
        return [(0, a * 64, 64, 1)]
    size = 8 if any(free) else 1
    stride = (64 if free[0] else 1) * (8 if free[1] else 1)
    return [(0, a * 64 + b * 8 + c, size, stride)]


def run(start, size, stride):
    return pl.ds(start, size) if stride == 1 else pl.ds(start, size, stride=stride)


SHARES = [((64 * f + p, 32, 2), (2 * f + p, 32, 16)) for f in range(6) for p in range(2)]
SHARES += [((384 + 32 * m, 32, 1), (12 + m, 32, 16)) for m in range(3)]


def share_directions(group):
    edges = [EDGES[4 * m + group // 2] for m in range(3)]
    return [OFFSETS.index(d) for d in [FACES[q // 2] for q in range(12)] + edges + [CORNERS[group]]]


def choice_table():
    table = np.zeros((128, 8, 128), np.float32)
    for group in range(8):
        for q, direction in enumerate(share_directions(group)):
            table[direction, group, 32 + q] = 1
    return table.reshape(128, 1024)


def few_lanes(rows):
    return lax.broadcasted_iota(jnp.int32, (rows, 128), 1) < 32


def to_pieces(rows, pieces):
    for there, here in SHARES:
        pieces[run(*there), :] = rows[run(*here), :]
    total = jnp.zeros((8, 128), F32)
    for n in range(4):
        part = jnp.where(few_lanes(8), rows[pl.ds(15 + 16 * n, 8, stride=64), :], 0.0)
        total = total + (pltpu.roll(part, 32 * n, 1) if n else part)
    pieces[pl.ds(480, 8), :] = total


def to_shares(pieces, rows, extra=None):
    for there, here in SHARES:
        rows[run(*here), :] = pieces[run(*there), :]
    for n in range(4):
        part = pieces[pl.ds(480, 8), :]
        part = pltpu.roll(part, 128 - 32 * n, 1) if n else part
        if extra is not None:
            part = jnp.where(few_lanes(8), part, extra)
        rows[pl.ds(15 + 16 * n, 8, stride=64), :] = part


def nn(x, y):
    return lax.dot_general(x, y, (((1,), (0,)), ((), ())), preferred_element_type=F32)


def nt(x, y):
    return lax.dot_general(x, y, (((1,), (1,)), ((), ())), preferred_element_type=F32)


def identity():
    rows = lax.broadcasted_iota(jnp.int32, (128, 128), 0)
    lanes = lax.broadcasted_iota(jnp.int32, (128, 128), 1)
    return (rows == lanes).astype(F32).astype(BF)


def pool_rows(s):
    rows = lax.broadcasted_iota(jnp.int32, (16, 512), 0) - 8 * s
    lanes = lax.broadcasted_iota(jnp.int32, (16, 512), 1)
    block = ((lanes >> 8) & 1) * 4 + ((lanes >> 5) & 1) * 2 + ((lanes >> 2) & 1)
    return (rows == block).astype(F32).astype(BF)


def pool_voxels(values, sums, first):
    for a in range(2):
        planes = values[a * 256 : a * 256 + 64]
        for n in range(1, 4):
            planes = planes + values[a * 256 + n * 64 : a * 256 + n * 64 + 64]
        for b in range(2):
            line = planes[b * 32 : b * 32 + 8]
            for n in range(1, 4):
                line = line + planes[b * 32 + n * 8 : b * 32 + n * 8 + 8]
            for c in range(2):
                at = first + 4 * a + 2 * b + c
                sums[at : at + 1, :] = jnp.sum(line[4 * c : 4 * c + 4], axis=0, keepdims=True)


def ask_kernel(
    feat, owner, slot, choice, msg,
    feat_v, owner_v, slot_v, choice_v, bricks, tables, voxels, pc, rows, msg_v, sems,
):
    pairs = (
        (owner, owner_v), (slot, slot_v), (choice, choice_v),
        (feat.at[0], feat_v.at[0]), (feat.at[1], feat_v.at[1]),
    )
    copies = [
        pltpu.make_async_copy(src, dst, sems.at[n]) for n, (src, dst) in enumerate(pairs)
    ]
    for copy in copies:
        copy.start()
    bricks[...] = jnp.zeros((16, 128), F32)
    for copy in copies[:3]:
        copy.wait()
    named = jnp.where(owner_v[...] >= 0, owner_v[...] * 2 + slot_v[...], -1)
    bricks[0:2, 0:26] = named.astype(F32)
    asked = nn(bricks[...].astype(BF), choice_v[...])
    for group in range(8):
        for s in range(2):
            tables[s, group : group + 1, :] = asked[s : s + 1, group * 128 : group * 128 + 128]
    sent = []
    for s in range(2):
        copies[3 + s].wait()
        voxels[s] = feat_v[s].astype(F32).T
        for d in OFFSETS:
            for at, first, size, stride in voxel_runs(d):
                pc[s, pl.ds(PIECE[d] + at, size), :] = voxels.at[s][run(first, size, stride), :]
        to_shares(pc.at[s], rows.at[s], tables[s])
        at = pl.ds(16 * s, 16)
        msg_v[:, at, :] = rows[s].astype(BF).reshape(32, 16, 128)
        sent.append(pltpu.make_async_copy(msg_v.at[:, at, :], msg.at[:, at, :], sems.at[5 + s]))
        sent[-1].start()
    for copy in sent:
        copy.wait()


def same_part():
    rows = lax.broadcasted_iota(jnp.int32, (16, 128), 0)
    lanes = lax.broadcasted_iota(jnp.int32, (16, 128), 1) & 15
    return (rows == lanes).astype(F32).astype(BF)


def route_kernel(got, out, named, hot):
    same = jnp.broadcast_to(same_part()[None], (32, 16, 128))
    zero = jnp.zeros((32, 16, 128), BF)
    ones = jnp.ones((128, 128), BF)
    part = lax.broadcasted_iota(jnp.int32, (16, 128), 0)
    lanes = lax.broadcasted_iota(jnp.int32, (16, 128), 1)
    place = (lanes == part + 32)[None]
    for s in range(2):
        table = got[:, 16 * s : 16 * s + 16, :].astype(F32)[:, 15:16, :]
        table = jnp.where(place, jnp.broadcast_to(table, (32, 16, 128)), 0.0)
        asked = nn(table.astype(BF).reshape(512, 128), ones)
        named[s] = asked.T[0:16].astype(BF)
        asked = asked.astype(BF).reshape(32, 16, 128)
        for n in range(8):
            here = ((lanes >> 4) + 8 * n).astype(F32).astype(BF)
            picked = jnp.where(asked == here[None], same, zero)
            hot[s * 512 : s * 512 + 512, n * 128 : n * 128 + 128] = picked.reshape(512, 128)
    answer = nn(hot[...], got[...].reshape(1024, 128)).astype(BF)
    for s in range(2):
        out[:, 16 * s : 16 * s + 16, :] = answer[s * 512 : s * 512 + 512].reshape(32, 16, 128)


def forward_kernel(
    parent, child, core, flags, feat, got, gout, weight, up, down,
    out, grad_out_t, wsum, send,
    rows_all, pc_all, mine_all, s0_all, s1_all, s2_all, cols, pooled, grad_pooled, out_v, grad_t, sems,
):
    eye = identity()
    acts, slopes = [], []
    for s in range(2):
        rows, pc, mine, s0, s1, s2 = (
            x.at[s] for x in (rows_all, pc_all, mine_all, s0_all, s1_all, s2_all)
        )
        live = flags[s : s + 1, 0:1]
        pool = pool_rows(s)
        mine[...] = (feat[s].astype(F32) * live).T
        grad_pooled[s] = nt(pool, gout[s]) * live
        rows[...] = got[:, 16 * s : 16 * s + 16, :].reshape(512, 128).astype(F32)
        to_pieces(rows, pc)
        for a in range(8):
            s1[pl.ds(8 + ((a + 1) * 10 + 1) * 8, 64), :] = mine[a * 64 : a * 64 + 64, :]
            for d, b in (((0, -1, 0), 0), ((0, 1, 0), 9)):
                s1[pl.ds(8 + ((a + 1) * 10 + b) * 8, 8), :] = pc[pl.ds(PIECE[d] + 8 * a, 8), :]
        for a, x in ((-1, 0), (1, 9)):
            s1[pl.ds(8 + (x * 10 + 1) * 8, 64), :] = pc[pl.ds(PIECE[a, 0, 0], 64), :]
            for b, y in ((-1, 0), (1, 9)):
                s1[pl.ds(8 + (x * 10 + y) * 8, 8), :] = pc[pl.ds(PIECE[a, b, 0], 8), :]
        s0[...] = s1[pl.ds(7, 800), :]
        s2[...] = s1[pl.ds(9, 800), :]
        for c, ref, lane in ((-1, s0, 0), (1, s2, 7)):
            for a in range(8):
                ref[pl.ds(((a + 1) * 10 + 1) * 8 + lane, 8, stride=8), :] = pc[
                    pl.ds(PIECE[0, 0, c] + 8 * a, 8), :
                ]
            for a, x in ((-1, 0), (1, 9)):
                ref[pl.ds((x * 10 + 1) * 8 + lane, 8, stride=8), :] = pc[
                    pl.ds(PIECE[a, 0, c], 8), :
                ]
                ref[pl.ds((10 + x) * 8 + lane, 8, stride=80), :] = pc[pl.ds(PIECE[0, a, c], 8), :]
                for b, y in ((-1, 0), (1, 9)):
                    ref[pl.ds((x * 10 + y) * 8 + lane, 1), :] = pc[pl.ds(PIECE[a, b, c], 1), :]
        for a in range(10):
            for b in range(3):
                for c, ref in enumerate((s0, s1, s2)):
                    start = (a * 10 + b) * 8 + (8 if c == 1 else 0)
                    at = 640 * s + 64 * a
                    cols[at : at + 64, (3 * b + c) * 128 : (3 * b + c) * 128 + 128] = ref[
                        pl.ds(start, 64), :
                    ].astype(BF)
        taps = nn(cols[640 * s : 640 * s + 640, :], weight[...])
        pre = taps[0:512, 0:128] + taps[64:576, 128:256] + taps[128:640, 256:384]
        pool_voxels(pre * (1.0 / (1.0 + jnp.exp(-pre))), pooled, 8 * s)
        pre = pre.T
        gate = 1.0 / (1.0 + jnp.exp(-pre))
        acts.append(pre * gate)
        slopes.append(gate * (1.0 + pre * (1.0 - gate)))
    second = lax.broadcasted_iota(jnp.int32, (16, 1), 0) >= 8
    valid = [
        ((parent[s] >= 0) & (parent[s] * 64 + child[s] >= 0)).astype(F32) * flags[s : s + 1, 0:1]
        for s in range(2)
    ]
    valid = jnp.where(second, valid[1], valid[0])
    coarse_in = (pooled[...] * (1.0 / 64.0) * valid).astype(BF)
    grad_out = ((grad_pooled[0] + grad_pooled[1]) * valid).astype(BF)
    coarse_pre = nn(coarse_in, up[...])
    gate = 1.0 / (1.0 + jnp.exp(-coarse_pre))
    coarse_mid = (coarse_pre * gate).astype(BF)
    grad_pre = nt(grad_out, down[...]) * (gate * (1.0 + coarse_pre * (1.0 - gate)))
    grad_pre = grad_pre.astype(BF)
    coarse_out = nn(coarse_mid, down[...]).astype(BF)
    grad_cin = nt(grad_pre, up[...]).astype(BF)
    lift = nt(eye, coarse_out).astype(BF)
    back = nt(eye, grad_cin).astype(BF)
    for s in range(2):
        live = flags[s : s + 1, 0:1]
        pool = pool_rows(s)
        grad_in = gout[s].astype(F32) * live + nn(back, pool) * (1.0 / 64.0)
        grad_t[s] = (grad_in * slopes[s]).astype(BF)
        out_v[s] = (feat[s].astype(F32) * live + acts[s] + nn(lift, pool)).astype(BF)
    copies = [
        pltpu.make_async_copy(grad_t, grad_out_t, sems.at[0]),
        pltpu.make_async_copy(out_v, out, sems.at[1]),
    ]
    for copy in copies:
        copy.start()

    def put(block, value):
        wsum[pl.ds(block * 128, 128), :] = value.astype(BF)

    grad_up = nn(nt(eye, coarse_in).astype(BF), grad_pre)
    for h in range(2):
        put(27 + h, grad_up[:, h * 128 : h * 128 + 128])
        middle = nt(eye, coarse_mid[:, h * 128 : h * 128 + 128]).astype(BF)
        put(29 + h, nn(middle, grad_out))
    put(31, jnp.zeros((128, 128), F32))
    for a in range(3):
        total = nn(grad_t[0], cols[64 * a : 64 * a + 512, :])
        total = total + nn(grad_t[1], cols[64 * a + 640 : 64 * a + 1152, :])
        for n in range(9):
            put(9 * a + n, total[:, n * 128 : n * 128 + 128].T)
    send[...] = wsum[pl.ds(pl.multiple_of((1 - core[0]) * 2048, 2048), 2048), :]
    for copy in copies:
        copy.wait()


def pair_kernel(core, line, wsum, other, own, one, two, three):
    for step, ref in enumerate((own, one, two, three)):
        at = pl.multiple_of(((line[0] + step) & 3) * 512, 512)
        kept = wsum[pl.ds(pl.multiple_of(core[0] * 2048 + at, 512), 512), :].astype(F32)
        ref[...] = (kept + other[pl.ds(at, 512), :].astype(F32)).astype(ref.dtype)


def backward_kernel(grad, weight, own, msg, lhs, acc_all, pc_all, rows_all, grad_t, sem):
    copy = pltpu.make_async_copy(grad, grad_t, sem.at[0])
    copy.start()
    zero = jnp.zeros((64, 128), BF)
    for a in range(3):
        for n in [*range(a), *range(8 + a, 10)]:
            for s in range(2):
                lhs[s, n * 64 : n * 64 + 64, a * 128 : a * 128 + 128] = zero
    copy.wait()
    low = (lax.broadcasted_iota(jnp.int32, (64, 1), 0) & 7) != 0
    high = (lax.broadcasted_iota(jnp.int32, (64, 1), 0) & 7) != 7

    for s in range(2):
        acc, pc, rows = acc_all.at[s], pc_all.at[s], rows_all.at[s]
        values = grad_t[s].astype(F32).T.astype(BF)
        for a in range(3):
            lhs[s, a * 64 : a * 64 + 512, a * 128 : a * 128 + 128] = values
        acc[...] = jnp.zeros_like(acc)
        for b in range(3):
            part = nt(lhs[s], weight[b * 384 : b * 384 + 384, :])
            for c in range(3):
                for a in range(10):
                    at = pl.ds(8 + (a * 10 + b) * 8, 64)
                    acc[c, at, :] += part[a * 64 : a * 64 + 64, c * 128 : c * 128 + 128]

        def middle(row, size):
            at = 8 + row
            total = acc[1, pl.ds(at, size), :]
            total = total + jnp.where(high[:size], acc[0, pl.ds(at + 1, size), :], 0.0)
            return total + jnp.where(low[:size], acc[2, pl.ds(at - 1, size), :], 0.0)

        for a in range(8):
            own[s, pl.ds(a * 64, 64), :] = middle(((a + 1) * 10 + 1) * 8, 64)
            for d, b in (((0, -1, 0), 0), ((0, 1, 0), 9)):
                pc[pl.ds(PIECE[d] + 8 * a, 8), :] = middle(((a + 1) * 10 + b) * 8, 8)
        for a, x in ((-1, 0), (1, 9)):
            pc[pl.ds(PIECE[a, 0, 0], 64), :] = middle((x * 10 + 1) * 8, 64)
            for b, y in ((-1, 0), (1, 9)):
                pc[pl.ds(PIECE[a, b, 0], 8), :] = middle((x * 10 + y) * 8, 8)
        for c, ref, lane in ((-1, acc.at[0], 8), (1, acc.at[2], 15)):
            for a in range(8):
                pc[pl.ds(PIECE[0, 0, c] + 8 * a, 8), :] = ref[
                    pl.ds(((a + 1) * 10 + 1) * 8 + lane, 8, stride=8), :
                ]
            for a, x in ((-1, 0), (1, 9)):
                pc[pl.ds(PIECE[a, 0, c], 8), :] = ref[pl.ds((x * 10 + 1) * 8 + lane, 8, stride=8), :]
                pc[pl.ds(PIECE[0, a, c], 8), :] = ref[pl.ds((10 + x) * 8 + lane, 8, stride=80), :]
                for b, y in ((-1, 0), (1, 9)):
                    pc[pl.ds(PIECE[a, b, c], 1), :] = ref[pl.ds((x * 10 + y) * 8 + lane, 1), :]
        to_shares(pc, rows)
        msg[:, 16 * s : 16 * s + 16, :] = rows[...].astype(BF).reshape(32, 16, 128)


def join_kernel(terms, own, away1, away2, away3, msg):
    msg[:, 0:32, :] = terms[...]
    total = own[...] + away1[...].astype(F32) + away2[...].astype(F32) + away3[...].astype(F32)
    msg[:, 32:48, :] = total.astype(BF).reshape(32, 16, 128)


def merge_kernel(got, named, out, hot):
    same = same_part()
    zero = jnp.zeros((16, 128), BF)
    share = jnp.sum(got[:, 32:48, :].astype(F32), axis=0).astype(BF)
    out[:, 32:48, :] = jnp.broadcast_to(share[None], (32, 16, 128))
    total = jnp.zeros((1024, 128), F32)
    for s in range(2):
        for n in range(4):
            asked = named[s, :, n * 128 : n * 128 + 128]
            for brick in range(64):
                hot[s, brick * 16 : brick * 16 + 16, n * 128 : n * 128 + 128] = jnp.where(
                    asked == jnp.full((16, 128), brick, BF), same, zero
                )
        total = total + nn(hot[s], got[:, 16 * s : 16 * s + 16, :].reshape(512, 128))
    out[:, 0:32, :] = total.astype(BF).reshape(32, 32, 128)


def finish_kernel(flags, got, own, gout, out, rows, pc, total):
    for s in range(2):
        live = flags[s : s + 1, 0:1]
        rows[...] = got[:, 16 * s : 16 * s + 16, :].reshape(512, 128).astype(F32)
        to_pieces(rows, pc)
        total[...] = own[s]
        for d in OFFSETS:
            for at, first, size, stride in voxel_runs(d):
                where = run(first, size, stride)
                total[where, :] = total[where, :] + pc[pl.ds(PIECE[d] + at, size), :]
        out[s] = (total[...].T + gout[s].astype(F32) * live).astype(BF)


def assemble_kernel(flip, core, line, *refs):
    parts, (conv, up, down, held, sems) = refs[:4], refs[-5:]
    half = core[0] ^ flip

    def moves(n, first):
        def copy(src, dst, k):
            return pltpu.make_async_copy(src, dst, sems.at[n, k])

        block = held.at[n]
        return (
            (first < 24, lambda: [copy(block, conv.at[pl.ds(first, 4)], 0)]),
            (
                first == 24,
                lambda: [
                    copy(block.at[0:3], conv.at[pl.ds(24, 3)], 0),
                    copy(block.at[3], up.at[:, pl.ds(0, 128)], 1),
                ],
            ),
            (
                first == 28,
                lambda: [
                    copy(block.at[0], up.at[:, pl.ds(128, 128)], 0),
                    copy(block.at[1], down.at[pl.ds(0, 128), :], 1),
                    copy(block.at[2], down.at[pl.ds(128, 128), :], 2),
                ],
            ),
        )

    firsts = [half * 16 + ((line[0] + n) & 3) * 4 for n in range(4)]
    for n, part in enumerate(parts):
        held[n] = part[...].astype(F32).reshape(4, 128, 128)
        for when, copies in moves(n, firsts[n]):

            @pl.when(when)
            def _():
                for copy in copies():
                    copy.start()

    for n in range(4):
        for when, copies in moves(n, firsts[n]):

            @pl.when(when)
            def _():
                for copy in copies():
                    copy.wait()


VM = pl.BlockSpec(memory_space=pltpu.VMEM)
SM = pl.BlockSpec(memory_space=pltpu.SMEM)


HB = pl.BlockSpec(memory_space=pltpu.HBM)


def call(
    kernel, shapes, scalars, arrays, scratch=(), flops=1e6, limit=24, ins=None, outs=None,
    alias=None, name=None,
):
    moved = sum(x.size * x.dtype.itemsize for x in arrays)
    moved += sum(int(np.prod(s.shape)) * s.dtype.itemsize for s in shapes)
    return pl.pallas_call(
        kernel,
        out_shape=shapes,
        in_specs=[SM] * len(scalars) + (ins or [VM] * len(arrays)),
        out_specs=outs or [VM] * len(shapes),
        input_output_aliases=alias or {},
        scratch_shapes=list(scratch),
        compiler_params=pltpu.CompilerParams(vmem_limit_bytes=limit * 2**20),
        cost_estimate=pl.CostEstimate(
            flops=int(flops), bytes_accessed=int(moved), transcendentals=0
        ),
        name=name,
    )(*scalars, *arrays)


def shape(dims, dtype):
    return jax.ShapeDtypeStruct(dims, dtype)


def on_device(
    features,
    grad_out,
    conv_weight,
    coarse_up,
    coarse_down,
    counts,
    neighbour_owner,
    neighbour_slot,
    parent,
    child_slot,
):
    grp = lax.axis_index("grp").astype(jnp.int32)
    core = (grp & 1).reshape(1)
    line = (grp >> 1).reshape(1)
    swap = [(i, i ^ 1) for i in range(8)]
    slots = lax.broadcasted_iota(jnp.int32, (8, 128), 0)
    flags = (slots < counts[0]).astype(F32)
    (msg,) = call(
        ask_kernel,
        [shape((32, 32, 128), BF)],
        [],
        [features, neighbour_owner, neighbour_slot, jnp.asarray(choice_table(), BF)],
        [
            pltpu.VMEM((2, 128, 512), BF),
            pltpu.VMEM((2, 26), jnp.int32),
            pltpu.VMEM((2, 26), jnp.int32),
            pltpu.VMEM((128, 1024), BF),
            pltpu.VMEM((16, 128), F32),
            pltpu.VMEM((2, 8, 128), F32),
            pltpu.VMEM((2, 512, 128), F32),
            pltpu.VMEM((2, 512, 128), F32),
            pltpu.VMEM((2, 512, 128), F32),
            pltpu.VMEM((32, 32, 128), BF),
            pltpu.SemaphoreType.DMA((7,)),
        ],
        flops=2e6,
        limit=60,
        ins=[HB] * 3 + [pl.BlockSpec(memory_space=pl.ANY)],
        outs=[HB],
        name="ask",
    )
    first = lax.all_to_all(msg, "dev", split_axis=0, concat_axis=0, tiled=True)
    answer, table = call(
        route_kernel,
        [shape((32, 32, 128), BF), shape((2, 16, 512), BF)],
        [],
        [first],
        [pltpu.VMEM((1024, 1024), BF)],
        flops=3e8,
        name="route",
    )
    halo = lax.all_to_all(answer, "dev", split_axis=0, concat_axis=0, tiled=True)
    weight = conv_weight.reshape(3, 1152, 128)
    weight = jnp.concatenate([weight[0], weight[1], weight[2]], axis=1)
    output, grad_pre, wsum, send = call(
        forward_kernel,
        [
            shape((2, 128, 512), BF),
            shape((2, 128, 512), BF),
            shape((4096, 128), BF),
            shape((2048, 128), BF),
        ],
        [parent, child_slot, core],
        [flags, features, halo, grad_out, weight, coarse_up, coarse_down],
        [
            pltpu.VMEM((2, 512, 128), F32),
            pltpu.VMEM((2, 512, 128), F32),
            pltpu.VMEM((2, 512, 128), F32),
            pltpu.VMEM((2, 800, 128), F32),
            pltpu.VMEM((2, 816, 128), F32),
            pltpu.VMEM((2, 800, 128), F32),
            pltpu.VMEM((1280, 1152), BF),
            pltpu.VMEM((16, 128), F32),
            pltpu.VMEM((2, 16, 128), F32),
            pltpu.VMEM((2, 128, 512), BF),
            pltpu.VMEM((2, 128, 512), BF),
            pltpu.SemaphoreType.DMA((2,)),
        ],
        flops=2e9,
        outs=[HB, HB, VM, VM],
        name="forward",
    )
    other = lax.ppermute(send, "grp", swap)
    own_sum, *away = call(
        pair_kernel,
        [shape((512, 128), F32)] + [shape((512, 128), BF)] * 3,
        [core, line],
        [wsum, other],
        name="pair",
    )
    away = [
        lax.ppermute(away[step - 1], "grp", [(i, (i + 2 * step) % 8) for i in range(8)])
        for step in (2, 1, 3)
    ]
    grad_pre, own_sum = lax.optimization_barrier((grad_pre, own_sum))
    own, terms = call(
        backward_kernel,
        [shape((2, 512, 128), F32), shape((32, 32, 128), BF)],
        [],
        [grad_pre, weight],
        [
            pltpu.VMEM((2, 640, 384), BF),
            pltpu.VMEM((2, 3, 816, 128), F32),
            pltpu.VMEM((2, 512, 128), F32),
            pltpu.VMEM((2, 512, 128), F32),
            pltpu.VMEM((2, 128, 512), BF),
            pltpu.SemaphoreType.DMA((1,)),
        ],
        flops=4e9,
        ins=[HB, VM],
        name="backward",
    )
    (terms,) = call(
        join_kernel, [shape((32, 48, 128), BF)], [], [terms, own_sum, *away], name="join"
    )
    terms = lax.all_to_all(terms, "dev", split_axis=0, concat_axis=0, tiled=True)
    (sums,) = call(
        merge_kernel,
        [shape((32, 48, 128), BF)],
        [],
        [terms, table],
        [pltpu.VMEM((2, 1024, 512), BF)],
        flops=3e8,
        name="merge",
    )
    back = lax.all_to_all(sums, "dev", split_axis=0, concat_axis=0, tiled=True)
    chunk = back[:, 32:48, :].reshape(512, 128)
    parts = {
        step: lax.ppermute(chunk, "grp", [(i, (i - 2 * step) % 8) for i in range(8)])
        for step in (2, 1, 3)
    }
    (grad_features,) = call(
        finish_kernel,
        [shape((2, 128, 512), BF)],
        [],
        [flags, back, own, grad_out],
        [pltpu.VMEM((512, 128), F32)] * 3,
        flops=3e8,
        name="finish",
    )
    parts, grad_features = lax.optimization_barrier((parts, grad_features))
    mine = [chunk, parts[1], parts[2], parts[3]]
    others = [lax.ppermute(x, "grp", swap) for x in mine]

    def assemble(flip, pieces, held):
        return call(
            functools.partial(assemble_kernel, flip),
            [shape((27, 128, 128), F32), shape((128, 256), F32), shape((256, 128), F32)],
            [core, line],
            pieces + held,
            [pltpu.VMEM((4, 4, 128, 128), F32), pltpu.SemaphoreType.DMA((4, 3))],
            ins=[VM] * 4 + [HB] * len(held),
            outs=[HB] * 3,
            alias={6 + n: n for n in range(len(held))},
            name="assemble",
        )

    grad_conv, grad_up, grad_down = assemble(1, others, list(assemble(0, mine, [])))
    return (output, grad_features, grad_conv, grad_up, grad_down)


def solution(mesh):
    return jax.shard_map(
        on_device,
        mesh=mesh,
        in_specs=(
            P(("grp", "dev"), None, None),
            P(("grp", "dev"), None, None),
            P(),
            P(),
            P(),
            P(("grp", "dev")),
            P(("grp", "dev"), None),
            P(("grp", "dev"), None),
            P(("grp", "dev")),
            P(("grp", "dev")),
        ),
        out_specs=(P(("grp", "dev"), None, None), P(("grp", "dev"), None, None), P(), P(), P()),
        check_vma=False,
    )
```

```python
import functools

import jax
import jax.numpy as jnp
import numpy as np
from jax import lax
from jax.experimental import pallas as pl
from jax.experimental.pallas import tpu as pltpu
from jax.sharding import PartitionSpec as P

BF = jnp.bfloat16
F32 = jnp.float32

OFFSETS = [
    (a, b, c) for a in (-1, 0, 1) for b in (-1, 0, 1) for c in (-1, 0, 1) if (a, b, c) != (0, 0, 0)
]
FACES = [d for d in OFFSETS if sum(map(abs, d)) == 1]
EDGES = [d for d in OFFSETS if sum(map(abs, d)) == 2]
CORNERS = [d for d in OFFSETS if sum(map(abs, d)) == 3]
PIECE = {d: 64 * n for n, d in enumerate(FACES)}
PIECE.update({d: 384 + 8 * n for n, d in enumerate(EDGES)})
PIECE.update({d: 480 + n for n, d in enumerate(CORNERS)})


def voxel_runs(d):
    a, b, c = (7 if x < 0 else 0 for x in d)
    free = [x == 0 for x in d]
    if free == [True, True, False]:
        return [(0, c, 64, 8)]
    if free == [True, False, True]:
        return [(8 * x, x * 64 + b * 8, 8, 1) for x in range(8)]
    if free == [False, True, True]:
        return [(0, a * 64, 64, 1)]
    size = 8 if any(free) else 1
    stride = (64 if free[0] else 1) * (8 if free[1] else 1)
    return [(0, a * 64 + b * 8 + c, size, stride)]


def run(start, size, stride):
    return pl.ds(start, size) if stride == 1 else pl.ds(start, size, stride=stride)


SHARES = [((64 * f + p, 32, 2), (2 * f + p, 32, 16)) for f in range(6) for p in range(2)]
SHARES += [((384 + 32 * m, 32, 1), (12 + m, 32, 16)) for m in range(3)]


def share_directions(group):
    edges = [EDGES[4 * m + group // 2] for m in range(3)]
    return [OFFSETS.index(d) for d in [FACES[q // 2] for q in range(12)] + edges + [CORNERS[group]]]


def choice_table():
    table = np.zeros((128, 8, 128), np.float32)
    for group in range(8):
        for q, direction in enumerate(share_directions(group)):
            table[direction, group, 32 + q] = 1
    return table.reshape(128, 1024)


def few_lanes(rows):
    return lax.broadcasted_iota(jnp.int32, (rows, 128), 1) < 32


def to_pieces(rows, pieces):
    for there, here in SHARES:
        pieces[run(*there), :] = rows[run(*here), :]
    total = jnp.zeros((8, 128), F32)
    for n in range(4):
        part = jnp.where(few_lanes(8), rows[pl.ds(15 + 16 * n, 8, stride=64), :], 0.0)
        total = total + (pltpu.roll(part, 32 * n, 1) if n else part)
    pieces[pl.ds(480, 8), :] = total


def to_shares(pieces, rows, extra=None):
    for there, here in SHARES:
        rows[run(*here), :] = pieces[run(*there), :]
    for n in range(4):
        part = pieces[pl.ds(480, 8), :]
        part = pltpu.roll(part, 128 - 32 * n, 1) if n else part
        if extra is not None:
            part = jnp.where(few_lanes(8), part, extra)
        rows[pl.ds(15 + 16 * n, 8, stride=64), :] = part


def nn(x, y):
    return lax.dot_general(x, y, (((1,), (0,)), ((), ())), preferred_element_type=F32)


def nt(x, y):
    return lax.dot_general(x, y, (((1,), (1,)), ((), ())), preferred_element_type=F32)


def identity():
    rows = lax.broadcasted_iota(jnp.int32, (128, 128), 0)
    lanes = lax.broadcasted_iota(jnp.int32, (128, 128), 1)
    return (rows == lanes).astype(F32).astype(BF)


def pool_rows(s):
    rows = lax.broadcasted_iota(jnp.int32, (16, 512), 0) - 8 * s
    lanes = lax.broadcasted_iota(jnp.int32, (16, 512), 1)
    block = ((lanes >> 8) & 1) * 4 + ((lanes >> 5) & 1) * 2 + ((lanes >> 2) & 1)
    return (rows == block).astype(F32).astype(BF)


def pool_voxels(values, sums, first):
    for a in range(2):
        planes = values[a * 256 : a * 256 + 64]
        for n in range(1, 4):
            planes = planes + values[a * 256 + n * 64 : a * 256 + n * 64 + 64]
        for b in range(2):
            line = planes[b * 32 : b * 32 + 8]
            for n in range(1, 4):
                line = line + planes[b * 32 + n * 8 : b * 32 + n * 8 + 8]
            for c in range(2):
                at = first + 4 * a + 2 * b + c
                sums[at : at + 1, :] = jnp.sum(line[4 * c : 4 * c + 4], axis=0, keepdims=True)


def ask_kernel(
    feat, owner, slot, choice, msg,
    feat_v, owner_v, slot_v, choice_v, bricks, tables, voxels, pc, rows, msg_v, sems,
):
    pairs = (
        (owner, owner_v), (slot, slot_v), (choice, choice_v),
        (feat.at[0], feat_v.at[0]), (feat.at[1], feat_v.at[1]),
    )
    copies = [
        pltpu.make_async_copy(src, dst, sems.at[n]) for n, (src, dst) in enumerate(pairs)
    ]
    for copy in copies:
        copy.start()
    bricks[...] = jnp.zeros((16, 128), F32)
    for copy in copies[:3]:
        copy.wait()
    named = jnp.where(owner_v[...] >= 0, owner_v[...] * 2 + slot_v[...], -1)
    bricks[0:2, 0:26] = named.astype(F32)
    asked = nn(bricks[...].astype(BF), choice_v[...])
    for group in range(8):
        for s in range(2):
            tables[s, group : group + 1, :] = asked[s : s + 1, group * 128 : group * 128 + 128]
    sent = []
    for s in range(2):
        copies[3 + s].wait()
        voxels[s] = feat_v[s].astype(F32).T
        for d in OFFSETS:
            for at, first, size, stride in voxel_runs(d):
                pc[s, pl.ds(PIECE[d] + at, size), :] = voxels.at[s][run(first, size, stride), :]
        to_shares(pc.at[s], rows.at[s], tables[s])
        at = pl.ds(16 * s, 16)
        msg_v[:, at, :] = rows[s].astype(BF).reshape(32, 16, 128)
        sent.append(pltpu.make_async_copy(msg_v.at[:, at, :], msg.at[:, at, :], sems.at[5 + s]))
        sent[-1].start()
    for copy in sent:
        copy.wait()


def same_part():
    rows = lax.broadcasted_iota(jnp.int32, (16, 128), 0)
    lanes = lax.broadcasted_iota(jnp.int32, (16, 128), 1) & 15
    return (rows == lanes).astype(F32).astype(BF)


def route_kernel(got, out, named, hot):
    same = jnp.broadcast_to(same_part()[None], (32, 16, 128))
    zero = jnp.zeros((32, 16, 128), BF)
    ones = jnp.ones((128, 128), BF)
    part = lax.broadcasted_iota(jnp.int32, (16, 128), 0)
    lanes = lax.broadcasted_iota(jnp.int32, (16, 128), 1)
    place = (lanes == part + 32)[None]
    for s in range(2):
        table = got[:, 16 * s : 16 * s + 16, :].astype(F32)[:, 15:16, :]
        table = jnp.where(place, jnp.broadcast_to(table, (32, 16, 128)), 0.0)
        asked = nn(table.astype(BF).reshape(512, 128), ones)
        named[s] = asked.T[0:16].astype(BF)
        asked = asked.astype(BF).reshape(32, 16, 128)
        for n in range(8):
            here = ((lanes >> 4) + 8 * n).astype(F32).astype(BF)
            picked = jnp.where(asked == here[None], same, zero)
            hot[s * 512 : s * 512 + 512, n * 128 : n * 128 + 128] = picked.reshape(512, 128)
    answer = nn(hot[...], got[...].reshape(1024, 128)).astype(BF)
    for s in range(2):
        out[:, 16 * s : 16 * s + 16, :] = answer[s * 512 : s * 512 + 512].reshape(32, 16, 128)


def forward_kernel(
    parent, child, core, flags, feat, got, gout, weight,
    out, grad_t, wsum, send,
    rows_all, pc_all, mine_all, s0_all, s1_all, s2_all, cols, pooled, grad_pooled, out_v, sem,
):
    eye = identity()
    up, down = weight[1152:1280, 0:256], weight[1152:1408, 256:384]
    acts, slopes = [], []
    for s in range(2):
        rows, pc, mine, s0, s1, s2 = (
            x.at[s] for x in (rows_all, pc_all, mine_all, s0_all, s1_all, s2_all)
        )
        live = flags[s : s + 1, 0:1]
        pool = pool_rows(s)
        mine[...] = (feat[s].astype(F32) * live).T
        grad_pooled[s] = nt(pool, gout[s]) * live
        rows[...] = got[:, 16 * s : 16 * s + 16, :].reshape(512, 128).astype(F32)
        to_pieces(rows, pc)
        for a in range(8):
            s1[pl.ds(8 + ((a + 1) * 10 + 1) * 8, 64), :] = mine[a * 64 : a * 64 + 64, :]
            for d, b in (((0, -1, 0), 0), ((0, 1, 0), 9)):
                s1[pl.ds(8 + ((a + 1) * 10 + b) * 8, 8), :] = pc[pl.ds(PIECE[d] + 8 * a, 8), :]
        for a, x in ((-1, 0), (1, 9)):
            s1[pl.ds(8 + (x * 10 + 1) * 8, 64), :] = pc[pl.ds(PIECE[a, 0, 0], 64), :]
            for b, y in ((-1, 0), (1, 9)):
                s1[pl.ds(8 + (x * 10 + y) * 8, 8), :] = pc[pl.ds(PIECE[a, b, 0], 8), :]
        s0[...] = s1[pl.ds(7, 800), :]
        s2[...] = s1[pl.ds(9, 800), :]
        for c, ref, lane in ((-1, s0, 0), (1, s2, 7)):
            for a in range(8):
                ref[pl.ds(((a + 1) * 10 + 1) * 8 + lane, 8, stride=8), :] = pc[
                    pl.ds(PIECE[0, 0, c] + 8 * a, 8), :
                ]
            for a, x in ((-1, 0), (1, 9)):
                ref[pl.ds((x * 10 + 1) * 8 + lane, 8, stride=8), :] = pc[
                    pl.ds(PIECE[a, 0, c], 8), :
                ]
                ref[pl.ds((10 + x) * 8 + lane, 8, stride=80), :] = pc[pl.ds(PIECE[0, a, c], 8), :]
                for b, y in ((-1, 0), (1, 9)):
                    ref[pl.ds((x * 10 + y) * 8 + lane, 1), :] = pc[pl.ds(PIECE[a, b, c], 1), :]
        for a in range(10):
            for b in range(3):
                for c, ref in enumerate((s0, s1, s2)):
                    start = (a * 10 + b) * 8 + (8 if c == 1 else 0)
                    at = 640 * s + 64 * a
                    cols[at : at + 64, (3 * b + c) * 128 : (3 * b + c) * 128 + 128] = ref[
                        pl.ds(start, 64), :
                    ].astype(BF)
        taps = nn(cols[640 * s : 640 * s + 640, :], weight[0:1152, :])
        pre = taps[0:512, 0:128] + taps[64:576, 128:256] + taps[128:640, 256:384]
        pool_voxels(pre * (1.0 / (1.0 + jnp.exp(-pre))), pooled, 8 * s)
        pre = pre.T
        gate = 1.0 / (1.0 + jnp.exp(-pre))
        acts.append(pre * gate)
        slopes.append(gate * (1.0 + pre * (1.0 - gate)))
    second = lax.broadcasted_iota(jnp.int32, (16, 1), 0) >= 8
    valid = [
        ((parent[s] >= 0) & (parent[s] * 64 + child[s] >= 0)).astype(F32) * flags[s : s + 1, 0:1]
        for s in range(2)
    ]
    valid = jnp.where(second, valid[1], valid[0])
    coarse_in = (pooled[...] * (1.0 / 64.0) * valid).astype(BF)
    grad_out = ((grad_pooled[0] + grad_pooled[1]) * valid).astype(BF)
    coarse_pre = nn(coarse_in, up)
    gate = 1.0 / (1.0 + jnp.exp(-coarse_pre))
    coarse_mid = (coarse_pre * gate).astype(BF)
    grad_pre = nt(grad_out, down) * (gate * (1.0 + coarse_pre * (1.0 - gate)))
    grad_pre = grad_pre.astype(BF)
    coarse_out = nn(coarse_mid, down).astype(BF)
    grad_cin = nt(grad_pre, up).astype(BF)
    lift = nt(eye, coarse_out).astype(BF)
    back = nt(eye, grad_cin).astype(BF)
    for s in range(2):
        live = flags[s : s + 1, 0:1]
        pool = pool_rows(s)
        grad_in = gout[s].astype(F32) * live + nn(back, pool) * (1.0 / 64.0)
        grad_t[s] = (grad_in * slopes[s]).astype(BF)
        out_v[s] = (feat[s].astype(F32) * live + acts[s] + nn(lift, pool)).astype(BF)
    copy = pltpu.make_async_copy(out_v, out, sem.at[0])
    copy.start()

    def put(block, value):
        wsum[pl.ds(block * 128, 128), :] = value.astype(BF)

    grad_up = nn(nt(eye, coarse_in).astype(BF), grad_pre)
    for h in range(2):
        put(27 + h, grad_up[:, h * 128 : h * 128 + 128])
        middle = nt(eye, coarse_mid[:, h * 128 : h * 128 + 128]).astype(BF)
        put(29 + h, nn(middle, grad_out))
    put(31, jnp.zeros((128, 128), F32))
    for a in range(3):
        total = nn(grad_t[0], cols[64 * a : 64 * a + 512, :])
        total = total + nn(grad_t[1], cols[64 * a + 640 : 64 * a + 1152, :])
        for n in range(9):
            put(9 * a + n, total[:, n * 128 : n * 128 + 128].T)
    send[...] = wsum[pl.ds(pl.multiple_of((1 - core[0]) * 2048, 2048), 2048), :]
    copy.wait()


def pair_kernel(core, line, wsum, other, grad, own, one, two, three, held):
    held[...] = grad[...]
    for step, ref in enumerate((own, one, two, three)):
        at = pl.multiple_of(((line[0] + step) & 3) * 512, 512)
        kept = wsum[pl.ds(pl.multiple_of(core[0] * 2048 + at, 512), 512), :].astype(F32)
        ref[...] = (kept + other[pl.ds(at, 512), :].astype(F32)).astype(ref.dtype)


def backward_kernel(grad_t, weight, own, msg, lhs, acc_all, pc_all, rows_all):
    zero = jnp.zeros((64, 128), BF)
    for a in range(3):
        for n in [*range(a), *range(8 + a, 10)]:
            for s in range(2):
                lhs[s, n * 64 : n * 64 + 64, a * 128 : a * 128 + 128] = zero
    low = (lax.broadcasted_iota(jnp.int32, (64, 1), 0) & 7) != 0
    high = (lax.broadcasted_iota(jnp.int32, (64, 1), 0) & 7) != 7

    for s in range(2):
        acc, pc, rows = acc_all.at[s], pc_all.at[s], rows_all.at[s]
        values = grad_t[s].astype(F32).T.astype(BF)
        for a in range(3):
            lhs[s, a * 64 : a * 64 + 512, a * 128 : a * 128 + 128] = values
        acc[...] = jnp.zeros_like(acc)
        for b in range(3):
            part = nt(lhs[s], weight[b * 384 : b * 384 + 384, :])
            for c in range(3):
                for a in range(10):
                    at = pl.ds(8 + (a * 10 + b) * 8, 64)
                    acc[c, at, :] += part[a * 64 : a * 64 + 64, c * 128 : c * 128 + 128]

        def middle(row, size):
            at = 8 + row
            total = acc[1, pl.ds(at, size), :]
            total = total + jnp.where(high[:size], acc[0, pl.ds(at + 1, size), :], 0.0)
            return total + jnp.where(low[:size], acc[2, pl.ds(at - 1, size), :], 0.0)

        for a in range(8):
            own[s, pl.ds(a * 64, 64), :] = middle(((a + 1) * 10 + 1) * 8, 64)
            for d, b in (((0, -1, 0), 0), ((0, 1, 0), 9)):
                pc[pl.ds(PIECE[d] + 8 * a, 8), :] = middle(((a + 1) * 10 + b) * 8, 8)
        for a, x in ((-1, 0), (1, 9)):
            pc[pl.ds(PIECE[a, 0, 0], 64), :] = middle((x * 10 + 1) * 8, 64)
            for b, y in ((-1, 0), (1, 9)):
                pc[pl.ds(PIECE[a, b, 0], 8), :] = middle((x * 10 + y) * 8, 8)
        for c, ref, lane in ((-1, acc.at[0], 8), (1, acc.at[2], 15)):
            for a in range(8):
                pc[pl.ds(PIECE[0, 0, c] + 8 * a, 8), :] = ref[
                    pl.ds(((a + 1) * 10 + 1) * 8 + lane, 8, stride=8), :
                ]
            for a, x in ((-1, 0), (1, 9)):
                pc[pl.ds(PIECE[a, 0, c], 8), :] = ref[pl.ds((x * 10 + 1) * 8 + lane, 8, stride=8), :]
                pc[pl.ds(PIECE[0, a, c], 8), :] = ref[pl.ds((10 + x) * 8 + lane, 8, stride=80), :]
                for b, y in ((-1, 0), (1, 9)):
                    pc[pl.ds(PIECE[a, b, c], 1), :] = ref[pl.ds((x * 10 + y) * 8 + lane, 1), :]
        to_shares(pc, rows)
        msg[:, 16 * s : 16 * s + 16, :] = rows[...].astype(BF).reshape(32, 16, 128)


def join_kernel(terms, own, away1, away2, away3, msg):
    msg[:, 0:32, :] = terms[...]
    total = own[...] + away1[...].astype(F32) + away2[...].astype(F32) + away3[...].astype(F32)
    msg[:, 32:48, :] = total.astype(BF).reshape(32, 16, 128)


def merge_kernel(got, named, out, hot):
    same = same_part()
    zero = jnp.zeros((16, 128), BF)
    share = jnp.sum(got[:, 32:48, :].astype(F32), axis=0).astype(BF)
    out[:, 32:48, :] = jnp.broadcast_to(share[None], (32, 16, 128))
    total = jnp.zeros((1024, 128), F32)
    for s in range(2):
        for n in range(4):
            asked = named[s, :, n * 128 : n * 128 + 128]
            for brick in range(64):
                hot[s, brick * 16 : brick * 16 + 16, n * 128 : n * 128 + 128] = jnp.where(
                    asked == jnp.full((16, 128), brick, BF), same, zero
                )
        total = total + nn(hot[s], got[:, 16 * s : 16 * s + 16, :].reshape(512, 128))
    out[:, 0:32, :] = total.astype(BF).reshape(32, 32, 128)


def finish_kernel(flags, got, own, gout, out, rows, pc, total):
    for s in range(2):
        live = flags[s : s + 1, 0:1]
        rows[...] = got[:, 16 * s : 16 * s + 16, :].reshape(512, 128).astype(F32)
        to_pieces(rows, pc)
        total[...] = own[s]
        for d in OFFSETS:
            for at, first, size, stride in voxel_runs(d):
                where = run(first, size, stride)
                total[where, :] = total[where, :] + pc[pl.ds(PIECE[d] + at, size), :]
        out[s] = (total[...].T + gout[s].astype(F32) * live).astype(BF)


def assemble_kernel(flip, core, line, *refs):
    parts, (conv, up, down, held, sems) = refs[:4], refs[-5:]
    half = core[0] ^ flip

    def moves(n, first):
        def copy(src, dst, k):
            return pltpu.make_async_copy(src, dst, sems.at[n, k])

        block = held.at[n]
        return (
            (first < 24, lambda: [copy(block, conv.at[pl.ds(first, 4)], 0)]),
            (
                first == 24,
                lambda: [
                    copy(block.at[0:3], conv.at[pl.ds(24, 3)], 0),
                    copy(block.at[3], up.at[:, pl.ds(0, 128)], 1),
                ],
            ),
            (
                first == 28,
                lambda: [
                    copy(block.at[0], up.at[:, pl.ds(128, 128)], 0),
                    copy(block.at[1], down.at[pl.ds(0, 128), :], 1),
                    copy(block.at[2], down.at[pl.ds(128, 128), :], 2),
                ],
            ),
        )

    firsts = [half * 16 + ((line[0] + n) & 3) * 4 for n in range(4)]
    for n, part in enumerate(parts):
        held[n] = part[...].astype(F32).reshape(4, 128, 128)
        for when, copies in moves(n, firsts[n]):

            @pl.when(when)
            def _():
                for copy in copies():
                    copy.start()

    for n in range(4):
        for when, copies in moves(n, firsts[n]):

            @pl.when(when)
            def _():
                for copy in copies():
                    copy.wait()


VM = pl.BlockSpec(memory_space=pltpu.VMEM)
SM = pl.BlockSpec(memory_space=pltpu.SMEM)


HB = pl.BlockSpec(memory_space=pltpu.HBM)


def call(
    kernel, shapes, scalars, arrays, scratch=(), flops=1e6, limit=24, ins=None, outs=None,
    alias=None, name=None,
):
    moved = sum(x.size * x.dtype.itemsize for x in arrays)
    moved += sum(int(np.prod(s.shape)) * s.dtype.itemsize for s in shapes)
    return pl.pallas_call(
        kernel,
        out_shape=shapes,
        in_specs=[SM] * len(scalars) + (ins or [VM] * len(arrays)),
        out_specs=outs or [VM] * len(shapes),
        input_output_aliases=alias or {},
        scratch_shapes=list(scratch),
        compiler_params=pltpu.CompilerParams(vmem_limit_bytes=limit * 2**20),
        cost_estimate=pl.CostEstimate(
            flops=int(flops), bytes_accessed=int(moved), transcendentals=0
        ),
        name=name,
    )(*scalars, *arrays)


def shape(dims, dtype):
    return jax.ShapeDtypeStruct(dims, dtype)


def on_device(
    features,
    grad_out,
    conv_weight,
    coarse_up,
    coarse_down,
    counts,
    neighbour_owner,
    neighbour_slot,
    parent,
    child_slot,
):
    grp = lax.axis_index("grp").astype(jnp.int32)
    core = (grp & 1).reshape(1)
    line = (grp >> 1).reshape(1)
    swap = [(i, i ^ 1) for i in range(8)]
    slots = lax.broadcasted_iota(jnp.int32, (8, 128), 0)
    flags = (slots < counts[0]).astype(F32)
    (msg,) = call(
        ask_kernel,
        [shape((32, 32, 128), BF)],
        [],
        [features, neighbour_owner, neighbour_slot, jnp.asarray(choice_table(), BF)],
        [
            pltpu.VMEM((2, 128, 512), BF),
            pltpu.VMEM((2, 26), jnp.int32),
            pltpu.VMEM((2, 26), jnp.int32),
            pltpu.VMEM((128, 1024), BF),
            pltpu.VMEM((16, 128), F32),
            pltpu.VMEM((2, 8, 128), F32),
            pltpu.VMEM((2, 512, 128), F32),
            pltpu.VMEM((2, 512, 128), F32),
            pltpu.VMEM((2, 512, 128), F32),
            pltpu.VMEM((32, 32, 128), BF),
            pltpu.SemaphoreType.DMA((7,)),
        ],
        flops=2e6,
        limit=60,
        ins=[HB] * 3 + [pl.BlockSpec(memory_space=pl.ANY)],
        outs=[HB],
        name="ask",
    )
    first = lax.all_to_all(msg, "dev", split_axis=0, concat_axis=0, tiled=True)
    answer, table = call(
        route_kernel,
        [shape((32, 32, 128), BF), shape((2, 16, 512), BF)],
        [],
        [first],
        [pltpu.VMEM((1024, 1024), BF)],
        flops=3e8,
        name="route",
    )
    halo = lax.all_to_all(answer, "dev", split_axis=0, concat_axis=0, tiled=True)
    weight = conv_weight.reshape(3, 1152, 128)
    weight = jnp.concatenate([weight[0], weight[1], weight[2]], axis=1)
    coarse = jnp.concatenate([jnp.pad(coarse_up, ((0, 128), (0, 0))), coarse_down], axis=1)
    weight = jnp.concatenate([weight, coarse], axis=0)
    output, grad_pre, wsum, send = call(
        forward_kernel,
        [
            shape((2, 128, 512), BF),
            shape((2, 128, 512), BF),
            shape((4096, 128), BF),
            shape((2048, 128), BF),
        ],
        [parent, child_slot, core],
        [flags, features, halo, grad_out, weight],
        [
            pltpu.VMEM((2, 512, 128), F32),
            pltpu.VMEM((2, 512, 128), F32),
            pltpu.VMEM((2, 512, 128), F32),
            pltpu.VMEM((2, 800, 128), F32),
            pltpu.VMEM((2, 816, 128), F32),
            pltpu.VMEM((2, 800, 128), F32),
            pltpu.VMEM((1280, 1152), BF),
            pltpu.VMEM((16, 128), F32),
            pltpu.VMEM((2, 16, 128), F32),
            pltpu.VMEM((2, 128, 512), BF),
            pltpu.SemaphoreType.DMA((1,)),
        ],
        flops=2e9,
        outs=[HB, VM, VM, VM],
        name="forward",
    )
    other = lax.ppermute(send, "grp", swap)
    own_sum, *away, grad_pre = call(
        pair_kernel,
        [shape((512, 128), F32)] + [shape((512, 128), BF)] * 3 + [shape((2, 128, 512), BF)],
        [core, line],
        [wsum, other, grad_pre],
        name="pair",
    )
    away = [
        lax.ppermute(away[step - 1], "grp", [(i, (i + 2 * step) % 8) for i in range(8)])
        for step in (2, 1, 3)
    ]
    own, terms = call(
        backward_kernel,
        [shape((2, 512, 128), F32), shape((32, 32, 128), BF)],
        [],
        [grad_pre, weight],
        [
            pltpu.VMEM((2, 640, 384), BF),
            pltpu.VMEM((2, 3, 816, 128), F32),
            pltpu.VMEM((2, 512, 128), F32),
            pltpu.VMEM((2, 512, 128), F32),
        ],
        flops=4e9,
        name="backward",
    )
    (terms,) = call(
        join_kernel, [shape((32, 48, 128), BF)], [], [terms, own_sum, *away], name="join"
    )
    terms = lax.all_to_all(terms, "dev", split_axis=0, concat_axis=0, tiled=True)
    (sums,) = call(
        merge_kernel,
        [shape((32, 48, 128), BF)],
        [],
        [terms, table],
        [pltpu.VMEM((2, 1024, 512), BF)],
        flops=3e8,
        name="merge",
    )
    back = lax.all_to_all(sums, "dev", split_axis=0, concat_axis=0, tiled=True)
    chunk = back[:, 32:48, :].reshape(512, 128)
    parts = {
        step: lax.ppermute(chunk, "grp", [(i, (i - 2 * step) % 8) for i in range(8)])
        for step in (2, 1, 3)
    }
    (grad_features,) = call(
        finish_kernel,
        [shape((2, 128, 512), BF)],
        [],
        [flags, back, own, grad_out],
        [pltpu.VMEM((512, 128), F32)] * 3,
        flops=3e8,
        name="finish",
    )
    parts, grad_features = lax.optimization_barrier((parts, grad_features))
    mine = [chunk, parts[1], parts[2], parts[3]]
    others = [lax.ppermute(x, "grp", swap) for x in mine]

    def assemble(flip, pieces, held):
        return call(
            functools.partial(assemble_kernel, flip),
            [shape((27, 128, 128), F32), shape((128, 256), F32), shape((256, 128), F32)],
            [core, line],
            pieces + held,
            [pltpu.VMEM((4, 4, 128, 128), F32), pltpu.SemaphoreType.DMA((4, 3))],
            ins=[VM] * 4 + [HB] * len(held),
            outs=[HB] * 3,
            alias={6 + n: n for n in range(len(held))},
            name="assemble",
        )

    grad_conv, grad_up, grad_down = assemble(1, others, list(assemble(0, mine, [])))
    return (output, grad_features, grad_conv, grad_up, grad_down)


def solution(mesh):
    return jax.shard_map(
        on_device,
        mesh=mesh,
        in_specs=(
            P(("grp", "dev"), None, None),
            P(("grp", "dev"), None, None),
            P(),
            P(),
            P(),
            P(("grp", "dev")),
            P(("grp", "dev"), None),
            P(("grp", "dev"), None),
            P(("grp", "dev")),
            P(("grp", "dev")),
        ),
        out_specs=(P(("grp", "dev"), None, None), P(("grp", "dev"), None, None), P(), P(), P()),
        check_vma=False,
    )
```

```python
import functools

import jax
import jax.numpy as jnp
import numpy as np
from jax import lax
from jax.experimental import pallas as pl
from jax.experimental.pallas import tpu as pltpu
from jax.sharding import PartitionSpec as P

BF = jnp.bfloat16
F32 = jnp.float32

OFFSETS = [
    (a, b, c) for a in (-1, 0, 1) for b in (-1, 0, 1) for c in (-1, 0, 1) if (a, b, c) != (0, 0, 0)
]
FACES = [d for d in OFFSETS if sum(map(abs, d)) == 1]
EDGES = [d for d in OFFSETS if sum(map(abs, d)) == 2]
CORNERS = [d for d in OFFSETS if sum(map(abs, d)) == 3]
PIECE = {d: 64 * n for n, d in enumerate(FACES)}
PIECE.update({d: 384 + 8 * n for n, d in enumerate(EDGES)})
PIECE.update({d: 480 + n for n, d in enumerate(CORNERS)})


def voxel_runs(d):
    a, b, c = (7 if x < 0 else 0 for x in d)
    free = [x == 0 for x in d]
    if free == [True, True, False]:
        return [(0, c, 64, 8)]
    if free == [True, False, True]:
        return [(8 * x, x * 64 + b * 8, 8, 1) for x in range(8)]
    if free == [False, True, True]:
        return [(0, a * 64, 64, 1)]
    size = 8 if any(free) else 1
    stride = (64 if free[0] else 1) * (8 if free[1] else 1)
    return [(0, a * 64 + b * 8 + c, size, stride)]


def run(start, size, stride):
    return pl.ds(start, size) if stride == 1 else pl.ds(start, size, stride=stride)


SHARES = [((64 * f + p, 32, 2), (2 * f + p, 32, 16)) for f in range(6) for p in range(2)]
SHARES += [((384 + 32 * m, 32, 1), (12 + m, 32, 16)) for m in range(3)]


def share_directions(group):
    edges = [EDGES[4 * m + group // 2] for m in range(3)]
    return [OFFSETS.index(d) for d in [FACES[q // 2] for q in range(12)] + edges + [CORNERS[group]]]


def choice_table():
    table = np.zeros((128, 8, 128), np.float32)
    for group in range(8):
        for q, direction in enumerate(share_directions(group)):
            table[direction, group, 32 + q] = 1
    return table.reshape(128, 1024)


def few_lanes(rows):
    return lax.broadcasted_iota(jnp.int32, (rows, 128), 1) < 32


def to_pieces(rows, pieces):
    for there, here in SHARES:
        pieces[run(*there), :] = rows[run(*here), :]
    total = jnp.zeros((8, 128), F32)
    for n in range(4):
        part = jnp.where(few_lanes(8), rows[pl.ds(15 + 16 * n, 8, stride=64), :], 0.0)
        total = total + (pltpu.roll(part, 32 * n, 1) if n else part)
    pieces[pl.ds(480, 8), :] = total


def to_shares(pieces, rows, extra=None):
    for there, here in SHARES:
        rows[run(*here), :] = pieces[run(*there), :]
    for n in range(4):
        part = pieces[pl.ds(480, 8), :]
        part = pltpu.roll(part, 128 - 32 * n, 1) if n else part
        if extra is not None:
            part = jnp.where(few_lanes(8), part, extra)
        rows[pl.ds(15 + 16 * n, 8, stride=64), :] = part


def nn(x, y):
    return lax.dot_general(x, y, (((1,), (0,)), ((), ())), preferred_element_type=F32)


def nt(x, y):
    return lax.dot_general(x, y, (((1,), (1,)), ((), ())), preferred_element_type=F32)


def identity():
    rows = lax.broadcasted_iota(jnp.int32, (128, 128), 0)
    lanes = lax.broadcasted_iota(jnp.int32, (128, 128), 1)
    return (rows == lanes).astype(F32).astype(BF)


def pool_rows(s):
    rows = lax.broadcasted_iota(jnp.int32, (16, 512), 0) - 8 * s
    lanes = lax.broadcasted_iota(jnp.int32, (16, 512), 1)
    block = ((lanes >> 8) & 1) * 4 + ((lanes >> 5) & 1) * 2 + ((lanes >> 2) & 1)
    return (rows == block).astype(F32).astype(BF)


def pool_voxels(values, sums, first):
    for a in range(2):
        planes = values[a * 256 : a * 256 + 64]
        for n in range(1, 4):
            planes = planes + values[a * 256 + n * 64 : a * 256 + n * 64 + 64]
        for b in range(2):
            line = planes[b * 32 : b * 32 + 8]
            for n in range(1, 4):
                line = line + planes[b * 32 + n * 8 : b * 32 + n * 8 + 8]
            for c in range(2):
                at = first + 4 * a + 2 * b + c
                sums[at : at + 1, :] = jnp.sum(line[4 * c : 4 * c + 4], axis=0, keepdims=True)


def ask_kernel(
    feat, owner, slot, choice, msg,
    feat_v, owner_v, slot_v, choice_v, bricks, tables, voxels, pc, rows, msg_v, sems,
):
    pairs = (
        (owner, owner_v), (slot, slot_v), (choice, choice_v),
        (feat.at[0], feat_v.at[0]), (feat.at[1], feat_v.at[1]),
    )
    copies = [
        pltpu.make_async_copy(src, dst, sems.at[n]) for n, (src, dst) in enumerate(pairs)
    ]
    for copy in copies:
        copy.start()
    bricks[...] = jnp.zeros((16, 128), F32)
    for copy in copies[:3]:
        copy.wait()
    named = jnp.where(owner_v[...] >= 0, owner_v[...] * 2 + slot_v[...], -1)
    bricks[0:2, 0:26] = named.astype(F32)
    asked = nn(bricks[...].astype(BF), choice_v[...])
    for group in range(8):
        for s in range(2):
            tables[s, group : group + 1, :] = asked[s : s + 1, group * 128 : group * 128 + 128]
    sent = []
    for s in range(2):
        copies[3 + s].wait()
        voxels[s] = feat_v[s].astype(F32).T
        for d in OFFSETS:
            for at, first, size, stride in voxel_runs(d):
                pc[s, pl.ds(PIECE[d] + at, size), :] = voxels.at[s][run(first, size, stride), :]
        to_shares(pc.at[s], rows.at[s], tables[s])
        at = pl.ds(16 * s, 16)
        msg_v[:, at, :] = rows[s].astype(BF).reshape(32, 16, 128)
        sent.append(pltpu.make_async_copy(msg_v.at[:, at, :], msg.at[:, at, :], sems.at[5 + s]))
        sent[-1].start()
    for copy in sent:
        copy.wait()


def same_part():
    rows = lax.broadcasted_iota(jnp.int32, (16, 128), 0)
    lanes = lax.broadcasted_iota(jnp.int32, (16, 128), 1) & 15
    return (rows == lanes).astype(F32).astype(BF)


def route_kernel(got, out, named, hot):
    same = jnp.broadcast_to(same_part()[None], (32, 16, 128))
    zero = jnp.zeros((32, 16, 128), BF)
    ones = jnp.ones((128, 128), BF)
    part = lax.broadcasted_iota(jnp.int32, (16, 128), 0)
    lanes = lax.broadcasted_iota(jnp.int32, (16, 128), 1)
    place = (lanes == part + 32)[None]
    for s in range(2):
        table = got[:, 16 * s : 16 * s + 16, :].astype(F32)[:, 15:16, :]
        table = jnp.where(place, jnp.broadcast_to(table, (32, 16, 128)), 0.0)
        asked = nn(table.astype(BF).reshape(512, 128), ones)
        named[s] = asked.T[0:16].astype(BF)
        asked = asked.astype(BF).reshape(32, 16, 128)
        for n in range(8):
            here = ((lanes >> 4) + 8 * n).astype(F32).astype(BF)
            picked = jnp.where(asked == here[None], same, zero)
            hot[s * 512 : s * 512 + 512, n * 128 : n * 128 + 128] = picked.reshape(512, 128)
    answer = nn(hot[...], got[...].reshape(1024, 128)).astype(BF)
    for s in range(2):
        out[:, 16 * s : 16 * s + 16, :] = answer[s * 512 : s * 512 + 512].reshape(32, 16, 128)


def forward_kernel(
    parent, child, core, flags, feat, got, gout, weight,
    out, grad_t, keep, send,
    rows_all, pc_all, mine_all, s0_all, s1_all, s2_all, cols, pooled, grad_pooled, out_v, wsum, sem,
):
    eye = identity()
    up, down = weight[1152:1280, 0:256], weight[1152:1408, 256:384]
    acts, slopes = [], []
    for s in range(2):
        rows, pc, mine, s0, s1, s2 = (
            x.at[s] for x in (rows_all, pc_all, mine_all, s0_all, s1_all, s2_all)
        )
        live = flags[s : s + 1, 0:1]
        pool = pool_rows(s)
        mine[...] = (feat[s].astype(F32) * live).T
        grad_pooled[s] = nt(pool, gout[s]) * live
        rows[...] = got[:, 16 * s : 16 * s + 16, :].reshape(512, 128).astype(F32)
        to_pieces(rows, pc)
        for a in range(8):
            s1[pl.ds(8 + ((a + 1) * 10 + 1) * 8, 64), :] = mine[a * 64 : a * 64 + 64, :]
            for d, b in (((0, -1, 0), 0), ((0, 1, 0), 9)):
                s1[pl.ds(8 + ((a + 1) * 10 + b) * 8, 8), :] = pc[pl.ds(PIECE[d] + 8 * a, 8), :]
        for a, x in ((-1, 0), (1, 9)):
            s1[pl.ds(8 + (x * 10 + 1) * 8, 64), :] = pc[pl.ds(PIECE[a, 0, 0], 64), :]
            for b, y in ((-1, 0), (1, 9)):
                s1[pl.ds(8 + (x * 10 + y) * 8, 8), :] = pc[pl.ds(PIECE[a, b, 0], 8), :]
        s0[...] = s1[pl.ds(7, 800), :]
        s2[...] = s1[pl.ds(9, 800), :]
        for c, ref, lane in ((-1, s0, 0), (1, s2, 7)):
            for a in range(8):
                ref[pl.ds(((a + 1) * 10 + 1) * 8 + lane, 8, stride=8), :] = pc[
                    pl.ds(PIECE[0, 0, c] + 8 * a, 8), :
                ]
            for a, x in ((-1, 0), (1, 9)):
                ref[pl.ds((x * 10 + 1) * 8 + lane, 8, stride=8), :] = pc[
                    pl.ds(PIECE[a, 0, c], 8), :
                ]
                ref[pl.ds((10 + x) * 8 + lane, 8, stride=80), :] = pc[pl.ds(PIECE[0, a, c], 8), :]
                for b, y in ((-1, 0), (1, 9)):
                    ref[pl.ds((x * 10 + y) * 8 + lane, 1), :] = pc[pl.ds(PIECE[a, b, c], 1), :]
        for a in range(10):
            for b in range(3):
                for c, ref in enumerate((s0, s1, s2)):
                    start = (a * 10 + b) * 8 + (8 if c == 1 else 0)
                    at = 640 * s + 64 * a
                    cols[at : at + 64, (3 * b + c) * 128 : (3 * b + c) * 128 + 128] = ref[
                        pl.ds(start, 64), :
                    ].astype(BF)
        taps = nn(cols[640 * s : 640 * s + 640, :], weight[0:1152, :])
        pre = taps[0:512, 0:128] + taps[64:576, 128:256] + taps[128:640, 256:384]
        pool_voxels(pre * (1.0 / (1.0 + jnp.exp(-pre))), pooled, 8 * s)
        pre = pre.T
        gate = 1.0 / (1.0 + jnp.exp(-pre))
        acts.append(pre * gate)
        slopes.append(gate * (1.0 + pre * (1.0 - gate)))
    second = lax.broadcasted_iota(jnp.int32, (16, 1), 0) >= 8
    valid = [
        ((parent[s] >= 0) & (parent[s] * 64 + child[s] >= 0)).astype(F32) * flags[s : s + 1, 0:1]
        for s in range(2)
    ]
    valid = jnp.where(second, valid[1], valid[0])
    coarse_in = (pooled[...] * (1.0 / 64.0) * valid).astype(BF)
    grad_out = ((grad_pooled[0] + grad_pooled[1]) * valid).astype(BF)
    coarse_pre = nn(coarse_in, up)
    gate = 1.0 / (1.0 + jnp.exp(-coarse_pre))
    coarse_mid = (coarse_pre * gate).astype(BF)
    grad_pre = nt(grad_out, down) * (gate * (1.0 + coarse_pre * (1.0 - gate)))
    grad_pre = grad_pre.astype(BF)
    coarse_out = nn(coarse_mid, down).astype(BF)
    grad_cin = nt(grad_pre, up).astype(BF)
    lift = nt(eye, coarse_out).astype(BF)
    back = nt(eye, grad_cin).astype(BF)
    for s in range(2):
        live = flags[s : s + 1, 0:1]
        pool = pool_rows(s)
        grad_in = gout[s].astype(F32) * live + nn(back, pool) * (1.0 / 64.0)
        grad_t[s] = (grad_in * slopes[s]).astype(BF)
        out_v[s] = (feat[s].astype(F32) * live + acts[s] + nn(lift, pool)).astype(BF)
    copy = pltpu.make_async_copy(out_v, out, sem.at[0])
    copy.start()

    def put(block, value):
        wsum[pl.ds(block * 128, 128), :] = value.astype(BF)

    grad_up = nn(nt(eye, coarse_in).astype(BF), grad_pre)
    for h in range(2):
        put(27 + h, grad_up[:, h * 128 : h * 128 + 128])
        middle = nt(eye, coarse_mid[:, h * 128 : h * 128 + 128]).astype(BF)
        put(29 + h, nn(middle, grad_out))
    put(31, jnp.zeros((128, 128), F32))
    for a in range(3):
        total = nn(grad_t[0], cols[64 * a : 64 * a + 512, :])
        total = total + nn(grad_t[1], cols[64 * a + 640 : 64 * a + 1152, :])
        for n in range(9):
            put(9 * a + n, total[:, n * 128 : n * 128 + 128].T)
    send[...] = wsum[pl.ds(pl.multiple_of((1 - core[0]) * 2048, 2048), 2048), :]
    keep[...] = wsum[pl.ds(pl.multiple_of(core[0] * 2048, 2048), 2048), :]
    copy.wait()


def pair_kernel(core, line, wsum, other, grad, own, one, two, three, held):
    held[...] = grad[...]
    for step, ref in enumerate((own, one, two, three)):
        at = pl.multiple_of(((line[0] + step) & 3) * 512, 512)
        kept = wsum[pl.ds(at, 512), :].astype(F32)
        ref[...] = (kept + other[pl.ds(at, 512), :].astype(F32)).astype(ref.dtype)


def backward_kernel(grad_t, weight, own, msg, lhs, acc_all, pc_all, rows_all):
    zero = jnp.zeros((64, 128), BF)
    for a in range(3):
        for n in [*range(a), *range(8 + a, 10)]:
            for s in range(2):
                lhs[s, n * 64 : n * 64 + 64, a * 128 : a * 128 + 128] = zero
    low = (lax.broadcasted_iota(jnp.int32, (64, 1), 0) & 7) != 0
    high = (lax.broadcasted_iota(jnp.int32, (64, 1), 0) & 7) != 7

    for s in range(2):
        acc, pc, rows = acc_all.at[s], pc_all.at[s], rows_all.at[s]
        values = grad_t[s].astype(F32).T.astype(BF)
        for a in range(3):
            lhs[s, a * 64 : a * 64 + 512, a * 128 : a * 128 + 128] = values
        acc[...] = jnp.zeros_like(acc)
        for b in range(3):
            part = nt(lhs[s], weight[b * 384 : b * 384 + 384, :])
            for c in range(3):
                for a in range(10):
                    at = pl.ds(8 + (a * 10 + b) * 8, 64)
                    acc[c, at, :] += part[a * 64 : a * 64 + 64, c * 128 : c * 128 + 128]

        def middle(row, size):
            at = 8 + row
            total = acc[1, pl.ds(at, size), :]
            total = total + jnp.where(high[:size], acc[0, pl.ds(at + 1, size), :], 0.0)
            return total + jnp.where(low[:size], acc[2, pl.ds(at - 1, size), :], 0.0)

        for a in range(8):
            own[s, pl.ds(a * 64, 64), :] = middle(((a + 1) * 10 + 1) * 8, 64)
            for d, b in (((0, -1, 0), 0), ((0, 1, 0), 9)):
                pc[pl.ds(PIECE[d] + 8 * a, 8), :] = middle(((a + 1) * 10 + b) * 8, 8)
        for a, x in ((-1, 0), (1, 9)):
            pc[pl.ds(PIECE[a, 0, 0], 64), :] = middle((x * 10 + 1) * 8, 64)
            for b, y in ((-1, 0), (1, 9)):
                pc[pl.ds(PIECE[a, b, 0], 8), :] = middle((x * 10 + y) * 8, 8)
        for c, ref, lane in ((-1, acc.at[0], 8), (1, acc.at[2], 15)):
            for a in range(8):
                pc[pl.ds(PIECE[0, 0, c] + 8 * a, 8), :] = ref[
                    pl.ds(((a + 1) * 10 + 1) * 8 + lane, 8, stride=8), :
                ]
            for a, x in ((-1, 0), (1, 9)):
                pc[pl.ds(PIECE[a, 0, c], 8), :] = ref[pl.ds((x * 10 + 1) * 8 + lane, 8, stride=8), :]
                pc[pl.ds(PIECE[0, a, c], 8), :] = ref[pl.ds((10 + x) * 8 + lane, 8, stride=80), :]
                for b, y in ((-1, 0), (1, 9)):
                    pc[pl.ds(PIECE[a, b, c], 1), :] = ref[pl.ds((x * 10 + y) * 8 + lane, 1), :]
        to_shares(pc, rows)
        msg[:, 16 * s : 16 * s + 16, :] = rows[...].astype(BF).reshape(32, 16, 128)


def join_kernel(terms, own, away1, away2, away3, msg):
    msg[:, 0:32, :] = terms[...]
    total = own[...] + away1[...].astype(F32) + away2[...].astype(F32) + away3[...].astype(F32)
    msg[:, 32:48, :] = total.astype(BF).reshape(32, 16, 128)


def merge_kernel(got, named, out, hot):
    same = same_part()
    zero = jnp.zeros((16, 128), BF)
    share = jnp.sum(got[:, 32:48, :].astype(F32), axis=0).astype(BF)
    out[:, 32:48, :] = jnp.broadcast_to(share[None], (32, 16, 128))
    total = jnp.zeros((1024, 128), F32)
    for s in range(2):
        for n in range(4):
            asked = named[s, :, n * 128 : n * 128 + 128]
            for brick in range(64):
                hot[s, brick * 16 : brick * 16 + 16, n * 128 : n * 128 + 128] = jnp.where(
                    asked == jnp.full((16, 128), brick, BF), same, zero
                )
        total = total + nn(hot[s], got[:, 16 * s : 16 * s + 16, :].reshape(512, 128))
    out[:, 0:32, :] = total.astype(BF).reshape(32, 32, 128)


def finish_kernel(flags, got, own, gout, out, rows, pc, total):
    for s in range(2):
        live = flags[s : s + 1, 0:1]
        rows[...] = got[:, 16 * s : 16 * s + 16, :].reshape(512, 128).astype(F32)
        to_pieces(rows, pc)
        total[...] = own[s]
        for d in OFFSETS:
            for at, first, size, stride in voxel_runs(d):
                where = run(first, size, stride)
                total[where, :] = total[where, :] + pc[pl.ds(PIECE[d] + at, size), :]
        out[s] = (total[...].T + gout[s].astype(F32) * live).astype(BF)


def assemble_kernel(flip, core, line, *refs):
    parts, (conv, up, down, held, sems) = refs[:4], refs[-5:]
    half = core[0] ^ flip

    def moves(n, first):
        def copy(src, dst, k):
            return pltpu.make_async_copy(src, dst, sems.at[n, k])

        block = held.at[n]
        return (
            (first < 24, lambda: [copy(block, conv.at[pl.ds(first, 4)], 0)]),
            (
                first == 24,
                lambda: [
                    copy(block.at[0:3], conv.at[pl.ds(24, 3)], 0),
                    copy(block.at[3], up.at[:, pl.ds(0, 128)], 1),
                ],
            ),
            (
                first == 28,
                lambda: [
                    copy(block.at[0], up.at[:, pl.ds(128, 128)], 0),
                    copy(block.at[1], down.at[pl.ds(0, 128), :], 1),
                    copy(block.at[2], down.at[pl.ds(128, 128), :], 2),
                ],
            ),
        )

    firsts = [half * 16 + ((line[0] + n) & 3) * 4 for n in range(4)]
    for n, part in enumerate(parts):
        held[n] = part[...].astype(F32).reshape(4, 128, 128)
        for when, copies in moves(n, firsts[n]):

            @pl.when(when)
            def _():
                for copy in copies():
                    copy.start()

    for n in range(4):
        for when, copies in moves(n, firsts[n]):

            @pl.when(when)
            def _():
                for copy in copies():
                    copy.wait()


VM = pl.BlockSpec(memory_space=pltpu.VMEM)
SM = pl.BlockSpec(memory_space=pltpu.SMEM)


HB = pl.BlockSpec(memory_space=pltpu.HBM)


def call(
    kernel, shapes, scalars, arrays, scratch=(), flops=1e6, limit=24, ins=None, outs=None,
    alias=None, name=None,
):
    moved = sum(x.size * x.dtype.itemsize for x in arrays)
    moved += sum(int(np.prod(s.shape)) * s.dtype.itemsize for s in shapes)
    return pl.pallas_call(
        kernel,
        out_shape=shapes,
        in_specs=[SM] * len(scalars) + (ins or [VM] * len(arrays)),
        out_specs=outs or [VM] * len(shapes),
        input_output_aliases=alias or {},
        scratch_shapes=list(scratch),
        compiler_params=pltpu.CompilerParams(vmem_limit_bytes=limit * 2**20),
        cost_estimate=pl.CostEstimate(
            flops=int(flops), bytes_accessed=int(moved), transcendentals=0
        ),
        name=name,
    )(*scalars, *arrays)


def shape(dims, dtype):
    return jax.ShapeDtypeStruct(dims, dtype)


def on_device(
    features,
    grad_out,
    conv_weight,
    coarse_up,
    coarse_down,
    counts,
    neighbour_owner,
    neighbour_slot,
    parent,
    child_slot,
):
    grp = lax.axis_index("grp").astype(jnp.int32)
    core = (grp & 1).reshape(1)
    line = (grp >> 1).reshape(1)
    swap = [(i, i ^ 1) for i in range(8)]
    slots = lax.broadcasted_iota(jnp.int32, (8, 128), 0)
    flags = (slots < counts[0]).astype(F32)
    (msg,) = call(
        ask_kernel,
        [shape((32, 32, 128), BF)],
        [],
        [features, neighbour_owner, neighbour_slot, jnp.asarray(choice_table(), BF)],
        [
            pltpu.VMEM((2, 128, 512), BF),
            pltpu.VMEM((2, 26), jnp.int32),
            pltpu.VMEM((2, 26), jnp.int32),
            pltpu.VMEM((128, 1024), BF),
            pltpu.VMEM((16, 128), F32),
            pltpu.VMEM((2, 8, 128), F32),
            pltpu.VMEM((2, 512, 128), F32),
            pltpu.VMEM((2, 512, 128), F32),
            pltpu.VMEM((2, 512, 128), F32),
            pltpu.VMEM((32, 32, 128), BF),
            pltpu.SemaphoreType.DMA((7,)),
        ],
        flops=2e6,
        limit=60,
        ins=[HB] * 3 + [pl.BlockSpec(memory_space=pl.ANY)],
        outs=[HB],
        name="ask",
    )
    first = lax.all_to_all(msg, "dev", split_axis=0, concat_axis=0, tiled=True)
    answer, table = call(
        route_kernel,
        [shape((32, 32, 128), BF), shape((2, 16, 512), BF)],
        [],
        [first],
        [pltpu.VMEM((1024, 1024), BF)],
        flops=3e8,
        name="route",
    )
    halo = lax.all_to_all(answer, "dev", split_axis=0, concat_axis=0, tiled=True)
    weight = conv_weight.reshape(3, 1152, 128)
    weight = jnp.concatenate([weight[0], weight[1], weight[2]], axis=1)
    coarse = jnp.concatenate([jnp.pad(coarse_up, ((0, 128), (0, 0))), coarse_down], axis=1)
    weight = jnp.concatenate([weight, coarse], axis=0)
    output, grad_pre, wsum, send = call(
        forward_kernel,
        [
            shape((2, 128, 512), BF),
            shape((2, 128, 512), BF),
            shape((2048, 128), BF),
            shape((2048, 128), BF),
        ],
        [parent, child_slot, core],
        [flags, features, halo, grad_out, weight],
        [
            pltpu.VMEM((2, 512, 128), F32),
            pltpu.VMEM((2, 512, 128), F32),
            pltpu.VMEM((2, 512, 128), F32),
            pltpu.VMEM((2, 800, 128), F32),
            pltpu.VMEM((2, 816, 128), F32),
            pltpu.VMEM((2, 800, 128), F32),
            pltpu.VMEM((1280, 1152), BF),
            pltpu.VMEM((16, 128), F32),
            pltpu.VMEM((2, 16, 128), F32),
            pltpu.VMEM((2, 128, 512), BF),
            pltpu.VMEM((4096, 128), BF),
            pltpu.SemaphoreType.DMA((1,)),
        ],
        flops=2e9,
        outs=[HB, VM, VM, VM],
        name="forward",
    )
    other = lax.ppermute(send, "grp", swap)
    own_sum, *away, grad_pre = call(
        pair_kernel,
        [shape((512, 128), F32)] + [shape((512, 128), BF)] * 3 + [shape((2, 128, 512), BF)],
        [core, line],
        [wsum, other, grad_pre],
        name="pair",
    )
    away = [
        lax.ppermute(away[step - 1], "grp", [(i, (i + 2 * step) % 8) for i in range(8)])
        for step in (1, 3, 2)
    ]
    own, terms = call(
        backward_kernel,
        [shape((2, 512, 128), F32), shape((32, 32, 128), BF)],
        [],
        [grad_pre, weight],
        [
            pltpu.VMEM((2, 640, 384), BF),
            pltpu.VMEM((2, 3, 816, 128), F32),
            pltpu.VMEM((2, 512, 128), F32),
            pltpu.VMEM((2, 512, 128), F32),
        ],
        flops=4e9,
        name="backward",
    )
    (terms,) = call(
        join_kernel, [shape((32, 48, 128), BF)], [], [terms, own_sum, *away], name="join"
    )
    terms = lax.all_to_all(terms, "dev", split_axis=0, concat_axis=0, tiled=True)
    (sums,) = call(
        merge_kernel,
        [shape((32, 48, 128), BF)],
        [],
        [terms, table],
        [pltpu.VMEM((2, 1024, 512), BF)],
        flops=3e8,
        name="merge",
    )
    back = lax.all_to_all(sums, "dev", split_axis=0, concat_axis=0, tiled=True)
    chunk = back[:, 32:48, :].reshape(512, 128)
    parts = {
        step: lax.ppermute(chunk, "grp", [(i, (i - 2 * step) % 8) for i in range(8)])
        for step in (1, 3, 2)
    }
    (grad_features,) = call(
        finish_kernel,
        [shape((2, 128, 512), BF)],
        [],
        [flags, back, own, grad_out],
        [pltpu.VMEM((512, 128), F32)] * 3,
        flops=3e8,
        name="finish",
    )
    parts, grad_features = lax.optimization_barrier((parts, grad_features))
    mine = [chunk, parts[1], parts[2], parts[3]]
    others = [lax.ppermute(x, "grp", swap) for x in mine]

    def assemble(flip, pieces, held):
        return call(
            functools.partial(assemble_kernel, flip),
            [shape((27, 128, 128), F32), shape((128, 256), F32), shape((256, 128), F32)],
            [core, line],
            pieces + held,
            [pltpu.VMEM((4, 4, 128, 128), F32), pltpu.SemaphoreType.DMA((4, 3))],
            ins=[VM] * 4 + [HB] * len(held),
            outs=[HB] * 3,
            alias={6 + n: n for n in range(len(held))},
            name="assemble",
        )

    grad_conv, grad_up, grad_down = assemble(1, others, list(assemble(0, mine, [])))
    return (output, grad_features, grad_conv, grad_up, grad_down)


def solution(mesh):
    return jax.shard_map(
        on_device,
        mesh=mesh,
        in_specs=(
            P(("grp", "dev"), None, None),
            P(("grp", "dev"), None, None),
            P(),
            P(),
            P(),
            P(("grp", "dev")),
            P(("grp", "dev"), None),
            P(("grp", "dev"), None),
            P(("grp", "dev")),
            P(("grp", "dev")),
        ),
        out_specs=(P(("grp", "dev"), None, None), P(("grp", "dev"), None, None), P(), P(), P()),
        check_vma=False,
    )
```

```python
import functools

import jax
import jax.numpy as jnp
import numpy as np
from jax import lax
from jax.experimental import pallas as pl
from jax.experimental.pallas import tpu as pltpu
from jax.sharding import PartitionSpec as P

BF = jnp.bfloat16
F32 = jnp.float32

OFFSETS = [
    (a, b, c) for a in (-1, 0, 1) for b in (-1, 0, 1) for c in (-1, 0, 1) if (a, b, c) != (0, 0, 0)
]
FACES = [d for d in OFFSETS if sum(map(abs, d)) == 1]
EDGES = [d for d in OFFSETS if sum(map(abs, d)) == 2]
CORNERS = [d for d in OFFSETS if sum(map(abs, d)) == 3]
PIECE = {d: 64 * n for n, d in enumerate(FACES)}
PIECE.update({d: 384 + 8 * n for n, d in enumerate(EDGES)})
PIECE.update({d: 480 + n for n, d in enumerate(CORNERS)})


def voxel_runs(d):
    a, b, c = (7 if x < 0 else 0 for x in d)
    free = [x == 0 for x in d]
    if free == [True, True, False]:
        return [(0, c, 64, 8)]
    if free == [True, False, True]:
        return [(8 * x, x * 64 + b * 8, 8, 1) for x in range(8)]
    if free == [False, True, True]:
        return [(0, a * 64, 64, 1)]
    size = 8 if any(free) else 1
    stride = (64 if free[0] else 1) * (8 if free[1] else 1)
    return [(0, a * 64 + b * 8 + c, size, stride)]


def run(start, size, stride):
    return pl.ds(start, size) if stride == 1 else pl.ds(start, size, stride=stride)


SHARES = [((64 * f + p, 32, 2), (2 * f + p, 32, 16)) for f in range(6) for p in range(2)]
SHARES += [((384 + 32 * m, 32, 1), (12 + m, 32, 16)) for m in range(3)]


def share_directions(group):
    edges = [EDGES[4 * m + group // 2] for m in range(3)]
    return [OFFSETS.index(d) for d in [FACES[q // 2] for q in range(12)] + edges + [CORNERS[group]]]


def choice_table():
    table = np.zeros((128, 8, 128), np.float32)
    for group in range(8):
        for q, direction in enumerate(share_directions(group)):
            table[direction, group, 32 + q] = 1
    return table.reshape(128, 1024)


def few_lanes(rows):
    return lax.broadcasted_iota(jnp.int32, (rows, 128), 1) < 32


def to_pieces(rows, pieces):
    for there, here in SHARES:
        pieces[run(*there), :] = rows[run(*here), :]
    total = jnp.zeros((8, 128), F32)
    for n in range(4):
        part = jnp.where(few_lanes(8), rows[pl.ds(15 + 16 * n, 8, stride=64), :], 0.0)
        total = total + (pltpu.roll(part, 32 * n, 1) if n else part)
    pieces[pl.ds(480, 8), :] = total


def to_shares(pieces, rows, extra=None):
    for there, here in SHARES:
        rows[run(*here), :] = pieces[run(*there), :]
    for n in range(4):
        part = pieces[pl.ds(480, 8), :]
        part = pltpu.roll(part, 128 - 32 * n, 1) if n else part
        if extra is not None:
            part = jnp.where(few_lanes(8), part, extra)
        rows[pl.ds(15 + 16 * n, 8, stride=64), :] = part


def nn(x, y):
    return lax.dot_general(x, y, (((1,), (0,)), ((), ())), preferred_element_type=F32)


def nt(x, y):
    return lax.dot_general(x, y, (((1,), (1,)), ((), ())), preferred_element_type=F32)


def identity():
    rows = lax.broadcasted_iota(jnp.int32, (128, 128), 0)
    lanes = lax.broadcasted_iota(jnp.int32, (128, 128), 1)
    return (rows == lanes).astype(F32).astype(BF)


def pool_rows(s):
    rows = lax.broadcasted_iota(jnp.int32, (16, 512), 0) - 8 * s
    lanes = lax.broadcasted_iota(jnp.int32, (16, 512), 1)
    block = ((lanes >> 8) & 1) * 4 + ((lanes >> 5) & 1) * 2 + ((lanes >> 2) & 1)
    return (rows == block).astype(F32).astype(BF)


def pool_voxels(values, sums, first):
    for a in range(2):
        planes = values[a * 256 : a * 256 + 64]
        for n in range(1, 4):
            planes = planes + values[a * 256 + n * 64 : a * 256 + n * 64 + 64]
        for b in range(2):
            line = planes[b * 32 : b * 32 + 8]
            for n in range(1, 4):
                line = line + planes[b * 32 + n * 8 : b * 32 + n * 8 + 8]
            for c in range(2):
                at = first + 4 * a + 2 * b + c
                sums[at : at + 1, :] = jnp.sum(line[4 * c : 4 * c + 4], axis=0, keepdims=True)


def ask_kernel(
    feat, owner, slot, choice, msg,
    feat_v, owner_v, slot_v, choice_v, bricks, tables, voxels, pc, rows, msg_v, sems,
):
    pairs = (
        (owner, owner_v), (slot, slot_v), (choice, choice_v),
        (feat.at[0], feat_v.at[0]), (feat.at[1], feat_v.at[1]),
    )
    copies = [
        pltpu.make_async_copy(src, dst, sems.at[n]) for n, (src, dst) in enumerate(pairs)
    ]
    for copy in copies:
        copy.start()
    bricks[...] = jnp.zeros((16, 128), F32)
    for copy in copies[:3]:
        copy.wait()
    named = jnp.where(owner_v[...] >= 0, owner_v[...] * 2 + slot_v[...], -1)
    bricks[0:2, 0:26] = named.astype(F32)
    asked = nn(bricks[...].astype(BF), choice_v[...])
    for group in range(8):
        for s in range(2):
            tables[s, group : group + 1, :] = asked[s : s + 1, group * 128 : group * 128 + 128]
    sent = []
    for s in range(2):
        copies[3 + s].wait()
        voxels[s] = feat_v[s].astype(F32).T
        for d in OFFSETS:
            for at, first, size, stride in voxel_runs(d):
                pc[s, pl.ds(PIECE[d] + at, size), :] = voxels.at[s][run(first, size, stride), :]
        to_shares(pc.at[s], rows.at[s], tables[s])
        at = pl.ds(16 * s, 16)
        msg_v[:, at, :] = rows[s].astype(BF).reshape(32, 16, 128)
        sent.append(pltpu.make_async_copy(msg_v.at[:, at, :], msg.at[:, at, :], sems.at[5 + s]))
        sent[-1].start()
    for copy in sent:
        copy.wait()


def same_part():
    rows = lax.broadcasted_iota(jnp.int32, (16, 128), 0) & 7
    lanes = lax.broadcasted_iota(jnp.int32, (16, 128), 1) & 7
    return (rows == lanes).astype(F32).astype(BF)


def split_parts(got, s):
    rows = got[:, 16 * s : 16 * s + 16, :].astype(F32)
    return rows[:, 0:8, :], rows[:, 8:16, :]


def route_kernel(got, out, named, hot):
    same = jnp.broadcast_to(same_part()[None], (16, 16, 128))
    zero = jnp.zeros((16, 16, 128), BF)
    ones = jnp.ones((128, 128), BF)
    part = lax.broadcasted_iota(jnp.int32, (8, 128), 0)
    lanes = lax.broadcasted_iota(jnp.int32, (8, 128), 1)
    brick = lax.broadcasted_iota(jnp.int32, (16, 128), 1) >> 3
    split = [split_parts(got, s) for s in range(2)]
    answers = []
    for h in range(2):
        for s in range(2):
            table = jnp.broadcast_to(split[s][1][:, 7:8, :], (32, 8, 128))
            table = jnp.where((lanes == part + 32 + 8 * h)[None], table, 0.0)
            asked = nn(table.reshape(256, 128).astype(BF), ones)
            named[h, :, s * 256 : s * 256 + 256] = asked.T[0:16].astype(BF)
            asked = asked.astype(BF).reshape(16, 16, 128)
            for n in range(4):
                here = (brick + 16 * n).astype(F32).astype(BF)
                picked = jnp.where(asked == here[None], same, zero).reshape(256, 128)
                hot[h, s * 256 : s * 256 + 256, n * 128 : n * 128 + 128] = picked
        held = jnp.stack([split[0][h], split[1][h]], axis=1).reshape(512, 128).astype(BF)
        answers.append(nn(hot[h], held))
    for s in range(2):
        rows = [x[s * 256 : s * 256 + 256].reshape(32, 8, 128) for x in answers]
        out[:, 16 * s : 16 * s + 16, :] = jnp.concatenate(rows, axis=1).astype(BF)


def forward_kernel(
    parent, child, core, flags, feat, got, gout, weight,
    out, grad_t, keep, send,
    rows_all, pc_all, mine_all, s0_all, s1_all, s2_all, cols, pooled, grad_pooled, out_v, wsum, sem,
):
    eye = identity()
    up, down = weight[1152:1280, 0:256], weight[1152:1408, 256:384]
    acts, slopes = [], []
    for s in range(2):
        rows, pc, mine, s0, s1, s2 = (
            x.at[s] for x in (rows_all, pc_all, mine_all, s0_all, s1_all, s2_all)
        )
        live = flags[s : s + 1, 0:1]
        pool = pool_rows(s)
        mine[...] = (feat[s].astype(F32) * live).T
        grad_pooled[s] = nt(pool, gout[s]) * live
        rows[...] = got[:, 16 * s : 16 * s + 16, :].reshape(512, 128).astype(F32)
        to_pieces(rows, pc)
        for a in range(8):
            s1[pl.ds(8 + ((a + 1) * 10 + 1) * 8, 64), :] = mine[a * 64 : a * 64 + 64, :]
            for d, b in (((0, -1, 0), 0), ((0, 1, 0), 9)):
                s1[pl.ds(8 + ((a + 1) * 10 + b) * 8, 8), :] = pc[pl.ds(PIECE[d] + 8 * a, 8), :]
        for a, x in ((-1, 0), (1, 9)):
            s1[pl.ds(8 + (x * 10 + 1) * 8, 64), :] = pc[pl.ds(PIECE[a, 0, 0], 64), :]
            for b, y in ((-1, 0), (1, 9)):
                s1[pl.ds(8 + (x * 10 + y) * 8, 8), :] = pc[pl.ds(PIECE[a, b, 0], 8), :]
        s0[...] = s1[pl.ds(7, 800), :]
        s2[...] = s1[pl.ds(9, 800), :]
        for c, ref, lane in ((-1, s0, 0), (1, s2, 7)):
            for a in range(8):
                ref[pl.ds(((a + 1) * 10 + 1) * 8 + lane, 8, stride=8), :] = pc[
                    pl.ds(PIECE[0, 0, c] + 8 * a, 8), :
                ]
            for a, x in ((-1, 0), (1, 9)):
                ref[pl.ds((x * 10 + 1) * 8 + lane, 8, stride=8), :] = pc[
                    pl.ds(PIECE[a, 0, c], 8), :
                ]
                ref[pl.ds((10 + x) * 8 + lane, 8, stride=80), :] = pc[pl.ds(PIECE[0, a, c], 8), :]
                for b, y in ((-1, 0), (1, 9)):
                    ref[pl.ds((x * 10 + y) * 8 + lane, 1), :] = pc[pl.ds(PIECE[a, b, c], 1), :]
        for a in range(10):
            for b in range(3):
                for c, ref in enumerate((s0, s1, s2)):
                    start = (a * 10 + b) * 8 + (8 if c == 1 else 0)
                    at = 640 * s + 64 * a
                    cols[at : at + 64, (3 * b + c) * 128 : (3 * b + c) * 128 + 128] = ref[
                        pl.ds(start, 64), :
                    ].astype(BF)
    pres = []
    for s in range(2):
        taps = nn(cols[640 * s : 640 * s + 640, :], weight[0:1152, :])
        pre = taps[0:512, 0:128] + taps[64:576, 128:256] + taps[128:640, 256:384]
        pres.append(pre)
    for s in range(2):
        pre = pres[s]
        pool_voxels(pre * (1.0 / (1.0 + jnp.exp(-pre))), pooled, 8 * s)
        pre = pre.T
        gate = 1.0 / (1.0 + jnp.exp(-pre))
        acts.append(pre * gate)
        slopes.append(gate * (1.0 + pre * (1.0 - gate)))
    second = lax.broadcasted_iota(jnp.int32, (16, 1), 0) >= 8
    valid = [
        ((parent[s] >= 0) & (parent[s] * 64 + child[s] >= 0)).astype(F32) * flags[s : s + 1, 0:1]
        for s in range(2)
    ]
    valid = jnp.where(second, valid[1], valid[0])
    coarse_in = (pooled[...] * (1.0 / 64.0) * valid).astype(BF)
    grad_out = ((grad_pooled[0] + grad_pooled[1]) * valid).astype(BF)
    coarse_pre = nn(coarse_in, up)
    gate = 1.0 / (1.0 + jnp.exp(-coarse_pre))
    coarse_mid = (coarse_pre * gate).astype(BF)
    grad_pre = nt(grad_out, down) * (gate * (1.0 + coarse_pre * (1.0 - gate)))
    grad_pre = grad_pre.astype(BF)
    coarse_out = nn(coarse_mid, down).astype(BF)
    grad_cin = nt(grad_pre, up).astype(BF)
    lift = nt(eye, coarse_out).astype(BF)
    back = nt(eye, grad_cin).astype(BF)
    for s in range(2):
        live = flags[s : s + 1, 0:1]
        pool = pool_rows(s)
        grad_in = gout[s].astype(F32) * live + nn(back, pool) * (1.0 / 64.0)
        grad_t[s] = (grad_in * slopes[s]).astype(BF)
        out_v[s] = (feat[s].astype(F32) * live + acts[s] + nn(lift, pool)).astype(BF)
    copy = pltpu.make_async_copy(out_v, out, sem.at[0])
    copy.start()

    def put(block, value):
        wsum[pl.ds(block * 128, 128), :] = value.astype(BF)

    grad_up = nn(nt(eye, coarse_in).astype(BF), grad_pre)
    for h in range(2):
        put(27 + h, grad_up[:, h * 128 : h * 128 + 128])
        middle = nt(eye, coarse_mid[:, h * 128 : h * 128 + 128]).astype(BF)
        put(29 + h, nn(middle, grad_out))
    put(31, jnp.zeros((128, 128), F32))
    for a in range(3):
        total = nn(grad_t[0], cols[64 * a : 64 * a + 512, :])
        total = total + nn(grad_t[1], cols[64 * a + 640 : 64 * a + 1152, :])
        for n in range(9):
            put(9 * a + n, total[:, n * 128 : n * 128 + 128].T)
    send[...] = wsum[pl.ds(pl.multiple_of((1 - core[0]) * 2048, 2048), 2048), :]
    keep[...] = wsum[pl.ds(pl.multiple_of(core[0] * 2048, 2048), 2048), :]
    copy.wait()


def pair_kernel(core, line, wsum, other, grad, own, one, two, three, held):
    held[...] = grad[...]
    for step, ref in enumerate((own, one, two, three)):
        at = pl.multiple_of(((line[0] + step) & 3) * 512, 512)
        kept = wsum[pl.ds(at, 512), :].astype(F32)
        ref[...] = (kept + other[pl.ds(at, 512), :].astype(F32)).astype(ref.dtype)


def backward_kernel(grad_t, weight, own, msg, lhs, acc_all, pc_all, rows_all):
    zero = jnp.zeros((64, 128), BF)
    for a in range(3):
        for n in [*range(a), *range(8 + a, 10)]:
            for s in range(2):
                lhs[s, n * 64 : n * 64 + 64, a * 128 : a * 128 + 128] = zero
    low = (lax.broadcasted_iota(jnp.int32, (64, 1), 0) & 7) != 0
    high = (lax.broadcasted_iota(jnp.int32, (64, 1), 0) & 7) != 7

    for s in range(2):
        acc, pc, rows = acc_all.at[s], pc_all.at[s], rows_all.at[s]
        values = grad_t[s].astype(F32).T.astype(BF)
        for a in range(3):
            lhs[s, a * 64 : a * 64 + 512, a * 128 : a * 128 + 128] = values
        acc[...] = jnp.zeros_like(acc)
        for b in range(3):
            part = nt(lhs[s], weight[b * 384 : b * 384 + 384, :])
            for c in range(3):
                for a in range(10):
                    at = pl.ds(8 + (a * 10 + b) * 8, 64)
                    acc[c, at, :] += part[a * 64 : a * 64 + 64, c * 128 : c * 128 + 128]

        def middle(row, size):
            at = 8 + row
            total = acc[1, pl.ds(at, size), :]
            total = total + jnp.where(high[:size], acc[0, pl.ds(at + 1, size), :], 0.0)
            return total + jnp.where(low[:size], acc[2, pl.ds(at - 1, size), :], 0.0)

        for a in range(8):
            own[s, pl.ds(a * 64, 64), :] = middle(((a + 1) * 10 + 1) * 8, 64)
            for d, b in (((0, -1, 0), 0), ((0, 1, 0), 9)):
                pc[pl.ds(PIECE[d] + 8 * a, 8), :] = middle(((a + 1) * 10 + b) * 8, 8)
        for a, x in ((-1, 0), (1, 9)):
            pc[pl.ds(PIECE[a, 0, 0], 64), :] = middle((x * 10 + 1) * 8, 64)
            for b, y in ((-1, 0), (1, 9)):
                pc[pl.ds(PIECE[a, b, 0], 8), :] = middle((x * 10 + y) * 8, 8)
        for c, ref, lane in ((-1, acc.at[0], 8), (1, acc.at[2], 15)):
            for a in range(8):
                pc[pl.ds(PIECE[0, 0, c] + 8 * a, 8), :] = ref[
                    pl.ds(((a + 1) * 10 + 1) * 8 + lane, 8, stride=8), :
                ]
            for a, x in ((-1, 0), (1, 9)):
                pc[pl.ds(PIECE[a, 0, c], 8), :] = ref[pl.ds((x * 10 + 1) * 8 + lane, 8, stride=8), :]
                pc[pl.ds(PIECE[0, a, c], 8), :] = ref[pl.ds((10 + x) * 8 + lane, 8, stride=80), :]
                for b, y in ((-1, 0), (1, 9)):
                    pc[pl.ds(PIECE[a, b, c], 1), :] = ref[pl.ds((x * 10 + y) * 8 + lane, 1), :]
        to_shares(pc, rows)
        msg[:, 16 * s : 16 * s + 16, :] = rows[...].astype(BF).reshape(32, 16, 128)


def join_kernel(terms, own, away1, away2, away3, msg):
    msg[:, 0:32, :] = terms[...]
    total = own[...] + away1[...].astype(F32) + away2[...].astype(F32) + away3[...].astype(F32)
    msg[:, 32:48, :] = total.astype(BF).reshape(32, 16, 128)


def merge_kernel(got, named, out, hot):
    same = same_part()
    zero = jnp.zeros((16, 128), BF)
    share = jnp.sum(got[:, 32:48, :].astype(F32), axis=0).astype(BF)
    out[:, 32:48, :] = jnp.broadcast_to(share[None], (32, 16, 128))
    second = lax.broadcasted_iota(jnp.int32, (16, 128), 0) >> 3
    split = [split_parts(got, s) for s in range(2)]
    totals = []
    for h in range(2):
        for n in range(4):
            asked = named[h, :, n * 128 : n * 128 + 128]
            for pair in range(32):
                here = (second + 2 * pair).astype(F32).astype(BF)
                hot[h, pair * 16 : pair * 16 + 16, n * 128 : n * 128 + 128] = jnp.where(
                    asked == here, same, zero
                )
        held = [x[h].reshape(256, 128) for x in split]
        totals.append(nn(hot[h], jnp.concatenate(held, axis=0).astype(BF)).reshape(64, 8, 128))
    total = jnp.concatenate(totals, axis=1).astype(BF)
    out[:, 0:32, :] = total.reshape(32, 32, 128)


def finish_kernel(flags, got, own, gout, out, rows, pc, total):
    for s in range(2):
        live = flags[s : s + 1, 0:1]
        rows[...] = got[:, 16 * s : 16 * s + 16, :].reshape(512, 128).astype(F32)
        to_pieces(rows, pc)
        total[...] = own[s]
        for d in OFFSETS:
            for at, first, size, stride in voxel_runs(d):
                where = run(first, size, stride)
                total[where, :] = total[where, :] + pc[pl.ds(PIECE[d] + at, size), :]
        out[s] = (total[...].T + gout[s].astype(F32) * live).astype(BF)


def assemble_kernel(flip, core, line, *refs):
    parts, (conv, up, down, held, sems) = refs[:4], refs[-5:]
    half = core[0] ^ flip

    def moves(n, first):
        def copy(src, dst, k):
            return pltpu.make_async_copy(src, dst, sems.at[n, k])

        block = held.at[n]
        return (
            (first < 24, lambda: [copy(block, conv.at[pl.ds(first, 4)], 0)]),
            (
                first == 24,
                lambda: [
                    copy(block.at[0:3], conv.at[pl.ds(24, 3)], 0),
                    copy(block.at[3], up.at[:, pl.ds(0, 128)], 1),
                ],
            ),
            (
                first == 28,
                lambda: [
                    copy(block.at[0], up.at[:, pl.ds(128, 128)], 0),
                    copy(block.at[1], down.at[pl.ds(0, 128), :], 1),
                    copy(block.at[2], down.at[pl.ds(128, 128), :], 2),
                ],
            ),
        )

    firsts = [half * 16 + ((line[0] + n) & 3) * 4 for n in range(4)]
    for n, part in enumerate(parts):
        held[n] = part[...].astype(F32).reshape(4, 128, 128)
        for when, copies in moves(n, firsts[n]):

            @pl.when(when)
            def _():
                for copy in copies():
                    copy.start()

    for n in range(4):
        for when, copies in moves(n, firsts[n]):

            @pl.when(when)
            def _():
                for copy in copies():
                    copy.wait()


VM = pl.BlockSpec(memory_space=pltpu.VMEM)
SM = pl.BlockSpec(memory_space=pltpu.SMEM)


HB = pl.BlockSpec(memory_space=pltpu.HBM)


def call(
    kernel, shapes, scalars, arrays, scratch=(), flops=1e6, limit=24, ins=None, outs=None,
    alias=None, name=None,
):
    moved = sum(x.size * x.dtype.itemsize for x in arrays)
    moved += sum(int(np.prod(s.shape)) * s.dtype.itemsize for s in shapes)
    return pl.pallas_call(
        kernel,
        out_shape=shapes,
        in_specs=[SM] * len(scalars) + (ins or [VM] * len(arrays)),
        out_specs=outs or [VM] * len(shapes),
        input_output_aliases=alias or {},
        scratch_shapes=list(scratch),
        compiler_params=pltpu.CompilerParams(vmem_limit_bytes=limit * 2**20),
        cost_estimate=pl.CostEstimate(
            flops=int(flops), bytes_accessed=int(moved), transcendentals=0
        ),
        name=name,
    )(*scalars, *arrays)


def shape(dims, dtype):
    return jax.ShapeDtypeStruct(dims, dtype)


def on_device(
    features,
    grad_out,
    conv_weight,
    coarse_up,
    coarse_down,
    counts,
    neighbour_owner,
    neighbour_slot,
    parent,
    child_slot,
):
    grp = lax.axis_index("grp").astype(jnp.int32)
    core = (grp & 1).reshape(1)
    line = (grp >> 1).reshape(1)
    swap = [(i, i ^ 1) for i in range(8)]
    slots = lax.broadcasted_iota(jnp.int32, (8, 128), 0)
    flags = (slots < counts[0]).astype(F32)
    (msg,) = call(
        ask_kernel,
        [shape((32, 32, 128), BF)],
        [],
        [features, neighbour_owner, neighbour_slot, jnp.asarray(choice_table(), BF)],
        [
            pltpu.VMEM((2, 128, 512), BF),
            pltpu.VMEM((2, 26), jnp.int32),
            pltpu.VMEM((2, 26), jnp.int32),
            pltpu.VMEM((128, 1024), BF),
            pltpu.VMEM((16, 128), F32),
            pltpu.VMEM((2, 8, 128), F32),
            pltpu.VMEM((2, 512, 128), F32),
            pltpu.VMEM((2, 512, 128), F32),
            pltpu.VMEM((2, 512, 128), F32),
            pltpu.VMEM((32, 32, 128), BF),
            pltpu.SemaphoreType.DMA((7,)),
        ],
        flops=2e6,
        limit=60,
        ins=[HB] * 3 + [pl.BlockSpec(memory_space=pl.ANY)],
        outs=[HB],
        name="ask",
    )
    first = lax.all_to_all(msg, "dev", split_axis=0, concat_axis=0, tiled=True)
    answer, table = call(
        route_kernel,
        [shape((32, 32, 128), BF), shape((2, 16, 512), BF)],
        [],
        [first],
        [pltpu.VMEM((2, 512, 512), BF)],
        flops=3e8,
        name="route",
    )
    halo = lax.all_to_all(answer, "dev", split_axis=0, concat_axis=0, tiled=True)
    weight = conv_weight.reshape(3, 1152, 128)
    weight = jnp.concatenate([weight[0], weight[1], weight[2]], axis=1)
    coarse = jnp.concatenate([jnp.pad(coarse_up, ((0, 128), (0, 0))), coarse_down], axis=1)
    weight = jnp.concatenate([weight, coarse], axis=0)
    output, grad_pre, wsum, send = call(
        forward_kernel,
        [
            shape((2, 128, 512), BF),
            shape((2, 128, 512), BF),
            shape((2048, 128), BF),
            shape((2048, 128), BF),
        ],
        [parent, child_slot, core],
        [flags, features, halo, grad_out, weight],
        [
            pltpu.VMEM((2, 512, 128), F32),
            pltpu.VMEM((2, 512, 128), F32),
            pltpu.VMEM((2, 512, 128), F32),
            pltpu.VMEM((2, 800, 128), F32),
            pltpu.VMEM((2, 816, 128), F32),
            pltpu.VMEM((2, 800, 128), F32),
            pltpu.VMEM((1280, 1152), BF),
            pltpu.VMEM((16, 128), F32),
            pltpu.VMEM((2, 16, 128), F32),
            pltpu.VMEM((2, 128, 512), BF),
            pltpu.VMEM((4096, 128), BF),
            pltpu.SemaphoreType.DMA((1,)),
        ],
        flops=2e9,
        outs=[HB, VM, VM, VM],
        name="forward",
    )
    other = lax.ppermute(send, "grp", swap)
    own_sum, *away, grad_pre = call(
        pair_kernel,
        [shape((512, 128), F32)] + [shape((512, 128), BF)] * 3 + [shape((2, 128, 512), BF)],
        [core, line],
        [wsum, other, grad_pre],
        name="pair",
    )
    away = [
        lax.ppermute(away[step - 1], "grp", [(i, (i + 2 * step) % 8) for i in range(8)])
        for step in (1, 3, 2)
    ]
    own, terms = call(
        backward_kernel,
        [shape((2, 512, 128), F32), shape((32, 32, 128), BF)],
        [],
        [grad_pre, weight],
        [
            pltpu.VMEM((2, 640, 384), BF),
            pltpu.VMEM((2, 3, 816, 128), F32),
            pltpu.VMEM((2, 512, 128), F32),
            pltpu.VMEM((2, 512, 128), F32),
        ],
        flops=4e9,
        name="backward",
    )
    (terms,) = call(
        join_kernel, [shape((32, 48, 128), BF)], [], [terms, own_sum, *away], name="join"
    )
    terms = lax.all_to_all(terms, "dev", split_axis=0, concat_axis=0, tiled=True)
    (sums,) = call(
        merge_kernel,
        [shape((32, 48, 128), BF)],
        [],
        [terms, table],
        [pltpu.VMEM((2, 512, 512), BF)],
        flops=3e8,
        name="merge",
    )
    back = lax.all_to_all(sums, "dev", split_axis=0, concat_axis=0, tiled=True)
    chunk = back[:, 32:48, :].reshape(512, 128)
    parts = {
        step: lax.ppermute(chunk, "grp", [(i, (i - 2 * step) % 8) for i in range(8)])
        for step in (1, 3, 2)
    }
    (grad_features,) = call(
        finish_kernel,
        [shape((2, 128, 512), BF)],
        [],
        [flags, back, own, grad_out],
        [pltpu.VMEM((512, 128), F32)] * 3,
        flops=3e8,
        name="finish",
    )
    for step in (1, 3, 2):
        parts[step], grad_features = lax.optimization_barrier((parts[step], grad_features))
    mine = [chunk, parts[1], parts[2], parts[3]]
    others = [lax.ppermute(x, "grp", swap) for x in mine]

    def assemble(flip, pieces, held):
        return call(
            functools.partial(assemble_kernel, flip),
            [shape((27, 128, 128), F32), shape((128, 256), F32), shape((256, 128), F32)],
            [core, line],
            pieces + held,
            [pltpu.VMEM((4, 4, 128, 128), F32), pltpu.SemaphoreType.DMA((4, 3))],
            ins=[VM] * 4 + [HB] * len(held),
            outs=[HB] * 3,
            alias={6 + n: n for n in range(len(held))},
            name="assemble",
        )

    grad_conv, grad_up, grad_down = assemble(1, others, list(assemble(0, mine, [])))
    return (output, grad_features, grad_conv, grad_up, grad_down)


def solution(mesh):
    return jax.shard_map(
        on_device,
        mesh=mesh,
        in_specs=(
            P(("grp", "dev"), None, None),
            P(("grp", "dev"), None, None),
            P(),
            P(),
            P(),
            P(("grp", "dev")),
            P(("grp", "dev"), None),
            P(("grp", "dev"), None),
            P(("grp", "dev")),
            P(("grp", "dev")),
        ),
        out_specs=(P(("grp", "dev"), None, None), P(("grp", "dev"), None, None), P(), P(), P()),
        check_vma=False,
    )
```

```python
import functools

import jax
import jax.numpy as jnp
import numpy as np
from jax import lax
from jax.experimental import pallas as pl
from jax.experimental.pallas import tpu as pltpu
from jax.sharding import PartitionSpec as P

BF = jnp.bfloat16
F32 = jnp.float32

OFFSETS = [
    (a, b, c) for a in (-1, 0, 1) for b in (-1, 0, 1) for c in (-1, 0, 1) if (a, b, c) != (0, 0, 0)
]
FACES = [d for d in OFFSETS if sum(map(abs, d)) == 1]
EDGES = [d for d in OFFSETS if sum(map(abs, d)) == 2]
CORNERS = [d for d in OFFSETS if sum(map(abs, d)) == 3]
PIECE = {d: 64 * n for n, d in enumerate(FACES)}
PIECE.update({d: 384 + 8 * n for n, d in enumerate(EDGES)})
PIECE.update({d: 480 + n for n, d in enumerate(CORNERS)})


def voxel_runs(d):
    a, b, c = (7 if x < 0 else 0 for x in d)
    free = [x == 0 for x in d]
    if free == [True, True, False]:
        return [(0, c, 64, 8)]
    if free == [True, False, True]:
        return [(8 * x, x * 64 + b * 8, 8, 1) for x in range(8)]
    if free == [False, True, True]:
        return [(0, a * 64, 64, 1)]
    size = 8 if any(free) else 1
    stride = (64 if free[0] else 1) * (8 if free[1] else 1)
    return [(0, a * 64 + b * 8 + c, size, stride)]


def run(start, size, stride):
    return pl.ds(start, size) if stride == 1 else pl.ds(start, size, stride=stride)


SHARES = [((64 * f + p, 32, 2), (2 * f + p, 32, 16)) for f in range(6) for p in range(2)]
SHARES += [((384 + 32 * m, 32, 1), (12 + m, 32, 16)) for m in range(3)]


def share_directions(group):
    edges = [EDGES[4 * m + group // 2] for m in range(3)]
    return [OFFSETS.index(d) for d in [FACES[q // 2] for q in range(12)] + edges + [CORNERS[group]]]


def choice_table():
    table = np.zeros((128, 8, 128), np.float32)
    for group in range(8):
        for q, direction in enumerate(share_directions(group)):
            table[direction, group, 32 + q] = 1
    return table.reshape(128, 1024)


def few_lanes(rows):
    return lax.broadcasted_iota(jnp.int32, (rows, 128), 1) < 32


def to_pieces(rows, pieces):
    for there, here in SHARES:
        pieces[run(*there), :] = rows[run(*here), :]
    total = jnp.zeros((8, 128), F32)
    for n in range(4):
        part = jnp.where(few_lanes(8), rows[pl.ds(15 + 16 * n, 8, stride=64), :], 0.0)
        total = total + (pltpu.roll(part, 32 * n, 1) if n else part)
    pieces[pl.ds(480, 8), :] = total


def to_shares(pieces, rows, extra=None):
    for there, here in SHARES:
        rows[run(*here), :] = pieces[run(*there), :]
    for n in range(4):
        part = pieces[pl.ds(480, 8), :]
        part = pltpu.roll(part, 128 - 32 * n, 1) if n else part
        if extra is not None:
            part = jnp.where(few_lanes(8), part, extra)
        rows[pl.ds(15 + 16 * n, 8, stride=64), :] = part


def nn(x, y):
    return lax.dot_general(x, y, (((1,), (0,)), ((), ())), preferred_element_type=F32)


def nt(x, y):
    return lax.dot_general(x, y, (((1,), (1,)), ((), ())), preferred_element_type=F32)


def identity():
    rows = lax.broadcasted_iota(jnp.int32, (128, 128), 0)
    lanes = lax.broadcasted_iota(jnp.int32, (128, 128), 1)
    return (rows == lanes).astype(F32).astype(BF)


def pool_rows(s):
    rows = lax.broadcasted_iota(jnp.int32, (16, 512), 0) - 8 * s
    lanes = lax.broadcasted_iota(jnp.int32, (16, 512), 1)
    block = ((lanes >> 8) & 1) * 4 + ((lanes >> 5) & 1) * 2 + ((lanes >> 2) & 1)
    return (rows == block).astype(F32).astype(BF)


def pool_voxels(values, sums, first):
    for a in range(2):
        planes = values[a * 256 : a * 256 + 64]
        for n in range(1, 4):
            planes = planes + values[a * 256 + n * 64 : a * 256 + n * 64 + 64]
        for b in range(2):
            line = planes[b * 32 : b * 32 + 8]
            for n in range(1, 4):
                line = line + planes[b * 32 + n * 8 : b * 32 + n * 8 + 8]
            for c in range(2):
                at = first + 4 * a + 2 * b + c
                sums[at : at + 1, :] = jnp.sum(line[4 * c : 4 * c + 4], axis=0, keepdims=True)


def ask_kernel(
    feat, owner, slot, choice, msg,
    feat_v, owner_v, slot_v, choice_v, bricks, tables, voxels, pc, rows, msg_v, sems,
):
    pairs = (
        (owner, owner_v), (slot, slot_v), (choice, choice_v),
        (feat.at[0], feat_v.at[0]), (feat.at[1], feat_v.at[1]),
    )
    copies = [
        pltpu.make_async_copy(src, dst, sems.at[n]) for n, (src, dst) in enumerate(pairs)
    ]
    for copy in copies:
        copy.start()
    bricks[...] = jnp.zeros((16, 128), F32)
    for copy in copies[:3]:
        copy.wait()
    named = jnp.where(owner_v[...] >= 0, owner_v[...] * 2 + slot_v[...], -1)
    bricks[0:2, 0:26] = named.astype(F32)
    asked = nn(bricks[...].astype(BF), choice_v[...])
    for group in range(8):
        for s in range(2):
            tables[s, group : group + 1, :] = asked[s : s + 1, group * 128 : group * 128 + 128]
    sent = []
    for s in range(2):
        copies[3 + s].wait()
        voxels[s] = feat_v[s].astype(F32).T
        for d in OFFSETS:
            for at, first, size, stride in voxel_runs(d):
                pc[s, pl.ds(PIECE[d] + at, size), :] = voxels.at[s][run(first, size, stride), :]
        to_shares(pc.at[s], rows.at[s], tables[s])
        at = pl.ds(16 * s, 16)
        msg_v[:, at, :] = rows[s].astype(BF).reshape(32, 16, 128)
        sent.append(pltpu.make_async_copy(msg_v.at[:, at, :], msg.at[:, at, :], sems.at[5 + s]))
        sent[-1].start()
    for copy in sent:
        copy.wait()


def same_part():
    rows = lax.broadcasted_iota(jnp.int32, (16, 128), 0) & 7
    lanes = lax.broadcasted_iota(jnp.int32, (16, 128), 1) & 7
    return (rows == lanes).astype(F32).astype(BF)


def split_parts(got, s):
    rows = got[:, 16 * s : 16 * s + 16, :].astype(F32)
    return rows[:, 0:8, :], rows[:, 8:16, :]


def route_kernel(got, out, named, hot):
    same = jnp.broadcast_to(same_part()[None], (16, 16, 128))
    zero = jnp.zeros((16, 16, 128), BF)
    ones = jnp.ones((128, 128), BF)
    part = lax.broadcasted_iota(jnp.int32, (8, 128), 0)
    lanes = lax.broadcasted_iota(jnp.int32, (8, 128), 1)
    brick = lax.broadcasted_iota(jnp.int32, (16, 128), 1) >> 3
    split = [split_parts(got, s) for s in range(2)]
    answers = []
    for h in range(2):
        for s in range(2):
            table = jnp.broadcast_to(split[s][1][:, 7:8, :], (32, 8, 128))
            table = jnp.where((lanes == part + 32 + 8 * h)[None], table, 0.0)
            asked = nn(table.reshape(256, 128).astype(BF), ones)
            named[h, :, s * 256 : s * 256 + 256] = asked.T[0:16].astype(BF)
            asked = asked.astype(BF).reshape(16, 16, 128)
            for n in range(4):
                here = (brick + 16 * n).astype(F32).astype(BF)
                picked = jnp.where(asked == here[None], same, zero).reshape(256, 128)
                hot[h, s * 256 : s * 256 + 256, n * 128 : n * 128 + 128] = picked
        held = jnp.stack([split[0][h], split[1][h]], axis=1).reshape(512, 128).astype(BF)
        answers.append(nn(hot[h], held))
    for s in range(2):
        rows = [x[s * 256 : s * 256 + 256].reshape(32, 8, 128) for x in answers]
        out[:, 16 * s : 16 * s + 16, :] = jnp.concatenate(rows, axis=1).astype(BF)


def forward_kernel(
    parent, child, core, flags, feat, got, gout, weight,
    out, grad_t, keep, send,
    rows_all, pc_all, s0_all, s1_all, s2_all, cols, pooled, grad_pooled, out_v, wsum, sem,
):
    eye = identity()
    up, down = weight[1152:1280, 0:256], weight[1152:1408, 256:384]
    acts, slopes = [], []
    for s in range(2):
        rows, pc, s0, s1, s2 = (x.at[s] for x in (rows_all, pc_all, s0_all, s1_all, s2_all))
        live = flags[s : s + 1, 0:1]
        pool = pool_rows(s)
        mine = (feat[s].astype(F32) * live).T
        grad_pooled[s] = nt(pool, gout[s]) * live
        rows[...] = got[:, 16 * s : 16 * s + 16, :].reshape(512, 128).astype(F32)
        to_pieces(rows, pc)
        for a in range(8):
            s1[pl.ds(8 + ((a + 1) * 10 + 1) * 8, 64), :] = mine[a * 64 : a * 64 + 64]
            for d, b in (((0, -1, 0), 0), ((0, 1, 0), 9)):
                s1[pl.ds(8 + ((a + 1) * 10 + b) * 8, 8), :] = pc[pl.ds(PIECE[d] + 8 * a, 8), :]
        for a, x in ((-1, 0), (1, 9)):
            s1[pl.ds(8 + (x * 10 + 1) * 8, 64), :] = pc[pl.ds(PIECE[a, 0, 0], 64), :]
            for b, y in ((-1, 0), (1, 9)):
                s1[pl.ds(8 + (x * 10 + y) * 8, 8), :] = pc[pl.ds(PIECE[a, b, 0], 8), :]
        s0[...] = s1[pl.ds(7, 800), :]
        s2[...] = s1[pl.ds(9, 800), :]
        for c, ref, lane in ((-1, s0, 0), (1, s2, 7)):
            for a in range(8):
                ref[pl.ds(((a + 1) * 10 + 1) * 8 + lane, 8, stride=8), :] = pc[
                    pl.ds(PIECE[0, 0, c] + 8 * a, 8), :
                ]
            for a, x in ((-1, 0), (1, 9)):
                ref[pl.ds((x * 10 + 1) * 8 + lane, 8, stride=8), :] = pc[
                    pl.ds(PIECE[a, 0, c], 8), :
                ]
                ref[pl.ds((10 + x) * 8 + lane, 8, stride=80), :] = pc[pl.ds(PIECE[0, a, c], 8), :]
                for b, y in ((-1, 0), (1, 9)):
                    ref[pl.ds((x * 10 + y) * 8 + lane, 1), :] = pc[pl.ds(PIECE[a, b, c], 1), :]
        for a in range(10):
            for b in range(3):
                for c, ref in enumerate((s0, s1, s2)):
                    start = (a * 10 + b) * 8 + (8 if c == 1 else 0)
                    at = 640 * s + 64 * a
                    cols[at : at + 64, (3 * b + c) * 128 : (3 * b + c) * 128 + 128] = ref[
                        pl.ds(start, 64), :
                    ].astype(BF)
    pres = []
    for s in range(2):
        taps = nn(cols[640 * s : 640 * s + 640, :], weight[0:1152, :])
        pre = taps[0:512, 0:128] + taps[64:576, 128:256] + taps[128:640, 256:384]
        pres.append(pre)
    for s in range(2):
        pre = pres[s]
        pool_voxels(pre * (1.0 / (1.0 + jnp.exp(-pre))), pooled, 8 * s)
        pre = pre.T
        gate = 1.0 / (1.0 + jnp.exp(-pre))
        acts.append(pre * gate)
        slopes.append(gate * (1.0 + pre * (1.0 - gate)))
    second = lax.broadcasted_iota(jnp.int32, (16, 1), 0) >= 8
    valid = [
        ((parent[s] >= 0) & (parent[s] * 64 + child[s] >= 0)).astype(F32) * flags[s : s + 1, 0:1]
        for s in range(2)
    ]
    valid = jnp.where(second, valid[1], valid[0])
    coarse_in = (pooled[...] * (1.0 / 64.0) * valid).astype(BF)
    grad_out = ((grad_pooled[0] + grad_pooled[1]) * valid).astype(BF)
    coarse_pre = nn(coarse_in, up)
    gate = 1.0 / (1.0 + jnp.exp(-coarse_pre))
    coarse_mid = (coarse_pre * gate).astype(BF)
    grad_pre = nt(grad_out, down) * (gate * (1.0 + coarse_pre * (1.0 - gate)))
    grad_pre = grad_pre.astype(BF)
    coarse_out = nn(coarse_mid, down).astype(BF)
    grad_cin = nt(grad_pre, up).astype(BF)
    lift = nt(eye, coarse_out).astype(BF)
    back = nt(eye, grad_cin).astype(BF)
    for s in range(2):
        live = flags[s : s + 1, 0:1]
        pool = pool_rows(s)
        grad_in = gout[s].astype(F32) * live + nn(back, pool) * (1.0 / 64.0)
        grad_t[s] = (grad_in * slopes[s]).astype(BF)
        out_v[s] = (feat[s].astype(F32) * live + acts[s] + nn(lift, pool)).astype(BF)
    copy = pltpu.make_async_copy(out_v, out, sem.at[0])
    copy.start()

    def put(block, value):
        wsum[pl.ds(block * 128, 128), :] = value.astype(BF)

    grad_up = nn(nt(eye, coarse_in).astype(BF), grad_pre)
    for h in range(2):
        put(27 + h, grad_up[:, h * 128 : h * 128 + 128])
        middle = nt(eye, coarse_mid[:, h * 128 : h * 128 + 128]).astype(BF)
        put(29 + h, nn(middle, grad_out))
    put(31, jnp.zeros((128, 128), F32))
    for a in range(3):
        total = nn(grad_t[0], cols[64 * a : 64 * a + 512, :])
        total = total + nn(grad_t[1], cols[64 * a + 640 : 64 * a + 1152, :])
        for n in range(9):
            put(9 * a + n, total[:, n * 128 : n * 128 + 128].T)
    send[...] = wsum[pl.ds(pl.multiple_of((1 - core[0]) * 2048, 2048), 2048), :]
    keep[...] = wsum[pl.ds(pl.multiple_of(core[0] * 2048, 2048), 2048), :]
    copy.wait()


def pair_kernel(core, line, wsum, other, grad, own, one, two, three, held):
    held[...] = grad[...]
    for step, ref in enumerate((own, one, two, three)):
        at = pl.multiple_of(((line[0] + step) & 3) * 512, 512)
        kept = wsum[pl.ds(at, 512), :].astype(F32)
        ref[...] = (kept + other[pl.ds(at, 512), :].astype(F32)).astype(ref.dtype)


def backward_kernel(grad_t, weight, own, msg, lhs, acc_all, pc_all, rows_all):
    zero = jnp.zeros((64, 128), BF)
    for a in range(3):
        for n in [*range(a), *range(8 + a, 10)]:
            for s in range(2):
                lhs[s, n * 64 : n * 64 + 64, a * 128 : a * 128 + 128] = zero
    low = (lax.broadcasted_iota(jnp.int32, (64, 1), 0) & 7) != 0
    high = (lax.broadcasted_iota(jnp.int32, (64, 1), 0) & 7) != 7

    for s in range(2):
        acc, pc, rows = acc_all.at[s], pc_all.at[s], rows_all.at[s]
        values = grad_t[s].astype(F32).T.astype(BF)
        for a in range(3):
            lhs[s, a * 64 : a * 64 + 512, a * 128 : a * 128 + 128] = values
        acc[...] = jnp.zeros_like(acc)
        for b in range(3):
            part = nt(lhs[s], weight[b * 384 : b * 384 + 384, :])
            for c in range(3):
                for a in range(10):
                    at = pl.ds(8 + (a * 10 + b) * 8, 64)
                    acc[c, at, :] += part[a * 64 : a * 64 + 64, c * 128 : c * 128 + 128]

        def middle(row, size):
            at = 8 + row
            total = acc[1, pl.ds(at, size), :]
            total = total + jnp.where(high[:size], acc[0, pl.ds(at + 1, size), :], 0.0)
            return total + jnp.where(low[:size], acc[2, pl.ds(at - 1, size), :], 0.0)

        for a in range(8):
            own[s, pl.ds(a * 64, 64), :] = middle(((a + 1) * 10 + 1) * 8, 64)
            for d, b in (((0, -1, 0), 0), ((0, 1, 0), 9)):
                pc[pl.ds(PIECE[d] + 8 * a, 8), :] = middle(((a + 1) * 10 + b) * 8, 8)
        for a, x in ((-1, 0), (1, 9)):
            pc[pl.ds(PIECE[a, 0, 0], 64), :] = middle((x * 10 + 1) * 8, 64)
            for b, y in ((-1, 0), (1, 9)):
                pc[pl.ds(PIECE[a, b, 0], 8), :] = middle((x * 10 + y) * 8, 8)
        for c, ref, lane in ((-1, acc.at[0], 8), (1, acc.at[2], 15)):
            for a in range(8):
                pc[pl.ds(PIECE[0, 0, c] + 8 * a, 8), :] = ref[
                    pl.ds(((a + 1) * 10 + 1) * 8 + lane, 8, stride=8), :
                ]
            for a, x in ((-1, 0), (1, 9)):
                pc[pl.ds(PIECE[a, 0, c], 8), :] = ref[pl.ds((x * 10 + 1) * 8 + lane, 8, stride=8), :]
                pc[pl.ds(PIECE[0, a, c], 8), :] = ref[pl.ds((10 + x) * 8 + lane, 8, stride=80), :]
                for b, y in ((-1, 0), (1, 9)):
                    pc[pl.ds(PIECE[a, b, c], 1), :] = ref[pl.ds((x * 10 + y) * 8 + lane, 1), :]
        to_shares(pc, rows)
        msg[:, 16 * s : 16 * s + 16, :] = rows[...].astype(BF).reshape(32, 16, 128)


def join_kernel(terms, own, away1, away2, away3, msg):
    msg[:, 0:32, :] = terms[...]
    total = own[...] + away1[...].astype(F32) + away2[...].astype(F32) + away3[...].astype(F32)
    msg[:, 32:48, :] = total.astype(BF).reshape(32, 16, 128)


def merge_kernel(got, named, out, hot):
    same = same_part()
    zero = jnp.zeros((16, 128), BF)
    share = jnp.sum(got[:, 32:48, :].astype(F32), axis=0).astype(BF)
    out[:, 32:48, :] = jnp.broadcast_to(share[None], (32, 16, 128))
    second = lax.broadcasted_iota(jnp.int32, (16, 128), 0) >> 3
    split = [split_parts(got, s) for s in range(2)]
    totals = []
    for h in range(2):
        for n in range(4):
            asked = named[h, :, n * 128 : n * 128 + 128]
            for pair in range(32):
                here = (second + 2 * pair).astype(F32).astype(BF)
                hot[h, pair * 16 : pair * 16 + 16, n * 128 : n * 128 + 128] = jnp.where(
                    asked == here, same, zero
                )
        held = [x[h].reshape(256, 128) for x in split]
        totals.append(nn(hot[h], jnp.concatenate(held, axis=0).astype(BF)).reshape(64, 8, 128))
    total = jnp.concatenate(totals, axis=1).astype(BF)
    out[:, 0:32, :] = total.reshape(32, 32, 128)


def finish_kernel(flags, got, own, gout, out, rows, pc, total):
    for s in range(2):
        live = flags[s : s + 1, 0:1]
        rows[...] = got[:, 16 * s : 16 * s + 16, :].reshape(512, 128).astype(F32)
        to_pieces(rows, pc)
        total[...] = own[s]
        for d in OFFSETS:
            for at, first, size, stride in voxel_runs(d):
                where = run(first, size, stride)
                total[where, :] = total[where, :] + pc[pl.ds(PIECE[d] + at, size), :]
        out[s] = (total[...].T + gout[s].astype(F32) * live).astype(BF)


def assemble_kernel(flip, core, line, *refs):
    parts, (conv, up, down, held, sems) = refs[:4], refs[-5:]
    half = core[0] ^ flip

    def moves(n, first):
        def copy(src, dst, k):
            return pltpu.make_async_copy(src, dst, sems.at[n, k])

        block = held.at[n]
        return (
            (first < 24, lambda: [copy(block, conv.at[pl.ds(first, 4)], 0)]),
            (
                first == 24,
                lambda: [
                    copy(block.at[0:3], conv.at[pl.ds(24, 3)], 0),
                    copy(block.at[3], up.at[:, pl.ds(0, 128)], 1),
                ],
            ),
            (
                first == 28,
                lambda: [
                    copy(block.at[0], up.at[:, pl.ds(128, 128)], 0),
                    copy(block.at[1], down.at[pl.ds(0, 128), :], 1),
                    copy(block.at[2], down.at[pl.ds(128, 128), :], 2),
                ],
            ),
        )

    firsts = [half * 16 + ((line[0] + n) & 3) * 4 for n in range(4)]
    for n, part in enumerate(parts):
        held[n] = part[...].astype(F32).reshape(4, 128, 128)
        for when, copies in moves(n, firsts[n]):

            @pl.when(when)
            def _():
                for copy in copies():
                    copy.start()

    for n in range(4):
        for when, copies in moves(n, firsts[n]):

            @pl.when(when)
            def _():
                for copy in copies():
                    copy.wait()


VM = pl.BlockSpec(memory_space=pltpu.VMEM)
SM = pl.BlockSpec(memory_space=pltpu.SMEM)


HB = pl.BlockSpec(memory_space=pltpu.HBM)


def call(
    kernel, shapes, scalars, arrays, scratch=(), flops=1e6, limit=24, ins=None, outs=None,
    alias=None, name=None,
):
    moved = sum(x.size * x.dtype.itemsize for x in arrays)
    moved += sum(int(np.prod(s.shape)) * s.dtype.itemsize for s in shapes)
    return pl.pallas_call(
        kernel,
        out_shape=shapes,
        in_specs=[SM] * len(scalars) + (ins or [VM] * len(arrays)),
        out_specs=outs or [VM] * len(shapes),
        input_output_aliases=alias or {},
        scratch_shapes=list(scratch),
        compiler_params=pltpu.CompilerParams(vmem_limit_bytes=limit * 2**20),
        cost_estimate=pl.CostEstimate(
            flops=int(flops), bytes_accessed=int(moved), transcendentals=0
        ),
        name=name,
    )(*scalars, *arrays)


def shape(dims, dtype):
    return jax.ShapeDtypeStruct(dims, dtype)


def on_device(
    features,
    grad_out,
    conv_weight,
    coarse_up,
    coarse_down,
    counts,
    neighbour_owner,
    neighbour_slot,
    parent,
    child_slot,
):
    grp = lax.axis_index("grp").astype(jnp.int32)
    core = (grp & 1).reshape(1)
    line = (grp >> 1).reshape(1)
    swap = [(i, i ^ 1) for i in range(8)]
    slots = lax.broadcasted_iota(jnp.int32, (8, 128), 0)
    flags = (slots < counts[0]).astype(F32)
    (msg,) = call(
        ask_kernel,
        [shape((32, 32, 128), BF)],
        [],
        [features, neighbour_owner, neighbour_slot, jnp.asarray(choice_table(), BF)],
        [
            pltpu.VMEM((2, 128, 512), BF),
            pltpu.VMEM((2, 26), jnp.int32),
            pltpu.VMEM((2, 26), jnp.int32),
            pltpu.VMEM((128, 1024), BF),
            pltpu.VMEM((16, 128), F32),
            pltpu.VMEM((2, 8, 128), F32),
            pltpu.VMEM((2, 512, 128), F32),
            pltpu.VMEM((2, 512, 128), F32),
            pltpu.VMEM((2, 512, 128), F32),
            pltpu.VMEM((32, 32, 128), BF),
            pltpu.SemaphoreType.DMA((7,)),
        ],
        flops=2e6,
        limit=60,
        ins=[HB] * 3 + [pl.BlockSpec(memory_space=pl.ANY)],
        outs=[HB],
        name="ask",
    )
    first = lax.all_to_all(msg, "dev", split_axis=0, concat_axis=0, tiled=True)
    answer, table = call(
        route_kernel,
        [shape((32, 32, 128), BF), shape((2, 16, 512), BF)],
        [],
        [first],
        [pltpu.VMEM((2, 512, 512), BF)],
        flops=3e8,
        name="route",
    )
    halo = lax.all_to_all(answer, "dev", split_axis=0, concat_axis=0, tiled=True)
    weight = conv_weight.reshape(3, 1152, 128)
    weight = jnp.concatenate([weight[0], weight[1], weight[2]], axis=1)
    coarse = jnp.concatenate([jnp.pad(coarse_up, ((0, 128), (0, 0))), coarse_down], axis=1)
    weight = jnp.concatenate([weight, coarse], axis=0)
    output, grad_pre, wsum, send = call(
        forward_kernel,
        [
            shape((2, 128, 512), BF),
            shape((2, 128, 512), BF),
            shape((2048, 128), BF),
            shape((2048, 128), BF),
        ],
        [parent, child_slot, core],
        [flags, features, halo, grad_out, weight],
        [
            pltpu.VMEM((2, 512, 128), F32),
            pltpu.VMEM((2, 512, 128), F32),
            pltpu.VMEM((2, 800, 128), F32),
            pltpu.VMEM((2, 816, 128), F32),
            pltpu.VMEM((2, 800, 128), F32),
            pltpu.VMEM((1280, 1152), BF),
            pltpu.VMEM((16, 128), F32),
            pltpu.VMEM((2, 16, 128), F32),
            pltpu.VMEM((2, 128, 512), BF),
            pltpu.VMEM((4096, 128), BF),
            pltpu.SemaphoreType.DMA((1,)),
        ],
        flops=2e9,
        outs=[HB, VM, VM, VM],
        name="forward",
    )
    other = lax.ppermute(send, "grp", swap)
    own_sum, *away, grad_pre = call(
        pair_kernel,
        [shape((512, 128), F32)] + [shape((512, 128), BF)] * 3 + [shape((2, 128, 512), BF)],
        [core, line],
        [wsum, other, grad_pre],
        name="pair",
    )
    away = [
        lax.ppermute(away[step - 1], "grp", [(i, (i + 2 * step) % 8) for i in range(8)])
        for step in (1, 3, 2)
    ]
    own, terms = call(
        backward_kernel,
        [shape((2, 512, 128), F32), shape((32, 32, 128), BF)],
        [],
        [grad_pre, weight],
        [
            pltpu.VMEM((2, 640, 384), BF),
            pltpu.VMEM((2, 3, 816, 128), F32),
            pltpu.VMEM((2, 512, 128), F32),
            pltpu.VMEM((2, 512, 128), F32),
        ],
        flops=4e9,
        name="backward",
    )
    (terms,) = call(
        join_kernel, [shape((32, 48, 128), BF)], [], [terms, own_sum, *away], name="join"
    )
    terms = lax.all_to_all(terms, "dev", split_axis=0, concat_axis=0, tiled=True)
    (sums,) = call(
        merge_kernel,
        [shape((32, 48, 128), BF)],
        [],
        [terms, table],
        [pltpu.VMEM((2, 512, 512), BF)],
        flops=3e8,
        name="merge",
    )
    back = lax.all_to_all(sums, "dev", split_axis=0, concat_axis=0, tiled=True)
    chunk = back[:, 32:48, :].reshape(512, 128)
    parts = {
        step: lax.ppermute(chunk, "grp", [(i, (i - 2 * step) % 8) for i in range(8)])
        for step in (1, 3, 2)
    }
    (grad_features,) = call(
        finish_kernel,
        [shape((2, 128, 512), BF)],
        [],
        [flags, back, own, grad_out],
        [pltpu.VMEM((512, 128), F32)] * 3,
        flops=3e8,
        name="finish",
    )
    for step in (1, 3, 2):
        parts[step], grad_features = lax.optimization_barrier((parts[step], grad_features))
    mine = [chunk, parts[1], parts[2], parts[3]]
    others = [lax.ppermute(x, "grp", swap) for x in mine]

    def assemble(flip, pieces, held):
        return call(
            functools.partial(assemble_kernel, flip),
            [shape((27, 128, 128), F32), shape((128, 256), F32), shape((256, 128), F32)],
            [core, line],
            pieces + held,
            [pltpu.VMEM((4, 4, 128, 128), F32), pltpu.SemaphoreType.DMA((4, 3))],
            ins=[VM] * 4 + [HB] * len(held),
            outs=[HB] * 3,
            alias={6 + n: n for n in range(len(held))},
            name="assemble",
        )

    grad_conv, grad_up, grad_down = assemble(1, others, list(assemble(0, mine, [])))
    return (output, grad_features, grad_conv, grad_up, grad_down)


def solution(mesh):
    return jax.shard_map(
        on_device,
        mesh=mesh,
        in_specs=(
            P(("grp", "dev"), None, None),
            P(("grp", "dev"), None, None),
            P(),
            P(),
            P(),
            P(("grp", "dev")),
            P(("grp", "dev"), None),
            P(("grp", "dev"), None),
            P(("grp", "dev")),
            P(("grp", "dev")),
        ),
        out_specs=(P(("grp", "dev"), None, None), P(("grp", "dev"), None, None), P(), P(), P()),
        check_vma=False,
    )
```

```python
import functools

import jax
import jax.numpy as jnp
import numpy as np
from jax import lax
from jax.experimental import pallas as pl
from jax.experimental.pallas import tpu as pltpu
from jax.sharding import PartitionSpec as P

BF = jnp.bfloat16
F32 = jnp.float32

OFFSETS = [
    (a, b, c) for a in (-1, 0, 1) for b in (-1, 0, 1) for c in (-1, 0, 1) if (a, b, c) != (0, 0, 0)
]
FACES = [d for d in OFFSETS if sum(map(abs, d)) == 1]
EDGES = [d for d in OFFSETS if sum(map(abs, d)) == 2]
CORNERS = [d for d in OFFSETS if sum(map(abs, d)) == 3]
PIECE = {d: 64 * n for n, d in enumerate(FACES)}
PIECE.update({d: 384 + 8 * n for n, d in enumerate(EDGES)})
PIECE.update({d: 480 + n for n, d in enumerate(CORNERS)})


def voxel_runs(d):
    a, b, c = (7 if x < 0 else 0 for x in d)
    free = [x == 0 for x in d]
    if free == [True, True, False]:
        return [(0, c, 64, 8)]
    if free == [True, False, True]:
        return [(8 * x, x * 64 + b * 8, 8, 1) for x in range(8)]
    if free == [False, True, True]:
        return [(0, a * 64, 64, 1)]
    size = 8 if any(free) else 1
    stride = (64 if free[0] else 1) * (8 if free[1] else 1)
    return [(0, a * 64 + b * 8 + c, size, stride)]


def run(start, size, stride):
    return pl.ds(start, size) if stride == 1 else pl.ds(start, size, stride=stride)


SHARES = [((64 * f + p, 32, 2), (2 * f + p, 32, 16)) for f in range(6) for p in range(2)]
SHARES += [((384 + 32 * m, 32, 1), (12 + m, 32, 16)) for m in range(3)]


def share_directions(group):
    edges = [EDGES[4 * m + group // 2] for m in range(3)]
    return [OFFSETS.index(d) for d in [FACES[q // 2] for q in range(12)] + edges + [CORNERS[group]]]


def choice_table():
    table = np.zeros((128, 8, 128), np.float32)
    for group in range(8):
        for q, direction in enumerate(share_directions(group)):
            table[direction, group, 32 + q] = 1
    return table.reshape(128, 1024)


def few_lanes(rows):
    return lax.broadcasted_iota(jnp.int32, (rows, 128), 1) < 32


def to_pieces(rows, pieces):
    for there, here in SHARES:
        pieces[run(*there), :] = rows[run(*here), :]
    total = jnp.zeros((8, 128), F32)
    for n in range(4):
        part = jnp.where(few_lanes(8), rows[pl.ds(15 + 16 * n, 8, stride=64), :], 0.0)
        total = total + (pltpu.roll(part, 32 * n, 1) if n else part)
    pieces[pl.ds(480, 8), :] = total


def to_shares(pieces, rows, extra=None):
    for there, here in SHARES:
        rows[run(*here), :] = pieces[run(*there), :]
    for n in range(4):
        part = pieces[pl.ds(480, 8), :]
        part = pltpu.roll(part, 128 - 32 * n, 1) if n else part
        if extra is not None:
            part = jnp.where(few_lanes(8), part, extra)
        rows[pl.ds(15 + 16 * n, 8, stride=64), :] = part


def nn(x, y):
    return lax.dot_general(x, y, (((1,), (0,)), ((), ())), preferred_element_type=F32)


def nt(x, y):
    return lax.dot_general(x, y, (((1,), (1,)), ((), ())), preferred_element_type=F32)


def identity():
    rows = lax.broadcasted_iota(jnp.int32, (128, 128), 0)
    lanes = lax.broadcasted_iota(jnp.int32, (128, 128), 1)
    return (rows == lanes).astype(F32).astype(BF)


def pool_rows(s):
    rows = lax.broadcasted_iota(jnp.int32, (16, 512), 0) - 8 * s
    lanes = lax.broadcasted_iota(jnp.int32, (16, 512), 1)
    block = ((lanes >> 8) & 1) * 4 + ((lanes >> 5) & 1) * 2 + ((lanes >> 2) & 1)
    return (rows == block).astype(F32).astype(BF)


def pool_voxels(values, sums, first):
    for a in range(2):
        planes = values[a * 256 : a * 256 + 64]
        for n in range(1, 4):
            planes = planes + values[a * 256 + n * 64 : a * 256 + n * 64 + 64]
        for b in range(2):
            line = planes[b * 32 : b * 32 + 8]
            for n in range(1, 4):
                line = line + planes[b * 32 + n * 8 : b * 32 + n * 8 + 8]
            for c in range(2):
                at = first + 4 * a + 2 * b + c
                sums[at : at + 1, :] = jnp.sum(line[4 * c : 4 * c + 4], axis=0, keepdims=True)


def ask_kernel(
    feat, owner, slot, choice, msg,
    feat_v, owner_v, slot_v, choice_v, bricks, tables, voxels, pc, rows, msg_v, sems,
):
    pairs = (
        (owner, owner_v), (slot, slot_v), (choice, choice_v),
        (feat.at[0], feat_v.at[0]), (feat.at[1], feat_v.at[1]),
    )
    copies = [
        pltpu.make_async_copy(src, dst, sems.at[n]) for n, (src, dst) in enumerate(pairs)
    ]
    for n in (3, 0, 1, 2, 4):
        copies[n].start()
    bricks[...] = jnp.zeros((16, 128), F32)
    for copy in copies[:3]:
        copy.wait()
    named = jnp.where(owner_v[...] >= 0, owner_v[...] * 2 + slot_v[...], -1)
    bricks[0:2, 0:26] = named.astype(F32)
    asked = nn(bricks[...].astype(BF), choice_v[...])
    for group in range(8):
        for s in range(2):
            tables[s, group : group + 1, :] = asked[s : s + 1, group * 128 : group * 128 + 128]
    sent = []
    for s in range(2):
        copies[3 + s].wait()
        voxels[s] = feat_v[s].astype(F32).T
        for d in OFFSETS:
            for at, first, size, stride in voxel_runs(d):
                pc[s, pl.ds(PIECE[d] + at, size), :] = voxels.at[s][run(first, size, stride), :]
        to_shares(pc.at[s], rows.at[s], tables[s])
        at = pl.ds(16 * s, 16)
        msg_v[:, at, :] = rows[s].astype(BF).reshape(32, 16, 128)
        sent.append(pltpu.make_async_copy(msg_v.at[:, at, :], msg.at[:, at, :], sems.at[5 + s]))
        sent[-1].start()
    for copy in sent:
        copy.wait()


def same_part():
    rows = lax.broadcasted_iota(jnp.int32, (16, 128), 0) & 7
    lanes = lax.broadcasted_iota(jnp.int32, (16, 128), 1) & 7
    return (rows == lanes).astype(F32).astype(BF)


def split_parts(got, s):
    rows = got[:, 16 * s : 16 * s + 16, :].astype(F32)
    return rows[:, 0:8, :], rows[:, 8:16, :]


def route_kernel(got, out, named, hot):
    same = jnp.broadcast_to(same_part()[None], (16, 16, 128))
    zero = jnp.zeros((16, 16, 128), BF)
    ones = jnp.ones((128, 128), BF)
    part = lax.broadcasted_iota(jnp.int32, (8, 128), 0)
    lanes = lax.broadcasted_iota(jnp.int32, (8, 128), 1)
    brick = lax.broadcasted_iota(jnp.int32, (16, 128), 1) >> 3
    split = [split_parts(got, s) for s in range(2)]
    answers = []
    for h in range(2):
        for s in range(2):
            table = jnp.broadcast_to(split[s][1][:, 7:8, :], (32, 8, 128))
            table = jnp.where((lanes == part + 32 + 8 * h)[None], table, 0.0)
            asked = nn(table.reshape(256, 128).astype(BF), ones)
            named[h, :, s * 256 : s * 256 + 256] = asked.T[0:16].astype(BF)
            asked = asked.astype(BF).reshape(16, 16, 128)
            for n in range(4):
                here = (brick + 16 * n).astype(F32).astype(BF)
                picked = jnp.where(asked == here[None], same, zero).reshape(256, 128)
                hot[h, s * 256 : s * 256 + 256, n * 128 : n * 128 + 128] = picked
        held = jnp.stack([split[0][h], split[1][h]], axis=1).reshape(512, 128).astype(BF)
        answers.append(nn(hot[h], held))
    for s in range(2):
        rows = [x[s * 256 : s * 256 + 256].reshape(32, 8, 128) for x in answers]
        out[:, 16 * s : 16 * s + 16, :] = jnp.concatenate(rows, axis=1).astype(BF)


def forward_kernel(
    parent, child, core, flags, feat, got, gout, weight,
    out, grad_t, keep, send,
    rows_all, pc_all, s0_all, s1_all, s2_all, cols, pooled, grad_pooled, out_v, wsum, sem,
):
    eye = identity()
    up, down = weight[1152:1280, 0:256], weight[1152:1408, 256:384]
    acts, slopes = [], []
    for s in range(2):
        rows, pc, s0, s1, s2 = (x.at[s] for x in (rows_all, pc_all, s0_all, s1_all, s2_all))
        live = flags[s : s + 1, 0:1]
        pool = pool_rows(s)
        mine = (feat[s].astype(F32) * live).T
        grad_pooled[s] = nt(pool, gout[s]) * live
        rows[...] = got[:, 16 * s : 16 * s + 16, :].reshape(512, 128).astype(F32)
        to_pieces(rows, pc)
        for a in range(8):
            s1[pl.ds(8 + ((a + 1) * 10 + 1) * 8, 64), :] = mine[a * 64 : a * 64 + 64]
            for d, b in (((0, -1, 0), 0), ((0, 1, 0), 9)):
                s1[pl.ds(8 + ((a + 1) * 10 + b) * 8, 8), :] = pc[pl.ds(PIECE[d] + 8 * a, 8), :]
        for a, x in ((-1, 0), (1, 9)):
            s1[pl.ds(8 + (x * 10 + 1) * 8, 64), :] = pc[pl.ds(PIECE[a, 0, 0], 64), :]
            for b, y in ((-1, 0), (1, 9)):
                s1[pl.ds(8 + (x * 10 + y) * 8, 8), :] = pc[pl.ds(PIECE[a, b, 0], 8), :]
        s0[...] = s1[pl.ds(7, 800), :]
        s2[...] = s1[pl.ds(9, 800), :]
        for c, ref, lane in ((-1, s0, 0), (1, s2, 7)):
            for a in range(8):
                ref[pl.ds(((a + 1) * 10 + 1) * 8 + lane, 8, stride=8), :] = pc[
                    pl.ds(PIECE[0, 0, c] + 8 * a, 8), :
                ]
            for a, x in ((-1, 0), (1, 9)):
                ref[pl.ds((x * 10 + 1) * 8 + lane, 8, stride=8), :] = pc[
                    pl.ds(PIECE[a, 0, c], 8), :
                ]
                ref[pl.ds((10 + x) * 8 + lane, 8, stride=80), :] = pc[pl.ds(PIECE[0, a, c], 8), :]
                for b, y in ((-1, 0), (1, 9)):
                    ref[pl.ds((x * 10 + y) * 8 + lane, 1), :] = pc[pl.ds(PIECE[a, b, c], 1), :]
        for a in range(10):
            for b in range(3):
                for c, ref in enumerate((s0, s1, s2)):
                    start = (a * 10 + b) * 8 + (8 if c == 1 else 0)
                    at = 640 * s + 64 * a
                    cols[at : at + 64, (3 * b + c) * 128 : (3 * b + c) * 128 + 128] = ref[
                        pl.ds(start, 64), :
                    ].astype(BF)
    pres = []
    for s in range(2):
        taps = nn(cols[640 * s : 640 * s + 640, :], weight[0:1152, :])
        pre = taps[0:512, 0:128] + taps[64:576, 128:256] + taps[128:640, 256:384]
        pres.append(pre)
    for s in range(2):
        pre = pres[s]
        pool_voxels(pre * (1.0 / (1.0 + jnp.exp(-pre))), pooled, 8 * s)
        pre = pre.T
        gate = 1.0 / (1.0 + jnp.exp(-pre))
        acts.append(pre * gate)
        slopes.append(gate * (1.0 + pre * (1.0 - gate)))
    second = lax.broadcasted_iota(jnp.int32, (16, 1), 0) >= 8
    valid = [
        ((parent[s] >= 0) & (parent[s] * 64 + child[s] >= 0)).astype(F32) * flags[s : s + 1, 0:1]
        for s in range(2)
    ]
    valid = jnp.where(second, valid[1], valid[0])
    coarse_in = (pooled[...] * (1.0 / 64.0) * valid).astype(BF)
    grad_out = ((grad_pooled[0] + grad_pooled[1]) * valid).astype(BF)
    coarse_pre = nn(coarse_in, up)
    gate = 1.0 / (1.0 + jnp.exp(-coarse_pre))
    coarse_mid = (coarse_pre * gate).astype(BF)
    grad_pre = nt(grad_out, down) * (gate * (1.0 + coarse_pre * (1.0 - gate)))
    grad_pre = grad_pre.astype(BF)
    coarse_out = nn(coarse_mid, down).astype(BF)
    grad_cin = nt(grad_pre, up).astype(BF)
    lift = nt(eye, coarse_out).astype(BF)
    back = nt(eye, grad_cin).astype(BF)
    for s in range(2):
        live = flags[s : s + 1, 0:1]
        pool = pool_rows(s)
        grad_in = gout[s].astype(F32) * live + nn(back, pool) * (1.0 / 64.0)
        grad_t[s] = (grad_in * slopes[s]).astype(BF)
        out_v[s] = (feat[s].astype(F32) * live + acts[s] + nn(lift, pool)).astype(BF)
    copy = pltpu.make_async_copy(out_v, out, sem.at[0])
    copy.start()

    def put(block, value):
        wsum[pl.ds(block * 128, 128), :] = value.astype(BF)

    grad_up = nn(nt(eye, coarse_in).astype(BF), grad_pre)
    for h in range(2):
        put(27 + h, grad_up[:, h * 128 : h * 128 + 128])
        middle = nt(eye, coarse_mid[:, h * 128 : h * 128 + 128]).astype(BF)
        put(29 + h, nn(middle, grad_out))
    put(31, jnp.zeros((128, 128), F32))
    for a in range(3):
        total = nn(grad_t[0], cols[64 * a : 64 * a + 512, :])
        total = total + nn(grad_t[1], cols[64 * a + 640 : 64 * a + 1152, :])
        for n in range(9):
            put(9 * a + n, total[:, n * 128 : n * 128 + 128].T)
    send[...] = wsum[pl.ds(pl.multiple_of((1 - core[0]) * 2048, 2048), 2048), :]
    keep[...] = wsum[pl.ds(pl.multiple_of(core[0] * 2048, 2048), 2048), :]
    copy.wait()


def pair_kernel(core, line, wsum, other, grad, own, one, two, three, held):
    held[...] = grad[...]
    for step, ref in enumerate((own, one, two, three)):
        at = pl.multiple_of(((line[0] + step) & 3) * 512, 512)
        kept = wsum[pl.ds(at, 512), :].astype(F32)
        ref[...] = (kept + other[pl.ds(at, 512), :].astype(F32)).astype(ref.dtype)


def backward_kernel(grad_t, weight, own, msg, lhs, acc_all, pc_all, rows_all):
    zero = jnp.zeros((64, 128), BF)
    for a in range(3):
        for n in [*range(a), *range(8 + a, 10)]:
            for s in range(2):
                lhs[s, n * 64 : n * 64 + 64, a * 128 : a * 128 + 128] = zero
    low = (lax.broadcasted_iota(jnp.int32, (64, 1), 0) & 7) != 0
    high = (lax.broadcasted_iota(jnp.int32, (64, 1), 0) & 7) != 7

    for s in range(2):
        acc, pc, rows = acc_all.at[s], pc_all.at[s], rows_all.at[s]
        values = grad_t[s].astype(F32).T.astype(BF)
        for a in range(3):
            lhs[s, a * 64 : a * 64 + 512, a * 128 : a * 128 + 128] = values
        acc[...] = jnp.zeros_like(acc)
        for b in range(3):
            part = nt(lhs[s], weight[b * 384 : b * 384 + 384, :])
            for c in range(3):
                for a in range(10):
                    at = pl.ds(8 + (a * 10 + b) * 8, 64)
                    acc[c, at, :] += part[a * 64 : a * 64 + 64, c * 128 : c * 128 + 128]

        def middle(row, size):
            at = 8 + row
            total = acc[1, pl.ds(at, size), :]
            total = total + jnp.where(high[:size], acc[0, pl.ds(at + 1, size), :], 0.0)
            return total + jnp.where(low[:size], acc[2, pl.ds(at - 1, size), :], 0.0)

        for a in range(8):
            own[s, pl.ds(a * 64, 64), :] = middle(((a + 1) * 10 + 1) * 8, 64)
            for d, b in (((0, -1, 0), 0), ((0, 1, 0), 9)):
                pc[pl.ds(PIECE[d] + 8 * a, 8), :] = middle(((a + 1) * 10 + b) * 8, 8)
        for a, x in ((-1, 0), (1, 9)):
            pc[pl.ds(PIECE[a, 0, 0], 64), :] = middle((x * 10 + 1) * 8, 64)
            for b, y in ((-1, 0), (1, 9)):
                pc[pl.ds(PIECE[a, b, 0], 8), :] = middle((x * 10 + y) * 8, 8)
        for c, ref, lane in ((-1, acc.at[0], 8), (1, acc.at[2], 15)):
            for a in range(8):
                pc[pl.ds(PIECE[0, 0, c] + 8 * a, 8), :] = ref[
                    pl.ds(((a + 1) * 10 + 1) * 8 + lane, 8, stride=8), :
                ]
            for a, x in ((-1, 0), (1, 9)):
                pc[pl.ds(PIECE[a, 0, c], 8), :] = ref[pl.ds((x * 10 + 1) * 8 + lane, 8, stride=8), :]
                pc[pl.ds(PIECE[0, a, c], 8), :] = ref[pl.ds((10 + x) * 8 + lane, 8, stride=80), :]
                for b, y in ((-1, 0), (1, 9)):
                    pc[pl.ds(PIECE[a, b, c], 1), :] = ref[pl.ds((x * 10 + y) * 8 + lane, 1), :]
        to_shares(pc, rows)
        msg[:, 16 * s : 16 * s + 16, :] = rows[...].astype(BF).reshape(32, 16, 128)


def join_kernel(terms, own, away1, away2, away3, msg):
    msg[:, 0:32, :] = terms[...]
    total = own[...] + away1[...].astype(F32) + away2[...].astype(F32) + away3[...].astype(F32)
    msg[:, 32:48, :] = total.astype(BF).reshape(32, 16, 128)


def merge_kernel(got, named, out, hot):
    same = same_part()
    zero = jnp.zeros((16, 128), BF)
    share = jnp.sum(got[:, 32:48, :].astype(F32), axis=0).astype(BF)
    out[:, 32:48, :] = jnp.broadcast_to(share[None], (32, 16, 128))
    second = lax.broadcasted_iota(jnp.int32, (16, 128), 0) >> 3
    split = [split_parts(got, s) for s in range(2)]
    totals = []
    for h in range(2):
        for n in range(4):
            asked = named[h, :, n * 128 : n * 128 + 128]
            for pair in range(32):
                here = (second + 2 * pair).astype(F32).astype(BF)
                hot[h, pair * 16 : pair * 16 + 16, n * 128 : n * 128 + 128] = jnp.where(
                    asked == here, same, zero
                )
        held = [x[h].reshape(256, 128) for x in split]
        totals.append(nn(hot[h], jnp.concatenate(held, axis=0).astype(BF)).reshape(64, 8, 128))
    total = jnp.concatenate(totals, axis=1).astype(BF)
    out[:, 0:32, :] = total.reshape(32, 32, 128)


def finish_kernel(flags, got, own, gout, out, rows, pc, total):
    for s in range(2):
        live = flags[s : s + 1, 0:1]
        rows[...] = got[:, 16 * s : 16 * s + 16, :].reshape(512, 128).astype(F32)
        to_pieces(rows, pc)
        total[...] = own[s]
        for d in OFFSETS:
            for at, first, size, stride in voxel_runs(d):
                where = run(first, size, stride)
                total[where, :] = total[where, :] + pc[pl.ds(PIECE[d] + at, size), :]
        out[s] = (total[...].T + gout[s].astype(F32) * live).astype(BF)


def assemble_kernel(flip, core, line, *refs):
    parts, (conv, up, down, held, sems) = refs[:4], refs[-5:]
    half = core[0] ^ flip

    def moves(n, first):
        def copy(src, dst, k):
            return pltpu.make_async_copy(src, dst, sems.at[n, k])

        block = held.at[n]
        return (
            (first < 24, lambda: [copy(block, conv.at[pl.ds(first, 4)], 0)]),
            (
                first == 24,
                lambda: [
                    copy(block.at[0:3], conv.at[pl.ds(24, 3)], 0),
                    copy(block.at[3], up.at[:, pl.ds(0, 128)], 1),
                ],
            ),
            (
                first == 28,
                lambda: [
                    copy(block.at[0], up.at[:, pl.ds(128, 128)], 0),
                    copy(block.at[1], down.at[pl.ds(0, 128), :], 1),
                    copy(block.at[2], down.at[pl.ds(128, 128), :], 2),
                ],
            ),
        )

    firsts = [half * 16 + ((line[0] + n) & 3) * 4 for n in range(4)]
    for n, part in enumerate(parts):
        held[n] = part[...].astype(F32).reshape(4, 128, 128)
        for when, copies in moves(n, firsts[n]):

            @pl.when(when)
            def _():
                for copy in copies():
                    copy.start()

    for n in range(4):
        for when, copies in moves(n, firsts[n]):

            @pl.when(when)
            def _():
                for copy in copies():
                    copy.wait()


VM = pl.BlockSpec(memory_space=pltpu.VMEM)
SM = pl.BlockSpec(memory_space=pltpu.SMEM)


HB = pl.BlockSpec(memory_space=pltpu.HBM)


def call(
    kernel, shapes, scalars, arrays, scratch=(), flops=1e6, limit=24, ins=None, outs=None,
    alias=None, name=None,
):
    moved = sum(x.size * x.dtype.itemsize for x in arrays)
    moved += sum(int(np.prod(s.shape)) * s.dtype.itemsize for s in shapes)
    return pl.pallas_call(
        kernel,
        out_shape=shapes,
        in_specs=[SM] * len(scalars) + (ins or [VM] * len(arrays)),
        out_specs=outs or [VM] * len(shapes),
        input_output_aliases=alias or {},
        scratch_shapes=list(scratch),
        compiler_params=pltpu.CompilerParams(vmem_limit_bytes=limit * 2**20),
        cost_estimate=pl.CostEstimate(
            flops=int(flops), bytes_accessed=int(moved), transcendentals=0
        ),
        name=name,
    )(*scalars, *arrays)


def shape(dims, dtype):
    return jax.ShapeDtypeStruct(dims, dtype)


def on_device(
    features,
    grad_out,
    conv_weight,
    coarse_up,
    coarse_down,
    counts,
    neighbour_owner,
    neighbour_slot,
    parent,
    child_slot,
):
    grp = lax.axis_index("grp").astype(jnp.int32)
    core = (grp & 1).reshape(1)
    line = (grp >> 1).reshape(1)
    swap = [(i, i ^ 1) for i in range(8)]
    slots = lax.broadcasted_iota(jnp.int32, (8, 128), 0)
    flags = (slots < counts[0]).astype(F32)
    (msg,) = call(
        ask_kernel,
        [shape((32, 32, 128), BF)],
        [],
        [features, neighbour_owner, neighbour_slot, jnp.asarray(choice_table(), BF)],
        [
            pltpu.VMEM((2, 128, 512), BF),
            pltpu.VMEM((2, 26), jnp.int32),
            pltpu.VMEM((2, 26), jnp.int32),
            pltpu.VMEM((128, 1024), BF),
            pltpu.VMEM((16, 128), F32),
            pltpu.VMEM((2, 8, 128), F32),
            pltpu.VMEM((2, 512, 128), F32),
            pltpu.VMEM((2, 512, 128), F32),
            pltpu.VMEM((2, 512, 128), F32),
            pltpu.VMEM((32, 32, 128), BF),
            pltpu.SemaphoreType.DMA((7,)),
        ],
        flops=2e6,
        limit=60,
        ins=[HB] * 3 + [pl.BlockSpec(memory_space=pl.ANY)],
        outs=[HB],
        name="ask",
    )
    first = lax.all_to_all(msg, "dev", split_axis=0, concat_axis=0, tiled=True)
    answer, table = call(
        route_kernel,
        [shape((32, 32, 128), BF), shape((2, 16, 512), BF)],
        [],
        [first],
        [pltpu.VMEM((2, 512, 512), BF)],
        flops=3e8,
        name="route",
    )
    halo = lax.all_to_all(answer, "dev", split_axis=0, concat_axis=0, tiled=True)
    weight = conv_weight.reshape(3, 1152, 128)
    weight = jnp.concatenate([weight[0], weight[1], weight[2]], axis=1)
    coarse = jnp.concatenate([jnp.pad(coarse_up, ((0, 128), (0, 0))), coarse_down], axis=1)
    weight = jnp.concatenate([weight, coarse], axis=0)
    output, grad_pre, wsum, send = call(
        forward_kernel,
        [
            shape((2, 128, 512), BF),
            shape((2, 128, 512), BF),
            shape((2048, 128), BF),
            shape((2048, 128), BF),
        ],
        [parent, child_slot, core],
        [flags, features, halo, grad_out, weight],
        [
            pltpu.VMEM((2, 512, 128), F32),
            pltpu.VMEM((2, 512, 128), F32),
            pltpu.VMEM((2, 800, 128), F32),
            pltpu.VMEM((2, 816, 128), F32),
            pltpu.VMEM((2, 800, 128), F32),
            pltpu.VMEM((1280, 1152), BF),
            pltpu.VMEM((16, 128), F32),
            pltpu.VMEM((2, 16, 128), F32),
            pltpu.VMEM((2, 128, 512), BF),
            pltpu.VMEM((4096, 128), BF),
            pltpu.SemaphoreType.DMA((1,)),
        ],
        flops=2e9,
        outs=[HB, VM, VM, VM],
        name="forward",
    )
    other = lax.ppermute(send, "grp", swap)
    own_sum, *away, grad_pre = call(
        pair_kernel,
        [shape((512, 128), F32)] + [shape((512, 128), BF)] * 3 + [shape((2, 128, 512), BF)],
        [core, line],
        [wsum, other, grad_pre],
        name="pair",
    )
    away = [
        lax.ppermute(away[step - 1], "grp", [(i, (i + 2 * step) % 8) for i in range(8)])
        for step in (1, 3, 2)
    ]
    own, terms = call(
        backward_kernel,
        [shape((2, 512, 128), F32), shape((32, 32, 128), BF)],
        [],
        [grad_pre, weight],
        [
            pltpu.VMEM((2, 640, 384), BF),
            pltpu.VMEM((2, 3, 816, 128), F32),
            pltpu.VMEM((2, 512, 128), F32),
            pltpu.VMEM((2, 512, 128), F32),
        ],
        flops=4e9,
        name="backward",
    )
    (terms,) = call(
        join_kernel, [shape((32, 48, 128), BF)], [], [terms, own_sum, *away], name="join"
    )
    terms = lax.all_to_all(terms, "dev", split_axis=0, concat_axis=0, tiled=True)
    (sums,) = call(
        merge_kernel,
        [shape((32, 48, 128), BF)],
        [],
        [terms, table],
        [pltpu.VMEM((2, 512, 512), BF)],
        flops=3e8,
        name="merge",
    )
    back = lax.all_to_all(sums, "dev", split_axis=0, concat_axis=0, tiled=True)
    chunk = back[:, 32:48, :].reshape(512, 128)
    parts = {
        step: lax.ppermute(chunk, "grp", [(i, (i - 2 * step) % 8) for i in range(8)])
        for step in (1, 3, 2)
    }
    (grad_features,) = call(
        finish_kernel,
        [shape((2, 128, 512), BF)],
        [],
        [flags, back, own, grad_out],
        [pltpu.VMEM((512, 128), F32)] * 3,
        flops=3e8,
        name="finish",
    )
    for step in (1, 3, 2):
        parts[step], grad_features = lax.optimization_barrier((parts[step], grad_features))
    mine = [chunk, parts[1], parts[2], parts[3]]
    others = [lax.ppermute(x, "grp", swap) for x in mine]

    def assemble(flip, pieces, held):
        return call(
            functools.partial(assemble_kernel, flip),
            [shape((27, 128, 128), F32), shape((128, 256), F32), shape((256, 128), F32)],
            [core, line],
            pieces + held,
            [pltpu.VMEM((4, 4, 128, 128), F32), pltpu.SemaphoreType.DMA((4, 3))],
            ins=[VM] * 4 + [HB] * len(held),
            outs=[HB] * 3,
            alias={6 + n: n for n in range(len(held))},
            name="assemble",
        )

    grad_conv, grad_up, grad_down = assemble(1, others, list(assemble(0, mine, [])))
    return (output, grad_features, grad_conv, grad_up, grad_down)


def solution(mesh):
    return jax.shard_map(
        on_device,
        mesh=mesh,
        in_specs=(
            P(("grp", "dev"), None, None),
            P(("grp", "dev"), None, None),
            P(),
            P(),
            P(),
            P(("grp", "dev")),
            P(("grp", "dev"), None),
            P(("grp", "dev"), None),
            P(("grp", "dev")),
            P(("grp", "dev")),
        ),
        out_specs=(P(("grp", "dev"), None, None), P(("grp", "dev"), None, None), P(), P(), P()),
        check_vma=False,
    )
```
